512 devices in a mesh: gx: 16 (over z), gy: 8 (over y, core), gz: 4 (over x).
Axes of the slice: x: 4, y: 4, z: 16, core: 2. Of those that a mesh axis runs over, the one named last changes fastest.
Arguments:
- coords: float32 [3, 524288], P(None, ('gx', 'gy', 'gz')), may hold values from 0 to 256, as said below
- polarizability: float32 [524288], P(('gx', 'gy', 'gz')), may hold values from 0.05 to 0.2
- external_field: float32 [3, 524288], P(None, ('gx', 'gy', 'gz')), may hold values from -1000 to 1000
- bead_live: int32 [524288], P(('gx', 'gy', 'gz')), may hold values from 0 to 1, as said below
- ghost_x: int32 [2, 131072], P(None, ('gx', 'gy', 'gz')), may hold values from 0 to 1023, as said below
- ghost_y: int32 [2, 393216], P(None, ('gx', 'gy', 'gz')), may hold values from 0 to 1535, as said below
- ghost_z: int32 [2, 1572864], P(None, ('gx', 'gy', 'gz')), may hold values from 0 to 3071, as said below
- pair_blocks: int32 [2, 110592], P(None, ('gx', 'gy', 'gz')), may hold values from 0 to 71, as said below
- pair_live: int32 [110592], P(('gx', 'gy', 'gz')), may hold values from 0 to 1, as said below
Outputs:
- dipoles: float32 [3, 524288], P(None, ('gx', 'gy', 'gz'))
- dipole_residual: float32 [3, 524288], P(None, ('gx', 'gy', 'gz'))
The draws below stay inside these ranges and needn't reach their ends.
Inputs may be any that keep to these rules, and one draw needn't show every extreme that they name: `coords`: beads sit near the sites of a cubic lattice of spacing 1: a brick is 16 x 4 * 2 x 8 sites at (16 i, 4 * 2 j, 8 * k), block b = 4-site column group (b // 2, b % 2) of 4 x 4 x 8 sites; every two beads, images included, are 0.6 or more apart. `bead_live`: the owned beads of a device are its first slots; some device owns all 1024 in every draw. `ghost_x`: each row lists every entry of the brick's face layer once, in any order. `ghost_y`: each row lists every entry of a face layer of the set after the gx section once, in any order. `ghost_z`: each row lists every entry of a layer of the set after the gy section once, in any order. `pair_blocks`: A device lists, for each of its blocks that holds an owned bead, the 27 blocks of the extended set beside it or equal to it, in any order, before all padding slots (zeros); some device fills all 216 slots in every draw. `pair_live`: ones first.
All inputs are finite; a program needn't handle non-finite values.
Results may differ from the reference program's by a relative error of at most 0.008.
Values sent between devices are 32-bit elements; how exact they have to be, the bound alone decides.
A program may use at most 64 MiB of HBM per device.

```python
import math
import jax
import jax.numpy as jnp
from jax import lax

BZ = 8
BY = 2
ITERS = 3
BLOCK = 128
NBLK = 8
NLOC = 1024
NPAIR = 216
NBEADS = 524288
N_GX = 16
N_GY = 8
N_GZ = 4


def lane_orders(key):
    subkeys = jax.random.split(key, N_GX * N_GY * N_GZ * NBLK)
    orders = jax.vmap(lambda single: jax.random.permutation(single, BLOCK))(subkeys)
    return orders.reshape(N_GX * N_GY * N_GZ, NBLK, BLOCK).astype(jnp.int32)


def device_places():
    device = jnp.arange(N_GX * N_GY * N_GZ, dtype=jnp.int32)
    return (device // (N_GY * N_GZ), device // N_GZ % N_GY, device % N_GZ)


def pool_slots(inverse, spot_x, spot_y):
    lanes = jnp.arange(BLOCK, dtype=jnp.int32)
    devices = inverse.shape[0]
    if 0 <= spot_x <= 3 and 0 <= spot_y < BY:
        block_id = spot_x * BY + spot_y
        return block_id * BLOCK + inverse[:, block_id, :]
    if 0 <= spot_y < BY:
        base = NLOC + (0 if spot_x < 0 else BY * BLOCK) + spot_y * BLOCK
    else:
        base = NLOC + 2 * BY * BLOCK + (0 if spot_y < 0 else 6 * BLOCK) + (spot_x + 1) * BLOCK
    return jnp.broadcast_to(base + lanes, (devices, BLOCK))


def shuffle_entries(key, table):
    width = table.shape[1]
    subkeys = jax.random.split(key, table.shape[0])
    orders = jax.vmap(lambda single: jax.random.permutation(single, width))(subkeys)
    return jnp.take_along_axis(table, orders.astype(jnp.int32), axis=1)


def pair_table(key):
    devices = N_GX * N_GY * N_GZ
    counts = jax.random.randint(jax.random.fold_in(key, 5), (devices,), NLOC // 2, NLOC + 1)
    fullest = jax.random.randint(jax.random.fold_in(key, 6), (), 0, devices)
    counts = counts.at[fullest].set(NLOC)
    live_blocks = (counts + BLOCK - 1) // BLOCK
    combos = jnp.arange(NPAIR, dtype=jnp.int32)
    targets = combos // 27
    moves = combos % 27
    step_x = moves // 9 - 1
    step_y = moves // 3 % 3 - 1
    step_z = moves % 3 - 1
    reach_x = targets // BY + step_x
    reach_y = targets % BY + step_y
    inside = (reach_x >= 0) & (reach_x <= 3) & (reach_y >= 0) & (reach_y < BY)
    in_rows = (reach_y >= 0) & (reach_y < BY)
    plane = jnp.where(inside, reach_x * BY + reach_y, jnp.where(in_rows, NBLK + jnp.where(reach_x < 0, 0, BY) + reach_y, NBLK + 2 * BY + jnp.where(reach_y < 0, 0, 6) + reach_x + 1))
    layer = NBLK + 2 * BY + 12 + jnp.where(step_z < 0, 0, 6 * (BY + 2)) + (reach_x + 1) * (BY + 2) + reach_y + 1
    sources = jnp.where(step_z == 0, plane, layer)
    alive = targets[None, :] < live_blocks[:, None]
    scores = jax.random.randint(jax.random.fold_in(key, 7), (devices, NPAIR), 0, 2 ** 20)
    scores = jnp.where(alive, scores, 2 ** 20) * NPAIR + combos[None, :]
    ordering = jnp.argsort(scores, axis=1)
    alive_sorted = jnp.take_along_axis(alive, ordering, axis=1)
    target_sorted = jnp.where(alive_sorted, targets[ordering], 0)
    source_sorted = jnp.where(alive_sorted, sources[ordering], 0)
    return (counts, jnp.stack([target_sorted, source_sorted]).astype(jnp.int32), alive_sorted)


def draw_coords(key, part):
    orders = lane_orders(key)
    key = jax.random.fold_in(key, 11)
    first, second, third = device_places()
    blocks = jnp.arange(NBLK, dtype=jnp.int32)
    cell_x = orders // (4 * BZ)
    cell_y = orders // BZ % 4
    cell_z = orders % BZ
    pos_x = first[:, None, None] * 16 + (blocks // BY)[None, :, None] * 4 + cell_x
    pos_y = second[:, None, None] * (4 * BY) + (blocks % BY)[None, :, None] * 4 + cell_y
    pos_z = third[:, None, None] * BZ + cell_z + 0 * blocks[None, :, None]
    lattice = jnp.stack([pos_x, pos_y, pos_z]).astype(jnp.float32) + 0.5
    jitter = jax.random.uniform(key, lattice.shape, jnp.float32, -0.1, 0.1)
    return (lattice + jitter).reshape(3, -1)


def draw_external_field(key, part):
    key = jax.random.fold_in(key, 21)
    first, second, third = device_places()
    ramp = first.astype(jnp.float32) / (N_GX - 1)
    shape = (3, N_GX * N_GY * N_GZ, NLOC)
    base = jnp.clip(jax.random.normal(key, shape, jnp.float32), -4.0, 4.0)
    scale = 4.0 * 3.0 ** ramp
    return (base * scale[None, :, None]).reshape(3, -1)


def draw_bead_live(key, part):
    counts, blocks, alive = pair_table(key)
    slots = jnp.arange(NLOC, dtype=jnp.int32)
    return (slots[None, :] < counts[:, None]).astype(jnp.int32).reshape(-1)


def draw_pair_blocks(key, part):
    counts, blocks, alive = pair_table(key)
    return blocks.reshape(2, -1)


def draw_pair_live(key, part):
    counts, blocks, alive = pair_table(key)
    return alive.astype(jnp.int32).reshape(-1)


def draw_ghost_x(key, part):
    inverse = jnp.argsort(lane_orders(key), axis=-1).astype(jnp.int32)
    key = jax.random.fold_in(key, 16)
    upper = jnp.concatenate([pool_slots(inverse, 3, spot) for spot in range(BY)], axis=1)
    lower = jnp.concatenate([pool_slots(inverse, 0, spot) for spot in range(BY)], axis=1)
    upper = shuffle_entries(jax.random.fold_in(key, 1), upper)
    lower = shuffle_entries(jax.random.fold_in(key, 2), lower)
    return jnp.stack([upper, lower]).reshape(2, -1).astype(jnp.int32)


def draw_ghost_y(key, part):
    inverse = jnp.argsort(lane_orders(key), axis=-1).astype(jnp.int32)
    key = jax.random.fold_in(key, 17)
    upper = jnp.concatenate([pool_slots(inverse, spot, BY - 1) for spot in range(-1, 5)], axis=1)
    lower = jnp.concatenate([pool_slots(inverse, spot, 0) for spot in range(-1, 5)], axis=1)
    upper = shuffle_entries(jax.random.fold_in(key, 1), upper)
    lower = shuffle_entries(jax.random.fold_in(key, 2), lower)
    return jnp.stack([upper, lower]).reshape(2, -1).astype(jnp.int32)


def draw_ghost_z(key, part):
    inverse = jnp.argsort(lane_orders(key), axis=-1).astype(jnp.int32)
    key = jax.random.fold_in(key, 18)
    layer = jnp.concatenate([pool_slots(inverse, spot_x, spot_y) for spot_x in range(-1, 5) for spot_y in range(-1, BY + 1)], axis=1)
    upper = shuffle_entries(jax.random.fold_in(key, 1), layer)
    lower = shuffle_entries(jax.random.fold_in(key, 2), layer)
    return jnp.stack([upper, lower]).reshape(2, -1).astype(jnp.int32)


def block_levels(stream_key, shape, shards, smallest, top_value):
    def one(position, blocks):
        steps = jax.random.uniform(jax.random.fold_in(jax.random.fold_in(stream_key, 6), position), (blocks,), jnp.float32, smallest / len(shards), top_value / len(shards))
        return jnp.repeat(jnp.exp(steps), shape[position] // blocks).reshape((-1,) + (1,) * (len(shape) - position - 1))

    level = one(*shards[0])
    for cut in shards[1:]:
        level = level * one(*cut)
    return level


def setup_inputs(seed: int = 0) -> dict:
    arg_keys = jax.random.split(jax.random.key(seed), 10)
    coords = draw_coords(jax.random.fold_in(arg_keys[9], 71), 0)
    polarizability = jnp.clip(jnp.exp(math.log(0.2) - 1.3862944 * jax.random.uniform(arg_keys[1], (NBEADS,), jnp.float32) ** block_levels(arg_keys[1], (NBEADS,), ((0, 512),), -0.2, 0.2)), 0.05, 0.2)
    external_field = draw_external_field(jax.random.fold_in(arg_keys[9], 71), 0)
    bead_live = draw_bead_live(jax.random.fold_in(arg_keys[9], 71), 0)
    ghost_x = draw_ghost_x(jax.random.fold_in(arg_keys[9], 71), 0)
    ghost_y = draw_ghost_y(jax.random.fold_in(arg_keys[9], 71), 0)
    ghost_z = draw_ghost_z(jax.random.fold_in(arg_keys[9], 71), 0)
    pair_blocks = draw_pair_blocks(jax.random.fold_in(arg_keys[9], 71), 0)
    pair_live = draw_pair_live(jax.random.fold_in(arg_keys[9], 71), 0)
    return dict(coords=coords, polarizability=polarizability, external_field=external_field, bead_live=bead_live, ghost_x=ghost_x, ghost_y=ghost_y, ghost_z=ghost_z, pair_blocks=pair_blocks, pair_live=pair_live)


CUTOFF_SQUARED = 12.25
THOLE_FACTOR = 0.02

def pair_field(target_geo, source_geo, source_mu, same_block):
    width = target_geo.shape[-1]
    delta_x = target_geo[0][:, :, None] - source_geo[0][:, None, :]
    delta_y = target_geo[1][:, :, None] - source_geo[1][:, None, :]
    delta_z = target_geo[2][:, :, None] - source_geo[2][:, None, :]
    diagonal_lane = jnp.arange(width)[:, None] == jnp.arange(width)[None, :]
    self_pair = jnp.logical_and(same_block, diagonal_lane[None])
    dist_sq = jnp.where(self_pair, 1.0, delta_x * delta_x + delta_y * delta_y + delta_z * delta_z)
    inverse = lax.rsqrt(dist_sq)
    inverse_cube = inverse * inverse * inverse
    margin = jnp.maximum(1.0 - dist_sq / CUTOFF_SQUARED, 0.0)
    taper = jnp.where(self_pair, 0.0, margin * margin)
    scaled = THOLE_FACTOR * dist_sq * jnp.sqrt(dist_sq) * lax.rsqrt(target_geo[3][:, :, None] * source_geo[3][:, None, :])
    damping = jnp.exp(-scaled)
    inner = taper * (1.0 - damping) * inverse_cube
    outer = 3.0 * taper * (1.0 - (1.0 + scaled) * damping) * inverse_cube * inverse * inverse
    moment_x = source_mu[0][:, None, :]
    moment_y = source_mu[1][:, None, :]
    moment_z = source_mu[2][:, None, :]
    along = delta_x * moment_x + delta_y * moment_y + delta_z * moment_z
    field_x = lax.optimization_barrier(jnp.sum(outer * along * delta_x - inner * moment_x, axis=2))
    field_y = lax.optimization_barrier(jnp.sum(outer * along * delta_y - inner * moment_y, axis=2))
    field_z = lax.optimization_barrier(jnp.sum(outer * along * delta_z - inner * moment_z, axis=2))
    return jnp.stack([field_x, field_y, field_z])

def spread(values, ghost_x, ghost_y, ghost_z, boxed):
    comps = values.shape[0]
    ghosted = values.reshape(comps, N_GX, N_GY, N_GZ, NLOC)
    sections = ((ghost_x, 1, N_GX, 0, 16.0 * N_GX), (ghost_y, 2, N_GY, 1, 4.0 * BY * N_GY), (ghost_z, 3, N_GZ, 2, 1.0 * BZ * N_GZ))
    for lists, axis_pos, count, row_pos, extent in sections:
        listed = lists.reshape(2, N_GX, N_GY, N_GZ, -1)
        pieces = [ghosted]
        for slot_index, offset in enumerate((1, -1)):
            chosen = jnp.broadcast_to(listed[slot_index][None], (comps,) + listed[slot_index].shape)
            sent = jnp.take_along_axis(ghosted, chosen, axis=4)
            arrived = jnp.roll(sent, offset, axis=axis_pos)
            if boxed:
                border = 0 if offset == 1 else count - 1
                layout = [1, 1, 1, 1]
                layout[axis_pos - 1] = count
                marks = (jnp.arange(count) == border).astype(values.dtype).reshape(layout)
                arrived = arrived.at[row_pos].add(-offset * extent * marks)
            pieces.append(arrived)
        ghosted = jnp.concatenate(pieces, axis=4)
    return ghosted.reshape(comps, N_GX * N_GY * N_GZ, -1)

def device_field(inputs):
    geometry, moments, blocks, alive = inputs
    geo_blocks = geometry.reshape(4, -1, BLOCK)
    moment_blocks = moments.reshape(3, -1, BLOCK)
    targets = blocks[0].reshape(27, NBLK)
    sources = blocks[1].reshape(27, NBLK)
    weights = alive.reshape(27, NBLK).astype(geometry.dtype)

    def accumulate(fields, group):
        target_ids, source_ids, weight_row = group
        contrib = pair_field(geo_blocks[:, target_ids], geo_blocks[:, source_ids], moment_blocks[:, source_ids], (target_ids == source_ids)[:, None, None])
        contrib = contrib * weight_row[None, :, None]
        return (fields.at[:, target_ids].add(contrib), None)
    start = jnp.zeros((3, NBLK, BLOCK), geometry.dtype)
    fields, _ = lax.scan(accumulate, start, (targets, sources, weights))
    return fields.reshape(3, NLOC)

def reference(coords, polarizability, external_field, bead_live, ghost_x, ghost_y, ghost_z, pair_blocks, pair_live):
    devices = N_GX * N_GY * N_GZ
    living = bead_live.astype(coords.dtype)
    geometry = jnp.concatenate([coords, polarizability[None]], axis=0)
    geo_pool = spread(geometry, ghost_x, ghost_y, ghost_z, True).transpose(1, 0, 2)
    blocks = pair_blocks.reshape(2, devices, NPAIR).transpose(1, 0, 2)
    alive = pair_live.reshape(devices, NPAIR)

    def applied(direction):
        moments = spread(direction, ghost_x, ghost_y, ghost_z, False).transpose(1, 0, 2)
        fields = lax.map(device_field, (geo_pool, moments, blocks, alive))
        fields = fields.transpose(1, 0, 2).reshape(3, -1)
        return living * (direction / polarizability[None] - fields)
    rhs = living * external_field
    dipoles = jnp.zeros_like(rhs)
    residual = rhs
    direction = rhs
    norm_now = jnp.sum(residual * residual)
    for iteration in range(ITERS):
        image = applied(direction)
        step_size = norm_now / jnp.sum(direction * image)
        dipoles = dipoles + step_size * direction
        residual = residual - step_size * image
        norm_next = jnp.sum(residual * residual)
        direction = residual + norm_next / norm_now * direction
        norm_now = norm_next
    return (dipoles, polarizability[None] * residual)
```

```python
import functools
import math

import jax
import jax.numpy as jnp
from jax import lax
from jax.experimental import pallas as pl
from jax.experimental.pallas import tpu as pltpu
from jax.sharding import PartitionSpec as P

BLOCK = 128
NBX, NBY = 4, 2
NBLK = NBX * NBY
CX, CY = NBX + 2, NBY + 2
NCOL = CX * CY
GROUP = 32
NGRP = BLOCK // GROUP
BRICK = (16.0, 8.0, 8.0)
CUTOFF_SQUARED = 12.25
THOLE_FACTOR = 0.02
CENTRE, HALF = 12.5, 8.5
FAR = 1.0e6
MESH = pl.DeviceIdType.MESH
HIGHEST = lax.Precision.HIGHEST
OFFSETS = [
    (x, y, z)
    for x in (-1, 0, 1)
    for y in (-1, 0, 1)
    for z in (-1, 0, 1)
    if (x, y, z) != (0, 0, 0)
]
GRAM = [(a, b) for a in range(4) for b in range(a, 4)]


def dot_rows(left, right, precision=HIGHEST):
    return lax.dot_general(
        left, right, (((1,), (0,)), ((), ())), precision=precision,
        preferred_element_type=jnp.float32,
    )


def dot_lanes(left, right, precision=HIGHEST):
    return lax.dot_general(
        left, right, (((1,), (1,)), ((), ())), precision=precision,
        preferred_element_type=jnp.float32,
    )


def iota(shape, axis):
    return lax.broadcasted_iota(jnp.int32, shape, axis)


def own_span(step, count):
    return (0, count) if step == 0 else ((count - 1, 1) if step > 0 else (0, 1))


def halo_span(step, count):
    return (1, count) if step == 0 else ((0, 1) if step > 0 else (count + 1, 1))


def inverse_list(list_ref, row, first, entries, tables):
    blocks = jnp.zeros((tables, BLOCK), jnp.float32)
    lanes = jnp.zeros((tables, BLOCK), jnp.float32)
    spot = iota((BLOCK, BLOCK), 1).astype(jnp.float32)
    for r in range(entries // BLOCK):
        entry = list_ref[row : row + 1, r * BLOCK : (r + 1) * BLOCK]
        high = jnp.right_shift(entry, 7) - first
        low = jnp.bitwise_and(entry, BLOCK - 1)
        pick = (iota((tables, BLOCK), 0) == high).astype(jnp.float32)
        place = (iota((BLOCK, BLOCK), 0) == low).astype(jnp.float32)
        both = jnp.concatenate([place, place * spot], axis=0).astype(jnp.bfloat16)
        found = dot_lanes(pick.astype(jnp.bfloat16), both, None)
        blocks = blocks + found[:, :BLOCK] * float(r + 1)
        lanes = lanes + found[:, BLOCK:]
    return blocks, lanes


def inverse_blocks(list_ref, row, entries):
    rows = entries // BLOCK
    total = jnp.zeros((rows, BLOCK), jnp.float32)
    for r in range(rows):
        entry = list_ref[row : row + 1, r * BLOCK : (r + 1) * BLOCK]
        high = jnp.right_shift(entry, 7)
        low = jnp.bitwise_and(entry, BLOCK - 1)
        pick = jnp.where(iota((rows, BLOCK), 0) == high, float(r), 0.0)
        place = (iota((BLOCK, BLOCK), 0) == low).astype(jnp.float32)
        total = total + dot_lanes(
            pick.astype(jnp.bfloat16), place.astype(jnp.bfloat16), None
        )
    return total


def look_up(table, index):
    high = jnp.right_shift(index, 7)
    low = jnp.bitwise_and(index, BLOCK - 1)
    out = jnp.zeros(index.shape, jnp.float32)
    for r in range(table.shape[0]):
        row = jnp.broadcast_to(table[r : r + 1, :], index.shape)
        out = jnp.where(high == r, jnp.take_along_axis(row, low, axis=1), out)
    return out


def place_of(sizes):
    return tuple(lax.axis_index(name) for name in ("gx", "gy", "gz"))


def neighbour(me, sizes, step):
    return tuple(lax.rem(m + s + n, n) for m, s, n in zip(me, step, sizes))


def greet(targets):
    barrier = pltpu.get_barrier_semaphore()
    for target in targets:
        pl.semaphore_signal(barrier, inc=1, device_id=target, device_id_type=MESH)
    return barrier


def halo_copies(buffer, send_sem, recv_sem, me, sizes):
    copies = []
    for n, step in enumerate(OFFSETS):
        (xs, xn), (ys, yn) = own_span(step[0], NBX), own_span(step[1], NBY)
        (xd, _), (yd, _) = halo_span(step[0], NBX), halo_span(step[1], NBY)
        copies.append(
            pltpu.make_async_remote_copy(
                src_ref=buffer.at[1, pl.ds(1 + xs, xn), pl.ds(1 + ys, yn)],
                dst_ref=buffer.at[1 - step[2], pl.ds(xd, xn), pl.ds(yd, yn)],
                send_sem=send_sem.at[n],
                recv_sem=recv_sem.at[n],
                device_id=neighbour(me, sizes, step),
                device_id_type=MESH,
            )
        )
    return copies


def field_kernel(
    sizes,
    coords, polar, external, live, ghost_x, ghost_y, ghost_z, pairs, alive,
    basis_out, gram_out,
    halo1, halo2, halo3, tabs_y, tabs_z, own_y, own_z, sends, recvs, tab_sends, tab_recvs,
    order, side, target, window, moved, marks, px, py, pz, inner_s, sums, basis,
):
    me = place_of(sizes)
    barrier = greet([neighbour(me, sizes, step) for step in OFFSETS])

    up_blocks, up_lanes = inverse_list(ghost_x, 0, 0, 2 * BLOCK, NBLK)
    down_blocks, down_lanes = inverse_list(ghost_x, 1, 0, 2 * BLOCK, NBLK)
    upper = iota((NBLK, BLOCK), 0) >= NBLK - NBY
    x_spot = jnp.where(
        upper, (up_blocks - 1.0) * BLOCK + up_lanes, (down_blocks - 1.0) * BLOCK + down_lanes
    )
    x_spot = jnp.maximum(x_spot, 0.0)
    lane = iota((1, BLOCK), 1)
    lane_f = lane.astype(jnp.float32)

    for b in range(NBLK):
        cut = slice(b * BLOCK, (b + 1) * BLOCK)
        alpha = polar[0:1, cut]
        living = live[0:1, cut].astype(jnp.float32)
        place = coords[:, cut]
        rhs = external[:, cut] * living
        code = lane_f + x_spot[b : b + 1, :] * BLOCK
        beta = lax.rsqrt(alpha) * math.sqrt(THOLE_FACTOR)
        tile = jnp.concatenate([place, beta, rhs, code], axis=0)
        more = jnp.concatenate(
            [living / alpha, living, jnp.zeros((6, BLOCK), jnp.float32)], axis=0
        )
        column = jnp.transpose(tile)
        z_row = place[2:3, :]
        z_col = column[:, 2:3]
        before = jnp.logical_or(
            z_row < z_col,
            jnp.logical_and(z_row == z_col, iota((BLOCK, BLOCK), 1) < iota((BLOCK, BLOCK), 0)),
        )
        rank = jnp.sum(before.astype(jnp.float32), axis=1, keepdims=True)
        one_hot = (rank == iota((BLOCK, BLOCK), 1).astype(jnp.float32)).astype(jnp.float32)
        order[b] = one_hot
        ranked = dot_rows(jnp.concatenate([tile, more], axis=0), one_hot)
        halo1[1, 1 + b // NBY, 1 + b % NBY] = ranked[:8]
        side[b] = ranked[8:]
        basis[0, b] = jnp.concatenate(
            [ranked[4:7], jnp.zeros((5, BLOCK), jnp.float32)], axis=0
        )
        flipped = jnp.transpose(ranked[:8])
        for g in range(NGRP):
            target[b * NGRP + g] = flipped[g * GROUP : (g + 1) * GROUP]

    pl.semaphore_wait(barrier, len(OFFSETS))
    first = halo_copies(halo1, sends.at[0], recvs.at[0], me, sizes)
    for copy in first:
        copy.start()

    for row in range(2):
        blocks, lanes = inverse_list(ghost_y, row, 0, 6 * BLOCK, 12)
        own_y[row, 0:12] = (blocks - 1.0) * BLOCK + lanes
        own_z[row] = inverse_blocks(ghost_z, row, 24 * BLOCK)
    tables = []
    for row, step_y in enumerate((1, -1)):
        for step_z in (-1, 0, 1):
            n = len(tables)
            tables.append(
                pltpu.make_async_remote_copy(
                    src_ref=own_y.at[row],
                    dst_ref=tabs_y.at[row, 1 - step_z],
                    send_sem=tab_sends.at[n],
                    recv_sem=tab_recvs.at[n],
                    device_id=neighbour(me, sizes, (0, step_y, step_z)),
                    device_id_type=MESH,
                )
            )
    for row, step_z in enumerate((1, -1)):
        n = len(tables)
        tables.append(
            pltpu.make_async_remote_copy(
                src_ref=own_z.at[row],
                dst_ref=tabs_z.at[row],
                send_sem=tab_sends.at[n],
                recv_sem=tab_recvs.at[n],
                device_id=neighbour(me, sizes, (0, 0, step_z)),
                device_id_type=MESH,
            )
        )
    for copy in tables:
        copy.start()

    count = pairs.shape[1]
    bits = jnp.left_shift(alive[0:1, :], pairs[0:1, :]).astype(jnp.float32)
    bits = jnp.broadcast_to(bits, (8, count)).astype(jnp.bfloat16)
    listed = (iota((BLOCK, count), 0) == pairs[1:2, :]).astype(jnp.float32)
    listed_by = dot_lanes(bits, listed.astype(jnp.bfloat16), None)

    for copy in first:
        copy.wait_recv()
    for copy in tables:
        copy.wait_recv()

    for role in range(3):
        for part in range(NCOL // 8):
            codes = jnp.concatenate(
                [
                    halo1[role, c // CY, c % CY, 7:8, :]
                    for c in range(part * 8, part * 8 + 8)
                ],
                axis=0,
            ).astype(jnp.int32)
            spot = jnp.right_shift(codes, 7)
            own_lane = jnp.bitwise_and(codes, BLOCK - 1)
            col = iota((8, BLOCK), 0) + part * 8
            cx, cy = jnp.right_shift(col, 2), jnp.bitwise_and(col, 3)
            block_y = jnp.bitwise_and(cy + 1, 1)
            entry = ((cx - 1) * NBY + block_y) * BLOCK + own_lane
            entry = jnp.where(cx == 0, NBLK * BLOCK + spot, entry)
            entry = jnp.where(cx == CX - 1, (NBLK + NBY) * BLOCK + spot, entry)
            low = look_up(tabs_y[0, role, 0:12], entry)
            high = look_up(tabs_y[1, role, 0:12], entry)
            found = jnp.where(cy == 0, low, jnp.where(cy == CY - 1, high, 0.0))
            valid = found >= 0.0
            found = jnp.maximum(found, 0.0).astype(jnp.int32)
            entry = jnp.where(cy == 0, 12 * BLOCK + found, entry)
            entry = jnp.where(cy == CY - 1, 18 * BLOCK + found, entry)
            if role == 1:
                block = jnp.right_shift(entry, 7)
            else:
                layer = look_up(tabs_z[role // 2], entry)
                block = layer.astype(jnp.int32) + (24 if role == 0 else 48)
            mark = jnp.take_along_axis(listed_by, block, axis=1)
            marks[role, part * 8 : part * 8 + 8] = jnp.where(valid, mark, 0.0)

    row8 = iota((8, BLOCK), 0)
    lane8 = iota((8, BLOCK), 1)
    edge = [
        (jnp.where(m == 0, -n * size, 0.0), jnp.where(m == n - 1, n * size, 0.0))
        for m, n, size in zip(me, sizes, BRICK)
    ]

    def shifted(role, cx, cy):
        tile = halo1[role, cx, cy]
        col = cx * CY + cy
        if cx in (0, CX - 1):
            tile = tile + jnp.where(row8 == 0, edge[0][0 if cx == 0 else 1], 0.0)
        if cy in (0, CY - 1):
            tile = tile + jnp.where(row8 == 1, edge[1][0 if cy == 0 else 1], 0.0)
        if role != 1:
            tile = tile + jnp.where(row8 == 2, edge[2][role // 2], 0.0)
        return jnp.where(row8 == 7, marks[role, col : col + 1, :], tile)

    def windows(below, middle, above, lanes):
        return (
            jnp.where(lanes >= 80, below, middle),
            jnp.where(lanes >= 112, below, middle),
            jnp.where(lanes < 16, above, middle),
            jnp.where(lanes < 48, above, middle),
        )

    for cx in range(CX):
        for cy in range(CY):
            tiles = windows(*[shifted(role, cx, cy) for role in range(3)], lane8)
            for g in range(NGRP):
                window[(cx * CY + cy) * NGRP + g] = tiles[g]

    def build(step, carry):
        block, g = step // NGRP, step % NGRP
        column = (block // NBY) * CY + block % NBY
        mine = target[step]
        tx, ty, tz, tb = [jnp.broadcast_to(mine[:, k : k + 1], (GROUP, BLOCK)) for k in range(4)]
        total = [jnp.zeros((GROUP, BLOCK), jnp.float32) for _ in range(3)]
        for c in range(9):
            tile = window[(column + (c // 3) * CY + c % 3) * NGRP + g]
            bit = jnp.right_shift(tile[7:8].astype(jnp.int32), block)
            seen = jnp.bitwise_and(bit, 1) == 1
            sx = jnp.where(seen, tile[0:1], FAR)
            dx, dy, dz = tx - sx, ty - tile[1:2], tz - tile[2:3]
            if c == 4:
                itself = iota((GROUP, BLOCK), 0) + g * GROUP == iota((GROUP, BLOCK), 1)
                dx = jnp.where(itself, FAR, dx)
            q = dx * dx + dy * dy + dz * dz
            inv = lax.rsqrt(q)
            inv2 = inv * inv
            margin = jnp.maximum(1.0 - q * (1.0 / CUTOFF_SQUARED), 0.0)
            scaled = q * (q * inv) * (tb * tile[3:4])
            damp = jnp.exp(-scaled)
            rest = 1.0 - damp
            inner = (margin * margin) * (inv2 * inv) * rest
            root = (3.0 * inv) * jnp.maximum(rest - scaled * damp, 1e-20)
            scale = margin * inv2 * root * lax.rsqrt(root)
            ax, ay, az = scale * dx, scale * dy, scale * dz
            slot = step * 9 + c
            px[slot], py[slot], pz[slot], inner_s[slot] = ax, ay, az, inner
            vx, vy, vz = tile[4:5], tile[5:6], tile[6:7]
            along = ax * vx + ay * vy + az * vz
            total[0] = total[0] + (along * ax - inner * vx)
            total[1] = total[1] + (along * ay - inner * vy)
            total[2] = total[2] + (along * az - inner * vz)
        for k in range(3):
            sums[block, k, pl.ds(pl.multiple_of(g * GROUP, GROUP), GROUP)] = total[k]
        return carry

    lax.fori_loop(0, NBLK * NGRP, build, 0)

    def apply(step, carry):
        block, g = step // NGRP, step % NGRP
        column = (block // NBY) * CY + block % NBY
        total = [jnp.zeros((GROUP, BLOCK), jnp.float32) for _ in range(3)]
        for c in range(9):
            tile = moved[(column + (c // 3) * CY + c % 3) * NGRP + g]
            slot = step * 9 + c
            ax, ay, az, inner = px[slot], py[slot], pz[slot], inner_s[slot]
            vx, vy, vz = tile[0:1], tile[1:2], tile[2:3]
            along = ax * vx + ay * vy + az * vz
            total[0] = total[0] + (along * ax - inner * vx)
            total[1] = total[1] + (along * ay - inner * vy)
            total[2] = total[2] + (along * az - inner * vz)
        for k in range(3):
            sums[block, k, pl.ds(pl.multiple_of(g * GROUP, GROUP), GROUP)] = total[k]
        return carry

    ones = jnp.ones((8, BLOCK), jnp.float32)

    def next_basis(level, halo):
        for b in range(NBLK):
            field = [dot_lanes(ones, sums[b, k]) for k in range(3)]
            field = jnp.where(row8 == 0, field[0], jnp.where(row8 == 1, field[1], field[2]))
            v = basis[level, b]
            rows = side[b]
            image = rows[0:1] * v - rows[1:2] * field
            image = (image - CENTRE * v) * (1.0 / HALF)
            if level > 0:
                image = 2.0 * image - basis[level - 1, b]
            image = jnp.where(row8 < 3, image, 0.0)
            basis[level + 1, b] = image
            if halo is not None:
                halo[1, 1 + b // NBY, 1 + b % NBY] = image[:4]

    lane4 = iota((4, BLOCK), 1)
    started = first + tables
    for level, halo in ((0, halo2), (1, halo3)):
        next_basis(level, halo)
        copies = halo_copies(halo, sends.at[level + 1], recvs.at[level + 1], me, sizes)
        for copy in copies:
            copy.start()
        for copy in copies:
            copy.wait_recv()
        for cx in range(CX):
            for cy in range(CY):
                tiles = windows(*[halo[role, cx, cy] for role in range(3)], lane4)
                for g in range(NGRP):
                    moved[(cx * CY + cy) * NGRP + g] = tiles[g]
        lax.fori_loop(0, NBLK * NGRP, apply, 0)
        started = started + copies
    next_basis(2, None)

    rows = []
    for a, b in GRAM:
        part = jnp.sum(basis[a] * basis[b], axis=0)
        rows.append(jnp.sum(part, axis=0, keepdims=True))
    rows.append(jnp.zeros((16 - len(GRAM), BLOCK), jnp.float32))
    gram_out[...] = jnp.concatenate(rows, axis=0)
    for b in range(NBLK):
        stacked = jnp.concatenate([basis[k, b] for k in range(4)], axis=0)
        basis_out[:, b * BLOCK : (b + 1) * BLOCK] = dot_lanes(stacked, order[b])
    for copy in started:
        copy.wait_send()


def reduce_kernel(sizes, basis, gram, polar, dipoles, residual, *scratch):
    slots, send_sems, recv_sems = scratch[0:3], scratch[3:6], scratch[6:9]
    me = place_of(sizes)
    partners = []
    for axis, n in enumerate(sizes):
        for s in range(1, n):
            step = [0, 0, 0]
            step[axis] = s
            partners.append(neighbour(me, sizes, step))
    barrier = greet(partners)
    total = gram[...]
    for axis, n in enumerate(sizes):
        slot, send, recv = slots[axis], send_sems[axis], recv_sems[axis]
        slot[me[axis]] = total
        if axis == 0:
            pl.semaphore_wait(barrier, len(partners))
        copies = []
        for s in range(1, n):
            step = [0, 0, 0]
            step[axis] = s
            copies.append(
                pltpu.make_async_remote_copy(
                    src_ref=slot.at[me[axis]],
                    dst_ref=slot.at[me[axis]],
                    send_sem=send.at[s - 1],
                    recv_sem=recv.at[s - 1],
                    device_id=neighbour(me, sizes, step),
                    device_id_type=MESH,
                )
            )
        for copy in copies:
            copy.start()
        for copy in copies:
            copy.wait()
        total = slot[0]
        for k in range(1, n):
            total = total + slot[k]

    whole = jnp.sum(total, axis=1, keepdims=True)
    products = {}
    for k, (a, b) in enumerate(GRAM):
        products[a, b] = products[b, a] = whole[k : k + 1, :]

    def inner(left, right):
        value = 0.0
        for a, p in enumerate(left):
            for b, q in enumerate(right):
                if p is not None and q is not None:
                    value = value + p * q * products[a, b]
        return value

    def plus(p, q):
        return q if p is None else (p if q is None else p + q)

    def times(scale, p):
        return None if p is None else scale * p

    def applied(c):
        out = [times(CENTRE, p) for p in c]
        if c[0] is not None:
            out[1] = plus(out[1], HALF * c[0])
        for k in (1, 2):
            if c[k] is not None:
                out[k - 1] = plus(out[k - 1], (0.5 * HALF) * c[k])
                out[k + 1] = plus(out[k + 1], (0.5 * HALF) * c[k])
        return out

    one = jnp.ones((1, 1), jnp.float32)
    left = [one, None, None, None]
    direction = list(left)
    answer = [None] * 4
    norm = products[0, 0]
    for _ in range(3):
        image = applied(direction)
        step = norm / inner(direction, image)
        answer = [plus(p, times(step, q)) for p, q in zip(answer, direction)]
        left = [plus(p, times(-step, q)) for p, q in zip(left, image)]
        after = inner(left, left)
        direction = [plus(p, times(after / norm, q)) for p, q in zip(left, direction)]
        norm = after

    def combined(coefficients):
        value = 0.0
        for k, c in enumerate(coefficients):
            if c is not None:
                value = value + c * basis[8 * k : 8 * k + 3, :]
        return value

    dipoles[...] = combined(answer)
    residual[...] = polar[...] * combined(left)


def per_device(
    sizes, coords, polarizability, external_field, bead_live,
    ghost_x, ghost_y, ghost_z, pair_blocks, pair_live,
):
    nloc = coords.shape[1]
    npair = pair_live.shape[0]
    vmem = pl.BlockSpec(memory_space=pltpu.VMEM)
    f32 = jnp.float32
    polar = polarizability.reshape(1, nloc)
    tensors = pltpu.VMEM((NBLK * NGRP * 9, GROUP, BLOCK), f32)
    steps = len(OFFSETS)
    basis, gram = pl.pallas_call(
        functools.partial(field_kernel, sizes),
        out_shape=(
            jax.ShapeDtypeStruct((32, nloc), f32),
            jax.ShapeDtypeStruct((16, BLOCK), f32),
        ),
        in_specs=[vmem] * 9,
        out_specs=(vmem, vmem),
        scratch_shapes=[
            pltpu.VMEM((3, CX, CY, 8, BLOCK), f32),
            pltpu.VMEM((3, CX, CY, 4, BLOCK), f32),
            pltpu.VMEM((3, CX, CY, 4, BLOCK), f32),
            pltpu.VMEM((2, 3, 16, BLOCK), f32),
            pltpu.VMEM((2, 24, BLOCK), f32),
            pltpu.VMEM((2, 16, BLOCK), f32),
            pltpu.VMEM((2, 24, BLOCK), f32),
            pltpu.SemaphoreType.DMA((3, steps)),
            pltpu.SemaphoreType.DMA((3, steps)),
            pltpu.SemaphoreType.DMA((8,)),
            pltpu.SemaphoreType.DMA((8,)),
            pltpu.VMEM((NBLK, BLOCK, BLOCK), f32),
            pltpu.VMEM((NBLK, 8, BLOCK), f32),
            pltpu.VMEM((NBLK * NGRP, GROUP, 8), f32),
            pltpu.VMEM((NCOL * NGRP, 8, BLOCK), f32),
            pltpu.VMEM((NCOL * NGRP, 4, BLOCK), f32),
            pltpu.VMEM((3, NCOL, BLOCK), f32),
            tensors, tensors, tensors, tensors,
            pltpu.VMEM((NBLK, 3, BLOCK, BLOCK), f32),
            pltpu.VMEM((4, NBLK, 8, BLOCK), f32),
        ],
        compiler_params=pltpu.CompilerParams(
            collective_id=0, has_side_effects=True, vmem_limit_bytes=48 * 2**20
        ),
    )(
        coords, polar, external_field, bead_live.reshape(1, nloc),
        ghost_x, ghost_y, ghost_z, pair_blocks, pair_live.reshape(1, npair),
    )
    return pl.pallas_call(
        functools.partial(reduce_kernel, sizes),
        out_shape=(
            jax.ShapeDtypeStruct((3, nloc), f32),
            jax.ShapeDtypeStruct((3, nloc), f32),
        ),
        in_specs=[vmem] * 3,
        out_specs=(vmem, vmem),
        scratch_shapes=[pltpu.VMEM((n, 16, BLOCK), f32) for n in sizes]
        + [pltpu.SemaphoreType.DMA((n - 1,)) for n in sizes] * 2,
        compiler_params=pltpu.CompilerParams(collective_id=1, has_side_effects=True),
    )(basis, gram, polar)


def solution(mesh):
    sizes = tuple(mesh.shape[name] for name in ("gx", "gy", "gz"))
    wide = P(None, ("gx", "gy", "gz"))
    flat = P(("gx", "gy", "gz"))
    return jax.shard_map(
        functools.partial(per_device, sizes),
        mesh=mesh,
        in_specs=(wide, flat, wide, flat, wide, wide, wide, wide, flat),
        out_specs=(wide, wide),
        check_vma=False,
    )
```

```python
import functools
import math

import jax
import jax.numpy as jnp
from jax import lax
from jax.experimental import pallas as pl
from jax.experimental.pallas import tpu as pltpu
from jax.sharding import PartitionSpec as P

BLOCK = 128
NBX, NBY = 4, 2
NBLK = NBX * NBY
CX, CY = NBX + 2, NBY + 2
NCOL = CX * CY
GROUP = 32
NGRP = BLOCK // GROUP
BRICK = (16.0, 8.0, 8.0)
CUTOFF_SQUARED = 12.25
THOLE_FACTOR = 0.02
CENTRE, HALF = 12.5, 8.5
FAR = 1.0e6
MESH = pl.DeviceIdType.MESH
HIGHEST = lax.Precision.HIGHEST
OFFSETS = [
    (x, y, z)
    for x in (-1, 0, 1)
    for y in (-1, 0, 1)
    for z in (-1, 0, 1)
    if (x, y, z) != (0, 0, 0)
]
GRAM = [(a, b) for a in range(4) for b in range(a, 4)]


def dot_rows(left, right, precision=HIGHEST):
    return lax.dot_general(
        left, right, (((1,), (0,)), ((), ())), precision=precision,
        preferred_element_type=jnp.float32,
    )


def dot_lanes(left, right, precision=HIGHEST):
    return lax.dot_general(
        left, right, (((1,), (1,)), ((), ())), precision=precision,
        preferred_element_type=jnp.float32,
    )


def iota(shape, axis):
    return lax.broadcasted_iota(jnp.int32, shape, axis)


def own_span(step, count):
    return (0, count) if step == 0 else ((count - 1, 1) if step > 0 else (0, 1))


def halo_span(step, count):
    return (1, count) if step == 0 else ((0, 1) if step > 0 else (count + 1, 1))


def inverse_list(list_ref, row, first, entries, tables):
    blocks = jnp.zeros((tables, BLOCK), jnp.float32)
    lanes = jnp.zeros((tables, BLOCK), jnp.float32)
    spot = iota((BLOCK, BLOCK), 1).astype(jnp.float32)
    for r in range(entries // BLOCK):
        entry = list_ref[row : row + 1, r * BLOCK : (r + 1) * BLOCK]
        high = jnp.right_shift(entry, 7) - first
        low = jnp.bitwise_and(entry, BLOCK - 1)
        pick = (iota((tables, BLOCK), 0) == high).astype(jnp.float32)
        place = (iota((BLOCK, BLOCK), 0) == low).astype(jnp.float32)
        both = jnp.concatenate([place, place * spot], axis=0).astype(jnp.bfloat16)
        found = dot_lanes(pick.astype(jnp.bfloat16), both, None)
        blocks = blocks + found[:, :BLOCK] * float(r + 1)
        lanes = lanes + found[:, BLOCK:]
    return blocks, lanes


def inverse_blocks(list_ref, row, entries):
    rows = entries // BLOCK
    total = jnp.zeros((rows, BLOCK), jnp.float32)
    for r in range(rows):
        entry = list_ref[row : row + 1, r * BLOCK : (r + 1) * BLOCK]
        high = jnp.right_shift(entry, 7)
        low = jnp.bitwise_and(entry, BLOCK - 1)
        pick = jnp.where(iota((rows, BLOCK), 0) == high, float(r), 0.0)
        place = (iota((BLOCK, BLOCK), 0) == low).astype(jnp.float32)
        total = total + dot_lanes(
            pick.astype(jnp.bfloat16), place.astype(jnp.bfloat16), None
        )
    return total


def look_up(table, index):
    high = jnp.right_shift(index, 7)
    low = jnp.bitwise_and(index, BLOCK - 1)
    out = jnp.zeros(index.shape, jnp.float32)
    for r in range(table.shape[0]):
        row = jnp.broadcast_to(table[r : r + 1, :], index.shape)
        out = jnp.where(high == r, jnp.take_along_axis(row, low, axis=1), out)
    return out


def place_of(sizes):
    return tuple(lax.axis_index(name) for name in ("gx", "gy", "gz"))


def neighbour(me, sizes, step):
    return tuple(lax.rem(m + s + n, n) for m, s, n in zip(me, step, sizes))


def greet(targets):
    barrier = pltpu.get_barrier_semaphore()
    for target in targets:
        pl.semaphore_signal(barrier, inc=1, device_id=target, device_id_type=MESH)
    return barrier


def halo_copies(buffer, send_sem, recv_sem, me, sizes):
    copies = []
    for n, step in enumerate(OFFSETS):
        (xs, xn), (ys, yn) = own_span(step[0], NBX), own_span(step[1], NBY)
        (xd, _), (yd, _) = halo_span(step[0], NBX), halo_span(step[1], NBY)
        copies.append(
            pltpu.make_async_remote_copy(
                src_ref=buffer.at[1, pl.ds(1 + xs, xn), pl.ds(1 + ys, yn)],
                dst_ref=buffer.at[1 - step[2], pl.ds(xd, xn), pl.ds(yd, yn)],
                send_sem=send_sem.at[n],
                recv_sem=recv_sem.at[n],
                device_id=neighbour(me, sizes, step),
                device_id_type=MESH,
            )
        )
    return copies


def partners_of(me, sizes):
    steps = []
    for axis, n in enumerate(sizes):
        for s in range(1, n):
            step = [0, 0, 0]
            step[axis] = s if 2 * s <= n else s - n
            steps.append(tuple(step))
    return steps


def reduce_along(axis, n, total, slot, send, recv, me, sizes):
    slot[me[axis]] = total
    copies = []
    for s in range(1, n):
        step = [0, 0, 0]
        step[axis] = s
        copies.append(
            pltpu.make_async_remote_copy(
                src_ref=slot.at[me[axis]],
                dst_ref=slot.at[me[axis]],
                send_sem=send.at[s - 1],
                recv_sem=recv.at[s - 1],
                device_id=neighbour(me, sizes, step),
                device_id_type=MESH,
            )
        )
    for copy in copies:
        copy.start()
    for copy in copies:
        copy.wait_recv()
    total = slot[0]
    for k in range(1, n):
        total = total + slot[k]
    return total, copies


def gradient_steps(products):
    def inner(left, right):
        value = 0.0
        for a, p in enumerate(left):
            for b, q in enumerate(right):
                if p is not None and q is not None:
                    value = value + p * q * products[a, b]
        return value

    def plus(p, q):
        return q if p is None else (p if q is None else p + q)

    def times(scale, p):
        return None if p is None else scale * p

    def applied(c):
        out = [times(CENTRE, p) for p in c]
        if c[0] is not None:
            out[1] = plus(out[1], HALF * c[0])
        for k in (1, 2):
            if c[k] is not None:
                out[k - 1] = plus(out[k - 1], (0.5 * HALF) * c[k])
                out[k + 1] = plus(out[k + 1], (0.5 * HALF) * c[k])
        return out

    left = [jnp.ones((1, 1), jnp.float32), None, None, None]
    direction = list(left)
    answer = [None] * 4
    norm = products[0, 0]
    for _ in range(3):
        image = applied(direction)
        step = norm / inner(direction, image)
        answer = [plus(p, times(step, q)) for p, q in zip(answer, direction)]
        left = [plus(p, times(-step, q)) for p, q in zip(left, image)]
        after = inner(left, left)
        direction = [plus(p, times(after / norm, q)) for p, q in zip(left, direction)]
        norm = after
    return answer, left


def field_kernel(
    sizes,
    coords_in, polar_in, external_in, live_in, ghost_x_in, ghost_y_in, ghost_z_in,
    pairs_in, alive_in,
    dipoles, residual,
    coords, polar, external, live, ghost_x, ghost_y, ghost_z, pairs, alive, loads,
    halo1, halo2, halo3, tabs_y, tabs_z, own_y, own_z, sends, recvs, tab_sends, tab_recvs,
    order, side, target, window, moved, marks, px, py, pz, inner_s, sums, basis, flat,
    slot_x, slot_y, slot_z, send_x, send_y, send_z, recv_x, recv_y, recv_z,
):
    me = place_of(sizes)
    outside = (
        coords_in, polar_in, external_in, live_in, ghost_x_in, ghost_y_in, ghost_z_in,
        pairs_in, alive_in,
    )
    inside = (coords, polar, external, live, ghost_x, ghost_y, ghost_z, pairs, alive)
    arriving = [
        pltpu.make_async_copy(far, near, loads.at[n])
        for n, (far, near) in enumerate(zip(outside, inside))
    ]
    for copy in arriving:
        copy.start()
    friends = dict.fromkeys(list(OFFSETS) + partners_of(me, sizes))
    barrier = greet([neighbour(me, sizes, step) for step in friends])
    for copy in arriving:
        copy.wait()

    up_blocks, up_lanes = inverse_list(ghost_x, 0, 0, 2 * BLOCK, NBLK)
    down_blocks, down_lanes = inverse_list(ghost_x, 1, 0, 2 * BLOCK, NBLK)
    upper = iota((NBLK, BLOCK), 0) >= NBLK - NBY
    x_spot = jnp.where(
        upper, (up_blocks - 1.0) * BLOCK + up_lanes, (down_blocks - 1.0) * BLOCK + down_lanes
    )
    x_spot = jnp.maximum(x_spot, 0.0)
    lane = iota((1, BLOCK), 1)
    lane_f = lane.astype(jnp.float32)

    for b in range(NBLK):
        cut = slice(b * BLOCK, (b + 1) * BLOCK)
        alpha = polar[0:1, cut]
        living = live[0:1, cut].astype(jnp.float32)
        place = coords[:, cut]
        rhs = external[:, cut] * living
        code = lane_f + x_spot[b : b + 1, :] * BLOCK
        beta = lax.rsqrt(alpha) * math.sqrt(THOLE_FACTOR)
        tile = jnp.concatenate([place, beta, rhs, code], axis=0)
        more = jnp.concatenate(
            [living / alpha, living, jnp.zeros((6, BLOCK), jnp.float32)], axis=0
        )
        column = jnp.transpose(tile)
        z_row = place[2:3, :]
        z_col = column[:, 2:3]
        before = jnp.logical_or(
            z_row < z_col,
            jnp.logical_and(z_row == z_col, iota((BLOCK, BLOCK), 1) < iota((BLOCK, BLOCK), 0)),
        )
        rank = jnp.sum(before.astype(jnp.float32), axis=1, keepdims=True)
        one_hot = (rank == iota((BLOCK, BLOCK), 1).astype(jnp.float32)).astype(jnp.float32)
        order[b] = one_hot
        ranked = dot_rows(jnp.concatenate([tile, more], axis=0), one_hot)
        halo1[1, 1 + b // NBY, 1 + b % NBY] = ranked[:8]
        side[b] = ranked[8:]
        basis[0, b] = jnp.concatenate(
            [ranked[4:7], jnp.zeros((5, BLOCK), jnp.float32)], axis=0
        )
        flipped = jnp.transpose(ranked[:8])
        for g in range(NGRP):
            target[b * NGRP + g] = flipped[g * GROUP : (g + 1) * GROUP]

    pl.semaphore_wait(barrier, len(friends))
    first = halo_copies(halo1, sends.at[0], recvs.at[0], me, sizes)
    for copy in first:
        copy.start()

    for row in range(2):
        blocks, lanes = inverse_list(ghost_y, row, 0, 6 * BLOCK, 12)
        own_y[row, 0:12] = (blocks - 1.0) * BLOCK + lanes
        own_z[row] = inverse_blocks(ghost_z, row, 24 * BLOCK)
    tables = []
    for row, step_y in enumerate((1, -1)):
        for step_z in (-1, 0, 1):
            n = len(tables)
            tables.append(
                pltpu.make_async_remote_copy(
                    src_ref=own_y.at[row],
                    dst_ref=tabs_y.at[row, 1 - step_z],
                    send_sem=tab_sends.at[n],
                    recv_sem=tab_recvs.at[n],
                    device_id=neighbour(me, sizes, (0, step_y, step_z)),
                    device_id_type=MESH,
                )
            )
    for row, step_z in enumerate((1, -1)):
        n = len(tables)
        tables.append(
            pltpu.make_async_remote_copy(
                src_ref=own_z.at[row],
                dst_ref=tabs_z.at[row],
                send_sem=tab_sends.at[n],
                recv_sem=tab_recvs.at[n],
                device_id=neighbour(me, sizes, (0, 0, step_z)),
                device_id_type=MESH,
            )
        )
    for copy in tables:
        copy.start()

    count = pairs.shape[1]
    bits = jnp.left_shift(alive[0:1, :], pairs[0:1, :]).astype(jnp.float32)
    bits = jnp.broadcast_to(bits, (8, count)).astype(jnp.bfloat16)
    listed = (iota((BLOCK, count), 0) == pairs[1:2, :]).astype(jnp.float32)
    listed_by = dot_lanes(bits, listed.astype(jnp.bfloat16), None)

    for copy in first:
        copy.wait_recv()
    for copy in tables:
        copy.wait_recv()

    for role in range(3):
        for part in range(NCOL // 8):
            codes = jnp.concatenate(
                [
                    halo1[role, c // CY, c % CY, 7:8, :]
                    for c in range(part * 8, part * 8 + 8)
                ],
                axis=0,
            ).astype(jnp.int32)
            spot = jnp.right_shift(codes, 7)
            own_lane = jnp.bitwise_and(codes, BLOCK - 1)
            col = iota((8, BLOCK), 0) + part * 8
            cx, cy = jnp.right_shift(col, 2), jnp.bitwise_and(col, 3)
            block_y = jnp.bitwise_and(cy + 1, 1)
            entry = ((cx - 1) * NBY + block_y) * BLOCK + own_lane
            entry = jnp.where(cx == 0, NBLK * BLOCK + spot, entry)
            entry = jnp.where(cx == CX - 1, (NBLK + NBY) * BLOCK + spot, entry)
            low = look_up(tabs_y[0, role, 0:12], entry)
            high = look_up(tabs_y[1, role, 0:12], entry)
            found = jnp.where(cy == 0, low, jnp.where(cy == CY - 1, high, 0.0))
            valid = found >= 0.0
            found = jnp.maximum(found, 0.0).astype(jnp.int32)
            entry = jnp.where(cy == 0, 12 * BLOCK + found, entry)
            entry = jnp.where(cy == CY - 1, 18 * BLOCK + found, entry)
            if role == 1:
                block = jnp.right_shift(entry, 7)
            else:
                layer = look_up(tabs_z[role // 2], entry)
                block = layer.astype(jnp.int32) + (24 if role == 0 else 48)
            mark = jnp.take_along_axis(listed_by, block, axis=1)
            marks[role, part * 8 : part * 8 + 8] = jnp.where(valid, mark, 0.0)

    row8 = iota((8, BLOCK), 0)
    lane8 = iota((8, BLOCK), 1)
    edge = [
        (jnp.where(m == 0, -n * size, 0.0), jnp.where(m == n - 1, n * size, 0.0))
        for m, n, size in zip(me, sizes, BRICK)
    ]

    def shifted(role, cx, cy):
        tile = halo1[role, cx, cy]
        col = cx * CY + cy
        if cx in (0, CX - 1):
            tile = tile + jnp.where(row8 == 0, edge[0][0 if cx == 0 else 1], 0.0)
        if cy in (0, CY - 1):
            tile = tile + jnp.where(row8 == 1, edge[1][0 if cy == 0 else 1], 0.0)
        if role != 1:
            tile = tile + jnp.where(row8 == 2, edge[2][role // 2], 0.0)
        return jnp.where(row8 == 7, marks[role, col : col + 1, :], tile)

    def windows(below, middle, above, lanes):
        return (
            jnp.where(lanes >= 80, below, middle),
            jnp.where(lanes >= 112, below, middle),
            jnp.where(lanes < 16, above, middle),
            jnp.where(lanes < 48, above, middle),
        )

    for cx in range(CX):
        for cy in range(CY):
            tiles = windows(*[shifted(role, cx, cy) for role in range(3)], lane8)
            for g in range(NGRP):
                window[(cx * CY + cy) * NGRP + g] = tiles[g]

    def build(step, carry):
        block, g = step // NGRP, step % NGRP
        column = (block // NBY) * CY + block % NBY
        mine = target[step]
        tx, ty, tz, tb = [jnp.broadcast_to(mine[:, k : k + 1], (GROUP, BLOCK)) for k in range(4)]
        total = [jnp.zeros((GROUP, BLOCK), jnp.float32) for _ in range(3)]
        for c in range(9):
            tile = window[(column + (c // 3) * CY + c % 3) * NGRP + g]
            bit = jnp.right_shift(tile[7:8].astype(jnp.int32), block)
            seen = jnp.bitwise_and(bit, 1) == 1
            sx = jnp.where(seen, tile[0:1], FAR)
            dx, dy, dz = tx - sx, ty - tile[1:2], tz - tile[2:3]
            if c == 4:
                itself = iota((GROUP, BLOCK), 0) + g * GROUP == iota((GROUP, BLOCK), 1)
                dx = jnp.where(itself, FAR, dx)
            q = dx * dx + dy * dy + dz * dz
            inv = lax.rsqrt(q)
            inv2 = inv * inv
            margin = jnp.maximum(1.0 - q * (1.0 / CUTOFF_SQUARED), 0.0)
            scaled = q * (q * inv) * (tb * tile[3:4])
            damp = jnp.exp(-scaled)
            rest = 1.0 - damp
            inner = (margin * margin) * (inv2 * inv) * rest
            root = (3.0 * inv) * jnp.maximum(rest - scaled * damp, 1e-20)
            scale = margin * inv2 * root * lax.rsqrt(root)
            ax, ay, az = scale * dx, scale * dy, scale * dz
            slot = step * 9 + c
            px[slot], py[slot], pz[slot], inner_s[slot] = ax, ay, az, inner
            vx, vy, vz = tile[4:5], tile[5:6], tile[6:7]
            along = ax * vx + ay * vy + az * vz
            total[0] = total[0] + (along * ax - inner * vx)
            total[1] = total[1] + (along * ay - inner * vy)
            total[2] = total[2] + (along * az - inner * vz)
        for k in range(3):
            sums[block, k, pl.ds(pl.multiple_of(g * GROUP, GROUP), GROUP)] = total[k]
        return carry

    lax.fori_loop(0, NBLK * NGRP, build, 0)

    def apply(step, carry):
        block, g = step // NGRP, step % NGRP
        column = (block // NBY) * CY + block % NBY
        total = [jnp.zeros((GROUP, BLOCK), jnp.float32) for _ in range(3)]
        for c in range(9):
            tile = moved[(column + (c // 3) * CY + c % 3) * NGRP + g]
            slot = step * 9 + c
            ax, ay, az, inner = px[slot], py[slot], pz[slot], inner_s[slot]
            vx, vy, vz = tile[0:1], tile[1:2], tile[2:3]
            along = ax * vx + ay * vy + az * vz
            total[0] = total[0] + (along * ax - inner * vx)
            total[1] = total[1] + (along * ay - inner * vy)
            total[2] = total[2] + (along * az - inner * vz)
        for k in range(3):
            sums[block, k, pl.ds(pl.multiple_of(g * GROUP, GROUP), GROUP)] = total[k]
        return carry

    ones = jnp.ones((8, BLOCK), jnp.float32)

    def next_basis(level, halo):
        for b in range(NBLK):
            field = [dot_lanes(ones, sums[b, k]) for k in range(3)]
            field = jnp.where(row8 == 0, field[0], jnp.where(row8 == 1, field[1], field[2]))
            v = basis[level, b]
            rows = side[b]
            image = rows[0:1] * v - rows[1:2] * field
            image = (image - CENTRE * v) * (1.0 / HALF)
            if level > 0:
                image = 2.0 * image - basis[level - 1, b]
            image = jnp.where(row8 < 3, image, 0.0)
            basis[level + 1, b] = image
            if halo is not None:
                halo[1, 1 + b // NBY, 1 + b % NBY] = image[:4]

    lane4 = iota((4, BLOCK), 1)
    started = first + tables
    for level, halo in ((0, halo2), (1, halo3)):
        next_basis(level, halo)
        copies = halo_copies(halo, sends.at[level + 1], recvs.at[level + 1], me, sizes)
        for copy in copies:
            copy.start()
        for copy in copies:
            copy.wait_recv()
        for cx in range(CX):
            for cy in range(CY):
                tiles = windows(*[halo[role, cx, cy] for role in range(3)], lane4)
                for g in range(NGRP):
                    moved[(cx * CY + cy) * NGRP + g] = tiles[g]
        lax.fori_loop(0, NBLK * NGRP, apply, 0)
        started = started + copies
    next_basis(2, None)

    rows = []
    for a, b in GRAM:
        part = jnp.sum(basis[a] * basis[b], axis=0)
        rows.append(jnp.sum(part, axis=0, keepdims=True))
    rows.append(jnp.zeros((BLOCK - len(GRAM), BLOCK), jnp.float32))
    total = dot_lanes(ones, jnp.concatenate(rows, axis=0))[0:1]
    slots, sent, got = (slot_x, slot_y, slot_z), (send_x, send_y, send_z), (recv_x, recv_y, recv_z)
    for axis, n in enumerate(sizes):
        total, copies = reduce_along(
            axis, n, total, slots[axis], sent[axis], got[axis], me, sizes
        )
        started = started + copies
        if axis == 0:
            for b in range(NBLK):
                stacked = jnp.concatenate([basis[k, b] for k in range(4)], axis=0)
                flat[:, b * BLOCK : (b + 1) * BLOCK] = dot_lanes(stacked, order[b])
    products = {}
    for k, (a, b) in enumerate(GRAM):
        products[a, b] = products[b, a] = total[:, k : k + 1]
    answer, left = gradient_steps(products)

    def combined(coefficients):
        value = 0.0
        for k, c in enumerate(coefficients):
            if c is not None:
                value = value + c * flat[8 * k : 8 * k + 3, :]
        return value

    dipoles[...] = combined(answer)
    residual[...] = polar[...] * combined(left)
    for copy in started:
        copy.wait_send()


def per_device(
    sizes, coords, polarizability, external_field, bead_live,
    ghost_x, ghost_y, ghost_z, pair_blocks, pair_live,
):
    nloc = coords.shape[1]
    vmem = pl.BlockSpec(memory_space=pltpu.VMEM)
    f32 = jnp.float32
    operands = (
        coords, polarizability.reshape(1, nloc), external_field, bead_live.reshape(1, nloc),
        ghost_x, ghost_y, ghost_z, pair_blocks, pair_live.reshape(1, pair_live.shape[0]),
    )
    tensors = pltpu.VMEM((NBLK * NGRP * 9, GROUP, BLOCK), f32)
    steps = len(OFFSETS)
    return pl.pallas_call(
        functools.partial(field_kernel, sizes),
        out_shape=(jax.ShapeDtypeStruct((3, nloc), f32),) * 2,
        in_specs=[pl.BlockSpec(memory_space=pl.ANY)] * len(operands),
        out_specs=(vmem, vmem),
        scratch_shapes=[pltpu.VMEM(x.shape, x.dtype) for x in operands]
        + [
            pltpu.SemaphoreType.DMA((len(operands),)),
            pltpu.VMEM((3, CX, CY, 8, BLOCK), f32),
            pltpu.VMEM((3, CX, CY, 4, BLOCK), f32),
            pltpu.VMEM((3, CX, CY, 4, BLOCK), f32),
            pltpu.VMEM((2, 3, 16, BLOCK), f32),
            pltpu.VMEM((2, 24, BLOCK), f32),
            pltpu.VMEM((2, 16, BLOCK), f32),
            pltpu.VMEM((2, 24, BLOCK), f32),
            pltpu.SemaphoreType.DMA((3, steps)),
            pltpu.SemaphoreType.DMA((3, steps)),
            pltpu.SemaphoreType.DMA((8,)),
            pltpu.SemaphoreType.DMA((8,)),
            pltpu.VMEM((NBLK, BLOCK, BLOCK), f32),
            pltpu.VMEM((NBLK, 8, BLOCK), f32),
            pltpu.VMEM((NBLK * NGRP, GROUP, 8), f32),
            pltpu.VMEM((NCOL * NGRP, 8, BLOCK), f32),
            pltpu.VMEM((NCOL * NGRP, 4, BLOCK), f32),
            pltpu.VMEM((3, NCOL, BLOCK), f32),
            tensors, tensors, tensors, tensors,
            pltpu.VMEM((NBLK, 3, BLOCK, BLOCK), f32),
            pltpu.VMEM((4, NBLK, 8, BLOCK), f32),
            pltpu.VMEM((32, nloc), f32),
        ]
        + [pltpu.VMEM((n, 1, BLOCK), f32) for n in sizes]
        + [pltpu.SemaphoreType.DMA((n - 1,)) for n in sizes] * 2,
        compiler_params=pltpu.CompilerParams(
            collective_id=0, has_side_effects=True, vmem_limit_bytes=48 * 2**20
        ),
    )(*operands)


def solution(mesh):
    sizes = tuple(mesh.shape[name] for name in ("gx", "gy", "gz"))
    wide = P(None, ("gx", "gy", "gz"))
    flat = P(("gx", "gy", "gz"))
    return jax.shard_map(
        functools.partial(per_device, sizes),
        mesh=mesh,
        in_specs=(wide, flat, wide, flat, wide, wide, wide, wide, flat),
        out_specs=(wide, wide),
        check_vma=False,
    )
```

```python
import functools
import math

import jax
import jax.numpy as jnp
from jax import lax
from jax.experimental import pallas as pl
from jax.experimental.pallas import tpu as pltpu
from jax.sharding import PartitionSpec as P

BLOCK = 128
NBX, NBY = 4, 2
NBLK = NBX * NBY
CX, CY = NBX + 2, NBY + 2
NCOL = CX * CY
GROUP = 32
NGRP = BLOCK // GROUP
BRICK = (16.0, 8.0, 8.0)
CUTOFF_SQUARED = 12.25
THOLE_FACTOR = 0.02
CENTRE, HALF = 12.5, 8.5
FAR = 1.0e6
MESH = pl.DeviceIdType.MESH
HIGHEST = lax.Precision.HIGHEST
OFFSETS = [
    (x, y, z)
    for x in (-1, 0, 1)
    for y in (-1, 0, 1)
    for z in (-1, 0, 1)
    if (x, y, z) != (0, 0, 0)
]
GRAM = [(a, b) for a in range(4) for b in range(a, 4)]


def dot_rows(left, right, precision=HIGHEST):
    return lax.dot_general(
        left, right, (((1,), (0,)), ((), ())), precision=precision,
        preferred_element_type=jnp.float32,
    )


def dot_lanes(left, right, precision=HIGHEST):
    return lax.dot_general(
        left, right, (((1,), (1,)), ((), ())), precision=precision,
        preferred_element_type=jnp.float32,
    )


def halves(x, parts):
    out = []
    for _ in range(parts):
        part = x.astype(jnp.bfloat16)
        out.append(part)
        x = x - part.astype(jnp.float32)
    return jnp.concatenate(out, axis=0)


def permuted(dot, x, one_hot):
    rows = x.shape[0]
    out = dot(halves(x, 3), one_hot, None)
    return out[:rows] + out[rows : 2 * rows] + out[2 * rows :]


def iota(shape, axis):
    return lax.broadcasted_iota(jnp.int32, shape, axis)


def own_span(step, count):
    return (0, count) if step == 0 else ((count - 1, 1) if step > 0 else (0, 1))


def halo_span(step, count):
    return (1, count) if step == 0 else ((0, 1) if step > 0 else (count + 1, 1))


def inverse_list(list_ref, row, first, entries, tables):
    blocks = jnp.zeros((tables, BLOCK), jnp.float32)
    lanes = jnp.zeros((tables, BLOCK), jnp.float32)
    spot = iota((BLOCK, BLOCK), 1).astype(jnp.float32)
    for r in range(entries // BLOCK):
        entry = list_ref[row : row + 1, r * BLOCK : (r + 1) * BLOCK]
        high = jnp.right_shift(entry, 7) - first
        low = jnp.bitwise_and(entry, BLOCK - 1)
        pick = (iota((tables, BLOCK), 0) == high).astype(jnp.float32)
        place = (iota((BLOCK, BLOCK), 0) == low).astype(jnp.float32)
        both = jnp.concatenate([place, place * spot], axis=0).astype(jnp.bfloat16)
        found = dot_lanes(pick.astype(jnp.bfloat16), both, None)
        blocks = blocks + found[:, :BLOCK] * float(r + 1)
        lanes = lanes + found[:, BLOCK:]
    return blocks, lanes


def inverse_blocks(list_ref, row, entries):
    rows = entries // BLOCK
    total = jnp.zeros((rows, BLOCK), jnp.float32)
    for r in range(rows):
        entry = list_ref[row : row + 1, r * BLOCK : (r + 1) * BLOCK]
        high = jnp.right_shift(entry, 7)
        low = jnp.bitwise_and(entry, BLOCK - 1)
        pick = jnp.where(iota((rows, BLOCK), 0) == high, float(r), 0.0)
        place = (iota((BLOCK, BLOCK), 0) == low).astype(jnp.float32)
        total = total + dot_lanes(
            pick.astype(jnp.bfloat16), place.astype(jnp.bfloat16), None
        )
    return total


def look_up(table, index):
    high = jnp.right_shift(index, 7)
    low = jnp.bitwise_and(index, BLOCK - 1)
    out = jnp.zeros(index.shape, jnp.float32)
    for r in range(table.shape[0]):
        row = jnp.broadcast_to(table[r : r + 1, :], index.shape)
        out = jnp.where(high == r, jnp.take_along_axis(row, low, axis=1), out)
    return out


def place_of(sizes):
    return tuple(lax.axis_index(name) for name in ("gx", "gy", "gz"))


def neighbour(me, sizes, step):
    return tuple(lax.rem(m + s + n, n) for m, s, n in zip(me, step, sizes))


def greet(targets):
    barrier = pltpu.get_barrier_semaphore()
    for target in targets:
        pl.semaphore_signal(barrier, inc=1, device_id=target, device_id_type=MESH)
    return barrier


def halo_copies(buffer, send_sem, recv_sem, me, sizes):
    copies = []
    for n, step in enumerate(OFFSETS):
        (xs, xn), (ys, yn) = own_span(step[0], NBX), own_span(step[1], NBY)
        (xd, _), (yd, _) = halo_span(step[0], NBX), halo_span(step[1], NBY)
        copies.append(
            pltpu.make_async_remote_copy(
                src_ref=buffer.at[1, pl.ds(1 + xs, xn), pl.ds(1 + ys, yn)],
                dst_ref=buffer.at[1 - step[2], pl.ds(xd, xn), pl.ds(yd, yn)],
                send_sem=send_sem.at[n],
                recv_sem=recv_sem.at[n],
                device_id=neighbour(me, sizes, step),
                device_id_type=MESH,
            )
        )
    return copies


def partners_of(me, sizes):
    steps = []
    for axis, n in enumerate(sizes):
        for s in range(1, n):
            step = [0, 0, 0]
            step[axis] = s if 2 * s <= n else s - n
            steps.append(tuple(step))
    return steps


def reduce_along(axis, n, total, slot, send, recv, me, sizes):
    slot[me[axis]] = total
    copies = []
    for s in range(1, n):
        step = [0, 0, 0]
        step[axis] = s
        copies.append(
            pltpu.make_async_remote_copy(
                src_ref=slot.at[me[axis]],
                dst_ref=slot.at[me[axis]],
                send_sem=send.at[s - 1],
                recv_sem=recv.at[s - 1],
                device_id=neighbour(me, sizes, step),
                device_id_type=MESH,
            )
        )
    for copy in copies:
        copy.start()
    for copy in copies:
        copy.wait_recv()
    total = slot[0]
    for k in range(1, n):
        total = total + slot[k]
    return total, copies


def gradient_steps(products):
    def inner(left, right):
        value = 0.0
        for a, p in enumerate(left):
            for b, q in enumerate(right):
                if p is not None and q is not None:
                    value = value + p * q * products[a, b]
        return value

    def plus(p, q):
        return q if p is None else (p if q is None else p + q)

    def times(scale, p):
        return None if p is None else scale * p

    def applied(c):
        out = [times(CENTRE, p) for p in c]
        if c[0] is not None:
            out[1] = plus(out[1], HALF * c[0])
        for k in (1, 2):
            if c[k] is not None:
                out[k - 1] = plus(out[k - 1], (0.5 * HALF) * c[k])
                out[k + 1] = plus(out[k + 1], (0.5 * HALF) * c[k])
        return out

    left = [jnp.ones((1, 1), jnp.float32), None, None, None]
    direction = list(left)
    answer = [None] * 4
    norm = products[0, 0]
    for _ in range(3):
        image = applied(direction)
        step = norm / inner(direction, image)
        answer = [plus(p, times(step, q)) for p, q in zip(answer, direction)]
        left = [plus(p, times(-step, q)) for p, q in zip(left, image)]
        after = inner(left, left)
        direction = [plus(p, times(after / norm, q)) for p, q in zip(left, direction)]
        norm = after
    return answer, left


def field_kernel(
    sizes,
    coords_in, polar_in, external_in, live_in, ghost_x_in, ghost_y_in, ghost_z_in,
    pairs_in, alive_in,
    dipoles, residual,
    coords, polar, external, live, ghost_x, ghost_y, ghost_z, pairs, alive, loads,
    halo1, halo2, halo3, tabs_y, tabs_z, own_y, own_z, sends, recvs, tab_sends, tab_recvs,
    order, side, target, window, listed_bits, moved, marks, px, py, pz, inner_s, sums, basis, flat,
    slot_x, slot_y, slot_z, send_x, send_y, send_z, recv_x, recv_y, recv_z,
):
    me = place_of(sizes)
    outside = (
        coords_in, polar_in, external_in, live_in, ghost_x_in, ghost_y_in, ghost_z_in,
        pairs_in, alive_in,
    )
    inside = (coords, polar, external, live, ghost_x, ghost_y, ghost_z, pairs, alive)
    arriving = [
        pltpu.make_async_copy(far, near, loads.at[n])
        for n, (far, near) in enumerate(zip(outside, inside))
    ]
    for copy in arriving:
        copy.start()
    friends = dict.fromkeys(list(OFFSETS) + partners_of(me, sizes))
    barrier = greet([neighbour(me, sizes, step) for step in friends])
    for copy in arriving:
        copy.wait()

    up_blocks, up_lanes = inverse_list(ghost_x, 0, 0, 2 * BLOCK, NBLK)
    down_blocks, down_lanes = inverse_list(ghost_x, 1, 0, 2 * BLOCK, NBLK)
    upper = iota((NBLK, BLOCK), 0) >= NBLK - NBY
    x_spot = jnp.where(
        upper, (up_blocks - 1.0) * BLOCK + up_lanes, (down_blocks - 1.0) * BLOCK + down_lanes
    )
    x_spot = jnp.maximum(x_spot, 0.0)
    lane = iota((1, BLOCK), 1)
    lane_f = lane.astype(jnp.float32)

    for b in range(NBLK):
        cut = slice(b * BLOCK, (b + 1) * BLOCK)
        alpha = polar[0:1, cut]
        living = live[0:1, cut].astype(jnp.float32)
        place = coords[:, cut]
        rhs = external[:, cut] * living
        code = lane_f + x_spot[b : b + 1, :] * BLOCK
        beta = lax.rsqrt(alpha) * math.sqrt(THOLE_FACTOR)
        tile = jnp.concatenate([place, beta, rhs, code], axis=0)
        more = jnp.concatenate(
            [living / alpha, living, jnp.zeros((6, BLOCK), jnp.float32)], axis=0
        )
        column = jnp.transpose(tile)
        z_row = place[2:3, :]
        z_col = column[:, 2:3]
        before = jnp.logical_or(
            z_row < z_col,
            jnp.logical_and(z_row == z_col, iota((BLOCK, BLOCK), 1) < iota((BLOCK, BLOCK), 0)),
        )
        rank = jnp.sum(before.astype(jnp.float32), axis=1, keepdims=True)
        one_hot = (rank == iota((BLOCK, BLOCK), 1).astype(jnp.float32)).astype(jnp.float32)
        one_hot = one_hot.astype(jnp.bfloat16)
        order[b] = one_hot
        ranked = permuted(dot_rows, jnp.concatenate([tile, more], axis=0), one_hot)
        halo1[1, 1 + b // NBY, 1 + b % NBY] = ranked[:8]
        side[b] = ranked[8:]
        basis[0, b] = jnp.concatenate(
            [ranked[4:7], jnp.zeros((5, BLOCK), jnp.float32)], axis=0
        )
        flipped = jnp.transpose(ranked[:8])
        for g in range(NGRP):
            target[b * NGRP + g] = flipped[g * GROUP : (g + 1) * GROUP]

    pl.semaphore_wait(barrier, len(friends))
    first = halo_copies(halo1, sends.at[0], recvs.at[0], me, sizes)
    for copy in first:
        copy.start()

    for row in range(2):
        blocks, lanes = inverse_list(ghost_y, row, 0, 6 * BLOCK, 12)
        own_y[row, 0:12] = (blocks - 1.0) * BLOCK + lanes
        own_z[row] = inverse_blocks(ghost_z, row, 24 * BLOCK)
    tables = []
    for row, step_y in enumerate((1, -1)):
        for step_z in (-1, 0, 1):
            n = len(tables)
            tables.append(
                pltpu.make_async_remote_copy(
                    src_ref=own_y.at[row],
                    dst_ref=tabs_y.at[row, 1 - step_z],
                    send_sem=tab_sends.at[n],
                    recv_sem=tab_recvs.at[n],
                    device_id=neighbour(me, sizes, (0, step_y, step_z)),
                    device_id_type=MESH,
                )
            )
    for row, step_z in enumerate((1, -1)):
        n = len(tables)
        tables.append(
            pltpu.make_async_remote_copy(
                src_ref=own_z.at[row],
                dst_ref=tabs_z.at[row],
                send_sem=tab_sends.at[n],
                recv_sem=tab_recvs.at[n],
                device_id=neighbour(me, sizes, (0, 0, step_z)),
                device_id_type=MESH,
            )
        )
    for copy in tables:
        copy.start()

    count = pairs.shape[1]
    bits = jnp.left_shift(alive[0:1, :], pairs[0:1, :]).astype(jnp.float32)
    bits = jnp.broadcast_to(bits, (8, count)).astype(jnp.bfloat16)
    listed = (iota((BLOCK, count), 0) == pairs[1:2, :]).astype(jnp.float32)
    listed_by = dot_lanes(bits, listed.astype(jnp.bfloat16), None)

    for copy in first:
        copy.wait_recv()
    for copy in tables:
        copy.wait_recv()

    for role in range(3):
        for part in range(NCOL // 8):
            codes = jnp.concatenate(
                [
                    halo1[role, c // CY, c % CY, 7:8, :]
                    for c in range(part * 8, part * 8 + 8)
                ],
                axis=0,
            ).astype(jnp.int32)
            spot = jnp.right_shift(codes, 7)
            own_lane = jnp.bitwise_and(codes, BLOCK - 1)
            col = iota((8, BLOCK), 0) + part * 8
            cx, cy = jnp.right_shift(col, 2), jnp.bitwise_and(col, 3)
            block_y = jnp.bitwise_and(cy + 1, 1)
            entry = ((cx - 1) * NBY + block_y) * BLOCK + own_lane
            entry = jnp.where(cx == 0, NBLK * BLOCK + spot, entry)
            entry = jnp.where(cx == CX - 1, (NBLK + NBY) * BLOCK + spot, entry)
            low = look_up(tabs_y[0, role, 0:12], entry)
            high = look_up(tabs_y[1, role, 0:12], entry)
            found = jnp.where(cy == 0, low, jnp.where(cy == CY - 1, high, 0.0))
            valid = found >= 0.0
            found = jnp.maximum(found, 0.0).astype(jnp.int32)
            entry = jnp.where(cy == 0, 12 * BLOCK + found, entry)
            entry = jnp.where(cy == CY - 1, 18 * BLOCK + found, entry)
            if role == 1:
                block = jnp.right_shift(entry, 7)
            else:
                layer = look_up(tabs_z[role // 2], entry)
                block = layer.astype(jnp.int32) + (24 if role == 0 else 48)
            mark = jnp.take_along_axis(listed_by, block, axis=1)
            marks[role, part * 8 : part * 8 + 8] = jnp.where(valid, mark, 0.0)

    row8 = iota((8, BLOCK), 0)
    lane8 = iota((8, BLOCK), 1)
    edge = [
        (jnp.where(m == 0, -n * size, 0.0), jnp.where(m == n - 1, n * size, 0.0))
        for m, n, size in zip(me, sizes, BRICK)
    ]

    def shifted(role, cx, cy):
        tile = halo1[role, cx, cy]
        col = cx * CY + cy
        if cx in (0, CX - 1):
            tile = tile + jnp.where(row8 == 0, edge[0][0 if cx == 0 else 1], 0.0)
        if cy in (0, CY - 1):
            tile = tile + jnp.where(row8 == 1, edge[1][0 if cy == 0 else 1], 0.0)
        if role != 1:
            tile = tile + jnp.where(row8 == 2, edge[2][role // 2], 0.0)
        return jnp.where(row8 == 7, marks[role, col : col + 1, :], tile)

    def windows(below, middle, above, lanes):
        return (
            jnp.where(lanes >= 80, below, middle),
            jnp.where(lanes >= 112, below, middle),
            jnp.where(lanes < 16, above, middle),
            jnp.where(lanes < 48, above, middle),
        )

    for cx in range(CX):
        for cy in range(CY):
            tiles = windows(*[shifted(role, cx, cy) for role in range(3)], lane8)
            for g in range(NGRP):
                for k in range(7):
                    window[(cx * CY + cy) * NGRP + g, k] = jnp.broadcast_to(
                        tiles[g][k : k + 1], (8, BLOCK)
                    )
                listed_bits[(cx * CY + cy) * NGRP + g] = jnp.broadcast_to(
                    tiles[g][7:8], (8, BLOCK)
                ).astype(jnp.int32)

    tiles_of = (GROUP // 8, 8, BLOCK)

    def keep_sums(block, g, total):
        for k in range(3):
            sums[block, k, pl.ds(pl.multiple_of(g * GROUP, GROUP), GROUP)] = total[k].reshape(
                GROUP, BLOCK
            )

    def build(step, carry):
        block, g = step // NGRP, step % NGRP
        column = (block // NBY) * CY + block % NBY
        mine = target[step]
        tx, ty, tz, tb = [
            jnp.broadcast_to(mine[:, k : k + 1], (GROUP, BLOCK)).reshape(tiles_of)
            for k in range(4)
        ]
        total = [jnp.zeros(tiles_of, jnp.float32) for _ in range(3)]
        bit = jnp.left_shift(1, block)
        for c in range(9):
            at = (column + (c // 3) * CY + c % 3) * NGRP + g
            seen = jnp.bitwise_and(listed_bits[at], bit) != 0
            sx = jnp.where(seen, window[at, 0], FAR)
            dx, dy, dz = tx - sx[None], ty - window[at, 1][None], tz - window[at, 2][None]
            if c == 4:
                mine_at = iota(tiles_of, 0) * 8 + iota(tiles_of, 1) + g * GROUP
                dx = jnp.where(mine_at == iota(tiles_of, 2), FAR, dx)
            q = dx * dx + dy * dy + dz * dz
            inv = lax.rsqrt(q)
            inv2 = inv * inv
            margin = jnp.maximum(CUTOFF_SQUARED - q, 0.0)
            scaled = q * (q * inv) * (tb * window[at, 3][None])
            damp = jnp.exp(-scaled)
            rest = 1.0 - damp
            near = margin * inv2
            inner = (near * margin) * (inv * rest)
            root = (3.0 * inv) * (rest - scaled * damp)
            scale = near * (root * lax.rsqrt(root))
            ax, ay, az = scale * dx, scale * dy, scale * dz
            slot = step * 9 + c
            px[slot], py[slot], pz[slot], inner_s[slot] = ax, ay, az, inner
            vx, vy, vz = window[at, 4][None], window[at, 5][None], window[at, 6][None]
            along = ax * vx + ay * vy + az * vz
            total[0] = total[0] + (along * ax - inner * vx)
            total[1] = total[1] + (along * ay - inner * vy)
            total[2] = total[2] + (along * az - inner * vz)
        keep_sums(block, g, total)
        return carry

    lax.fori_loop(0, NBLK * NGRP, build, 0)

    def apply(step, carry):
        block, g = step // NGRP, step % NGRP
        column = (block // NBY) * CY + block % NBY
        total = [jnp.zeros(tiles_of, jnp.float32) for _ in range(3)]
        for c in range(9):
            at = (column + (c // 3) * CY + c % 3) * NGRP + g
            slot = step * 9 + c
            ax, ay, az, inner = px[slot], py[slot], pz[slot], inner_s[slot]
            vx, vy, vz = moved[at, 0][None], moved[at, 1][None], moved[at, 2][None]
            along = ax * vx + ay * vy + az * vz
            total[0] = total[0] + (along * ax - inner * vx)
            total[1] = total[1] + (along * ay - inner * vy)
            total[2] = total[2] + (along * az - inner * vz)
        keep_sums(block, g, total)
        return carry

    ones = jnp.ones((8, BLOCK), jnp.float32)
    ones_half = ones.astype(jnp.bfloat16)

    def next_basis(level, halo):
        for b in range(NBLK):
            parts = [halves(sums[b, k], 2) for k in range(3)]
            field = dot_lanes(ones_half, jnp.concatenate(parts, axis=0), None)
            field = [
                field[:, 2 * k * BLOCK : (2 * k + 1) * BLOCK]
                + field[:, (2 * k + 1) * BLOCK : (2 * k + 2) * BLOCK]
                for k in range(3)
            ]
            field = jnp.where(row8 == 0, field[0], jnp.where(row8 == 1, field[1], field[2]))
            field = field * (1.0 / CUTOFF_SQUARED**2)
            v = basis[level, b]
            rows = side[b]
            image = rows[0:1] * v - rows[1:2] * field
            image = (image - CENTRE * v) * (1.0 / HALF)
            if level > 0:
                image = 2.0 * image - basis[level - 1, b]
            image = jnp.where(row8 < 3, image, 0.0)
            basis[level + 1, b] = image
            if halo is not None:
                halo[1, 1 + b // NBY, 1 + b % NBY] = image[:4]

    lane4 = iota((4, BLOCK), 1)
    started = first + tables
    for level, halo in ((0, halo2), (1, halo3)):
        next_basis(level, halo)
        copies = halo_copies(halo, sends.at[level + 1], recvs.at[level + 1], me, sizes)
        for copy in copies:
            copy.start()
        for copy in copies:
            copy.wait_recv()
        for cx in range(CX):
            for cy in range(CY):
                tiles = windows(*[halo[role, cx, cy] for role in range(3)], lane4)
                for g in range(NGRP):
                    for k in range(3):
                        moved[(cx * CY + cy) * NGRP + g, k] = jnp.broadcast_to(
                            tiles[g][k : k + 1], (8, BLOCK)
                        )
        lax.fori_loop(0, NBLK * NGRP, apply, 0)
        started = started + copies
    next_basis(2, None)

    rows = []
    for a, b in GRAM:
        part = jnp.sum(basis[a] * basis[b], axis=0)
        rows.append(jnp.sum(part, axis=0, keepdims=True))
    rows.append(jnp.zeros((BLOCK - len(GRAM), BLOCK), jnp.float32))
    total = dot_lanes(ones, jnp.concatenate(rows, axis=0))[0:1]
    slots, sent, got = (slot_x, slot_y, slot_z), (send_x, send_y, send_z), (recv_x, recv_y, recv_z)
    for axis, n in enumerate(sizes):
        total, copies = reduce_along(
            axis, n, total, slots[axis], sent[axis], got[axis], me, sizes
        )
        started = started + copies
        if axis == 0:
            for b in range(NBLK):
                stacked = jnp.concatenate([basis[k, b] for k in range(4)], axis=0)
                flat[:, b * BLOCK : (b + 1) * BLOCK] = permuted(dot_lanes, stacked, order[b])
    products = {}
    for k, (a, b) in enumerate(GRAM):
        products[a, b] = products[b, a] = total[:, k : k + 1]
    answer, left = gradient_steps(products)

    def combined(coefficients):
        value = 0.0
        for k, c in enumerate(coefficients):
            if c is not None:
                value = value + c * flat[8 * k : 8 * k + 3, :]
        return value

    dipoles[...] = combined(answer)
    residual[...] = polar[...] * combined(left)
    for copy in started:
        copy.wait_send()


def per_device(
    sizes, coords, polarizability, external_field, bead_live,
    ghost_x, ghost_y, ghost_z, pair_blocks, pair_live,
):
    nloc = coords.shape[1]
    vmem = pl.BlockSpec(memory_space=pltpu.VMEM)
    f32 = jnp.float32
    operands = (
        coords, polarizability.reshape(1, nloc), external_field, bead_live.reshape(1, nloc),
        ghost_x, ghost_y, ghost_z, pair_blocks, pair_live.reshape(1, pair_live.shape[0]),
    )
    tensors = pltpu.VMEM((NBLK * NGRP * 9, GROUP // 8, 8, BLOCK), f32)
    steps = len(OFFSETS)
    return pl.pallas_call(
        functools.partial(field_kernel, sizes),
        out_shape=(jax.ShapeDtypeStruct((3, nloc), f32),) * 2,
        in_specs=[pl.BlockSpec(memory_space=pltpu.HBM)] * len(operands),
        out_specs=(vmem, vmem),
        scratch_shapes=[pltpu.VMEM(x.shape, x.dtype) for x in operands]
        + [
            pltpu.SemaphoreType.DMA((len(operands),)),
            pltpu.VMEM((3, CX, CY, 8, BLOCK), f32),
            pltpu.VMEM((3, CX, CY, 4, BLOCK), f32),
            pltpu.VMEM((3, CX, CY, 4, BLOCK), f32),
            pltpu.VMEM((2, 3, 16, BLOCK), f32),
            pltpu.VMEM((2, 24, BLOCK), f32),
            pltpu.VMEM((2, 16, BLOCK), f32),
            pltpu.VMEM((2, 24, BLOCK), f32),
            pltpu.SemaphoreType.DMA((3, steps)),
            pltpu.SemaphoreType.DMA((3, steps)),
            pltpu.SemaphoreType.DMA((8,)),
            pltpu.SemaphoreType.DMA((8,)),
            pltpu.VMEM((NBLK, BLOCK, BLOCK), jnp.bfloat16),
            pltpu.VMEM((NBLK, 8, BLOCK), f32),
            pltpu.VMEM((NBLK * NGRP, GROUP, 8), f32),
            pltpu.VMEM((NCOL * NGRP, 7, 8, BLOCK), f32),
            pltpu.VMEM((NCOL * NGRP, 8, BLOCK), jnp.int32),
            pltpu.VMEM((NCOL * NGRP, 3, 8, BLOCK), f32),
            pltpu.VMEM((3, NCOL, BLOCK), f32),
            tensors, tensors, tensors, tensors,
            pltpu.VMEM((NBLK, 3, BLOCK, BLOCK), f32),
            pltpu.VMEM((4, NBLK, 8, BLOCK), f32),
            pltpu.VMEM((32, nloc), f32),
        ]
        + [pltpu.VMEM((n, 1, BLOCK), f32) for n in sizes]
        + [pltpu.SemaphoreType.DMA((n - 1,)) for n in sizes] * 2,
        compiler_params=pltpu.CompilerParams(
            collective_id=0, has_side_effects=True, vmem_limit_bytes=63 * 2**20
        ),
    )(*operands)


def solution(mesh):
    sizes = tuple(mesh.shape[name] for name in ("gx", "gy", "gz"))
    wide = P(None, ("gx", "gy", "gz"))
    flat = P(("gx", "gy", "gz"))
    return jax.shard_map(
        functools.partial(per_device, sizes),
        mesh=mesh,
        in_specs=(wide, flat, wide, flat, wide, wide, wide, wide, flat),
        out_specs=(wide, wide),
        check_vma=False,
    )
```

```python
import functools
import math

import jax
import jax.numpy as jnp
from jax import lax
from jax.experimental import pallas as pl
from jax.experimental.pallas import tpu as pltpu
from jax.sharding import PartitionSpec as P

BLOCK = 128
NBX, NBY = 4, 2
NBLK = NBX * NBY
CX, CY = NBX + 2, NBY + 2
NCOL = CX * CY
GROUP = 32
NGRP = BLOCK // GROUP
BRICK = (16.0, 8.0, 8.0)
CUTOFF_SQUARED = 12.25
THOLE_FACTOR = 0.02
CENTRE, HALF = 12.5, 8.5
FAR = 1.0e6
MESH = pl.DeviceIdType.MESH
HIGHEST = lax.Precision.HIGHEST
OFFSETS = [
    (x, y, z)
    for x in (-1, 0, 1)
    for y in (-1, 0, 1)
    for z in (-1, 0, 1)
    if (x, y, z) != (0, 0, 0)
]
GRAM = [(a, b) for a in range(4) for b in range(a, 4)]


def dot_rows(left, right, precision=HIGHEST):
    return lax.dot_general(
        left, right, (((1,), (0,)), ((), ())), precision=precision,
        preferred_element_type=jnp.float32,
    )


def dot_lanes(left, right, precision=HIGHEST):
    return lax.dot_general(
        left, right, (((1,), (1,)), ((), ())), precision=precision,
        preferred_element_type=jnp.float32,
    )


def halves(x, parts):
    out = []
    for _ in range(parts):
        part = x.astype(jnp.bfloat16)
        out.append(part)
        x = x - part.astype(jnp.float32)
    return jnp.concatenate(out, axis=0)


def permuted(dot, x, one_hot):
    rows = x.shape[0]
    out = dot(halves(x, 3), one_hot, None)
    return out[:rows] + out[rows : 2 * rows] + out[2 * rows :]


def iota(shape, axis):
    return lax.broadcasted_iota(jnp.int32, shape, axis)


def own_span(step, count):
    return (0, count) if step == 0 else ((count - 1, 1) if step > 0 else (0, 1))


def halo_span(step, count):
    return (1, count) if step == 0 else ((0, 1) if step > 0 else (count + 1, 1))


def site_ranks(place):
    tie = iota((BLOCK, BLOCK), 0) < iota((BLOCK, BLOCK), 1)
    base = jnp.zeros((NBLK, BLOCK), jnp.float32)
    for axis, shift in ((2, 4), (0, 2), (1, 0)):
        key = base + place[axis]
        column = jnp.transpose(key)
        ranks = []
        for b in range(NBLK):
            left = jnp.broadcast_to(column[:, b : b + 1], (BLOCK, BLOCK))
            right = jnp.broadcast_to(key[b : b + 1, :], (BLOCK, BLOCK))
            before = jnp.logical_or(left < right, jnp.logical_and(left == right, tie))
            ranks.append(jnp.sum(jnp.where(before, 1.0, 0.0), axis=0, keepdims=True))
        rank = jnp.concatenate(ranks, axis=0).astype(jnp.int32)
        base = jnp.right_shift(rank, shift).astype(jnp.float32) * 512.0
    return rank


def site_lanes(rank):
    z, x, y = jnp.right_shift(rank, 4), jnp.right_shift(rank, 2) & 3, rank & 3
    cube = jnp.right_shift(z, 1) * 4 + jnp.right_shift(x, 1) * 2 + jnp.right_shift(y, 1)
    return cube * 8 + (z & 1) * 4 + (x & 1) * 2 + (y & 1)


def inverse_list(list_ref, row, first, entries, tables):
    blocks = jnp.zeros((tables, BLOCK), jnp.float32)
    lanes = jnp.zeros((tables, BLOCK), jnp.float32)
    spot = iota((BLOCK, BLOCK), 1).astype(jnp.float32)
    for r in range(entries // BLOCK):
        entry = list_ref[row : row + 1, r * BLOCK : (r + 1) * BLOCK]
        high = jnp.right_shift(entry, 7) - first
        low = jnp.bitwise_and(entry, BLOCK - 1)
        pick = (iota((tables, BLOCK), 0) == high).astype(jnp.float32)
        place = (iota((BLOCK, BLOCK), 0) == low).astype(jnp.float32)
        both = jnp.concatenate([place, place * spot], axis=0).astype(jnp.bfloat16)
        found = dot_lanes(pick.astype(jnp.bfloat16), both, None)
        blocks = blocks + found[:, :BLOCK] * float(r + 1)
        lanes = lanes + found[:, BLOCK:]
    return blocks, lanes


def inverse_blocks(list_ref, row, entries):
    rows = entries // BLOCK
    total = jnp.zeros((rows, BLOCK), jnp.float32)
    for r in range(rows):
        entry = list_ref[row : row + 1, r * BLOCK : (r + 1) * BLOCK]
        high = jnp.right_shift(entry, 7)
        low = jnp.bitwise_and(entry, BLOCK - 1)
        pick = jnp.where(iota((rows, BLOCK), 0) == high, float(r), 0.0)
        place = (iota((BLOCK, BLOCK), 0) == low).astype(jnp.float32)
        total = total + dot_lanes(
            pick.astype(jnp.bfloat16), place.astype(jnp.bfloat16), None
        )
    return total


def look_up(table, index):
    high = jnp.right_shift(index, 7)
    low = jnp.bitwise_and(index, BLOCK - 1)
    out = jnp.zeros(index.shape, jnp.float32)
    for r in range(table.shape[0]):
        row = jnp.broadcast_to(table[r : r + 1, :], index.shape)
        out = jnp.where(high == r, jnp.take_along_axis(row, low, axis=1), out)
    return out


def place_of(sizes):
    return tuple(lax.axis_index(name) for name in ("gx", "gy", "gz"))


def neighbour(me, sizes, step):
    return tuple(lax.rem(m + s + n, n) for m, s, n in zip(me, step, sizes))


def greet(targets):
    barrier = pltpu.get_barrier_semaphore()
    for target in targets:
        pl.semaphore_signal(barrier, inc=1, device_id=target, device_id_type=MESH)
    return barrier


def bytes_of(view, sem):
    return pltpu.make_async_copy(view, view, sem)


def halo_copies(buffer, send_sem, recv_sem, me, sizes):
    copies = []
    for step in OFFSETS:
        (xs, xn), (ys, yn) = own_span(step[0], NBX), own_span(step[1], NBY)
        (xd, _), (yd, _) = halo_span(step[0], NBX), halo_span(step[1], NBY)
        copies.append(
            pltpu.make_async_remote_copy(
                src_ref=buffer.at[1, pl.ds(1 + xs, xn), pl.ds(1 + ys, yn)],
                dst_ref=buffer.at[1 - step[2], pl.ds(xd, xn), pl.ds(yd, yn)],
                send_sem=send_sem,
                recv_sem=recv_sem,
                device_id=neighbour(me, sizes, step),
                device_id_type=MESH,
            )
        )
    return copies


def sum_stages(sizes):
    def near(step):
        return tuple(s if 2 * s <= n else s - n for s, n in zip(step, sizes))

    along = [near((s, 0, 0)) for s in range(1, sizes[0])]
    across = [near((0, y, z)) for y in range(sizes[1]) for z in range(sizes[2]) if y + z > 0]
    far_first = lambda step: -sum(abs(s) for s in step)
    return sorted(along, key=far_first), sorted(across, key=far_first)


def reduce_over(steps, total, slot, place, send, recv, me, sizes):
    slot[place] = total
    copies = []
    for step in steps:
        copies.append(
            pltpu.make_async_remote_copy(
                src_ref=slot.at[place],
                dst_ref=slot.at[place],
                send_sem=send,
                recv_sem=recv,
                device_id=neighbour(me, sizes, step),
                device_id_type=MESH,
            )
        )
    for copy in copies:
        copy.start()
    everyone = slot.at[pl.ds(0, len(steps))]
    bytes_of(everyone, recv).wait()
    total = slot[0]
    for k in range(1, len(steps) + 1):
        total = total + slot[k]
    return total, (everyone, send)


def gradient_steps(products):
    def inner(left, right):
        value = 0.0
        for a, p in enumerate(left):
            for b, q in enumerate(right):
                if p is not None and q is not None:
                    value = value + p * q * products[a, b]
        return value

    def plus(p, q):
        return q if p is None else (p if q is None else p + q)

    def times(scale, p):
        return None if p is None else scale * p

    def applied(c):
        out = [times(CENTRE, p) for p in c]
        if c[0] is not None:
            out[1] = plus(out[1], HALF * c[0])
        for k in (1, 2):
            if c[k] is not None:
                out[k - 1] = plus(out[k - 1], (0.5 * HALF) * c[k])
                out[k + 1] = plus(out[k + 1], (0.5 * HALF) * c[k])
        return out

    left = [jnp.ones((1, 1), jnp.float32), None, None, None]
    direction = list(left)
    answer = [None] * 4
    norm = products[0, 0]
    for _ in range(3):
        image = applied(direction)
        step = norm / inner(direction, image)
        answer = [plus(p, times(step, q)) for p, q in zip(answer, direction)]
        left = [plus(p, times(-step, q)) for p, q in zip(left, image)]
        after = inner(left, left)
        direction = [plus(p, times(after / norm, q)) for p, q in zip(left, direction)]
        norm = after
    return answer, left


def field_kernel(
    sizes,
    coords_in, polar_in, external_in, live_in, ghost_x_in, ghost_y_in, ghost_z_in,
    pairs_in, alive_in,
    answers,
    coords, polar, external, live, ghost_x, ghost_y, ghost_z, pairs, alive, loads,
    halo1, halo2, halo3, tabs_y, tabs_z, own_y, own_z, sends, recvs,
    order, side, target, window, moved, marks, px, py, pz, inner_s, sums, basis, flat,
    slot_x, slot_y,
):
    me = place_of(sizes)
    outside = (
        coords_in, polar_in, external_in, live_in, ghost_x_in, ghost_y_in, ghost_z_in,
        pairs_in, alive_in,
    )
    inside = (coords, polar, external, live, ghost_x, ghost_y, ghost_z, pairs, alive)
    arriving = [
        pltpu.make_async_copy(far, near, loads.at[n])
        for n, (far, near) in enumerate(zip(outside, inside))
    ]
    for copy in arriving:
        copy.start()
    friends = dict.fromkeys(list(OFFSETS) + sum(sum_stages(sizes), []))
    barrier = greet([neighbour(me, sizes, step) for step in friends])
    for copy in arriving:
        copy.wait()

    up_blocks, up_lanes = inverse_list(ghost_x, 0, 0, 2 * BLOCK, NBLK)
    down_blocks, down_lanes = inverse_list(ghost_x, 1, 0, 2 * BLOCK, NBLK)
    upper = iota((NBLK, BLOCK), 0) >= NBLK - NBY
    x_spot = jnp.where(
        upper, (up_blocks - 1.0) * BLOCK + up_lanes, (down_blocks - 1.0) * BLOCK + down_lanes
    )
    x_spot = jnp.maximum(x_spot, 0.0)
    lane = iota((1, BLOCK), 1)
    lane_f = lane.astype(jnp.float32)

    lanes_of = site_lanes(
        site_ranks(
            [
                jnp.concatenate(
                    [coords[k : k + 1, b * BLOCK : (b + 1) * BLOCK] for b in range(NBLK)], axis=0
                )
                for k in range(3)
            ]
        )
    )
    for b in range(NBLK):
        cut = slice(b * BLOCK, (b + 1) * BLOCK)
        alpha = polar[0:1, cut]
        living = live[0:1, cut].astype(jnp.float32)
        place = coords[:, cut]
        rhs = external[:, cut] * living
        code = lane_f + x_spot[b : b + 1, :] * BLOCK
        beta = lax.rsqrt(alpha) * math.sqrt(THOLE_FACTOR)
        tile = jnp.concatenate([place, beta, rhs, code], axis=0)
        more = jnp.concatenate(
            [living / alpha, living, jnp.zeros((6, BLOCK), jnp.float32)], axis=0
        )
        one_hot = jnp.where(iota((BLOCK, BLOCK), 0) == lanes_of[b : b + 1, :], 1.0, 0.0)
        one_hot = one_hot.astype(jnp.bfloat16)
        order[b] = one_hot
        ranked = permuted(dot_lanes, jnp.concatenate([tile, more], axis=0), one_hot)
        halo1[1, 1 + b // NBY, 1 + b % NBY] = ranked[:8]
        side[b] = ranked[8:]
        basis[0, b] = jnp.concatenate(
            [ranked[4:7], jnp.zeros((5, BLOCK), jnp.float32)], axis=0
        )
        flipped = jnp.transpose(ranked[:8])
        for g in range(NGRP):
            target[b * NGRP + g] = flipped[g * GROUP : (g + 1) * GROUP]

    pl.semaphore_wait(barrier, len(friends))
    for copy in halo_copies(halo1, sends.at[0], recvs.at[0], me, sizes):
        copy.start()

    for row in range(2):
        blocks, lanes = inverse_list(ghost_y, row, 0, 6 * BLOCK, 12)
        own_y[row, 0:12] = (blocks - 1.0) * BLOCK + lanes
        own_z[row] = inverse_blocks(ghost_z, row, 24 * BLOCK)
    tables = []
    for row, step_y in enumerate((1, -1)):
        for step_z in (-1, 0, 1):
            tables.append(
                pltpu.make_async_remote_copy(
                    src_ref=own_y.at[row],
                    dst_ref=tabs_y.at[row, 1 - step_z],
                    send_sem=sends.at[3],
                    recv_sem=recvs.at[3],
                    device_id=neighbour(me, sizes, (0, step_y, step_z)),
                    device_id_type=MESH,
                )
            )
    for row, step_z in enumerate((1, -1)):
        tables.append(
            pltpu.make_async_remote_copy(
                src_ref=own_z.at[row],
                dst_ref=tabs_z.at[row],
                send_sem=sends.at[3],
                recv_sem=recvs.at[3],
                device_id=neighbour(me, sizes, (0, 0, step_z)),
                device_id_type=MESH,
            )
        )
    for copy in tables:
        copy.start()

    count = pairs.shape[1]
    bits = jnp.left_shift(alive[0:1, :], pairs[0:1, :]).astype(jnp.float32)
    bits = jnp.broadcast_to(bits, (8, count)).astype(jnp.bfloat16)
    listed = (iota((BLOCK, count), 0) == pairs[1:2, :]).astype(jnp.float32)
    listed_by = dot_lanes(bits, listed.astype(jnp.bfloat16), None)

    halo_bytes = window.at[pl.ds(0, 3 * NCOL - NBLK)]
    table_bytes = window.at[pl.ds(0, (6 * 16 + 2 * 24) // 8)]
    bytes_of(halo_bytes, recvs.at[0]).wait()
    bytes_of(table_bytes, recvs.at[3]).wait()

    for role in range(3):
        for part in range(NCOL // 8):
            codes = jnp.concatenate(
                [
                    halo1[role, c // CY, c % CY, 7:8, :]
                    for c in range(part * 8, part * 8 + 8)
                ],
                axis=0,
            ).astype(jnp.int32)
            spot = jnp.right_shift(codes, 7)
            own_lane = jnp.bitwise_and(codes, BLOCK - 1)
            col = iota((8, BLOCK), 0) + part * 8
            cx, cy = jnp.right_shift(col, 2), jnp.bitwise_and(col, 3)
            block_y = jnp.bitwise_and(cy + 1, 1)
            entry = ((cx - 1) * NBY + block_y) * BLOCK + own_lane
            entry = jnp.where(cx == 0, NBLK * BLOCK + spot, entry)
            entry = jnp.where(cx == CX - 1, (NBLK + NBY) * BLOCK + spot, entry)
            low = look_up(tabs_y[0, role, 0:12], entry)
            high = look_up(tabs_y[1, role, 0:12], entry)
            found = jnp.where(cy == 0, low, jnp.where(cy == CY - 1, high, 0.0))
            valid = found >= 0.0
            found = jnp.maximum(found, 0.0).astype(jnp.int32)
            entry = jnp.where(cy == 0, 12 * BLOCK + found, entry)
            entry = jnp.where(cy == CY - 1, 18 * BLOCK + found, entry)
            if role == 1:
                block = jnp.right_shift(entry, 7)
            else:
                layer = look_up(tabs_z[role // 2], entry)
                block = layer.astype(jnp.int32) + (24 if role == 0 else 48)
            mark = jnp.take_along_axis(listed_by, block, axis=1)
            marks[role, part * 8 : part * 8 + 8] = jnp.where(valid, mark, 0.0)

    row8 = iota((8, BLOCK), 0)
    lane8 = iota((8, BLOCK), 1)
    edge = [
        (jnp.where(m == 0, -n * size, 0.0), jnp.where(m == n - 1, n * size, 0.0))
        for m, n, size in zip(me, sizes, BRICK)
    ]

    def shifted(role, cx, cy):
        tile = halo1[role, cx, cy]
        col = cx * CY + cy
        if cx in (0, CX - 1):
            tile = tile + jnp.where(row8 == 0, edge[0][0 if cx == 0 else 1], 0.0)
        if cy in (0, CY - 1):
            tile = tile + jnp.where(row8 == 1, edge[1][0 if cy == 0 else 1], 0.0)
        if role != 1:
            tile = tile + jnp.where(row8 == 2, edge[2][role // 2], 0.0)
        return jnp.where(row8 == 7, marks[role, col : col + 1, :], tile)

    def windows(tile_at, rows, put):
        lanes = iota((rows, BLOCK), 1)
        z_site = jnp.right_shift(lanes, 5) * 2 + (jnp.right_shift(lanes, 2) & 1)
        x_site = (jnp.right_shift(lanes, 4) & 1) * 2 + (jnp.right_shift(lanes, 1) & 1)
        y_site = (jnp.right_shift(lanes, 3) & 1) * 2 + (lanes & 1)
        from_low_x = (x_site >= 1, x_site >= 3)
        from_low_y = (y_site >= 1, y_site >= 3)
        layered = {}
        for cx in range(CX):
            for cy in range(CY):
                below, middle, above = [tile_at(role, cx, cy) for role in range(3)]
                layered[cx, cy] = (
                    jnp.where(z_site >= 5, below, middle),
                    jnp.where(z_site >= 7, below, middle),
                    jnp.where(z_site < 1, above, middle),
                    jnp.where(z_site < 3, above, middle),
                )
        for g in range(NGRP):
            for bx in range(NBX):
                mixed_x = [
                    [
                        jnp.where(low, layered[bx, cy][g], layered[bx + 2, cy][g])
                        for cy in range(CY)
                    ]
                    for low in from_low_x
                ]
                for by in range(NBY):
                    own = [layered[bx + 1, cy][g] for cy in range(CY)]
                    tiles = [own[by + 1], mixed_x[0][by + 1], mixed_x[1][by + 1]]
                    for source in (own, mixed_x[0], mixed_x[1]):
                        tiles += [jnp.where(low, source[by], source[by + 2]) for low in from_low_y]
                    for k, tile in enumerate(tiles):
                        put(((bx * NBY + by) * NGRP + g) * 9 + k, tile)

    def put_window(at, tile):
        window[at] = tile

    windows(shifted, 8, put_window)

    cubes = [(hx, hy) for hx in range(2) for hy in range(2)]

    def windows_of(hx, hy):
        return (0, 1 + hx, 3 + hy, 5 + 2 * hx + hy)

    def spread_row(tile, k):
        return jnp.broadcast_to(tile[k : k + 1], (8, BLOCK))

    def add_field(total, tensor, moment):
        ax, ay, az, inner = tensor
        vx, vy, vz = moment
        along = ax * vx + ay * vy + az * vz
        parts = [along * a - inner * v for a, v in ((ax, vx), (ay, vy), (az, vz))]
        return parts if total is None else [t + p for t, p in zip(total, parts)]

    def keep_sums(block, g, u, total):
        for k in range(3):
            sums[block, k, pl.ds(pl.multiple_of(g * GROUP + u * 8, 8), 8)] = total[k]

    def build(step, carry):
        block, g = step // NGRP, step % NGRP
        mine = target[step]
        sources = []
        for w in range(9):
            tile = window[step * 9 + w]
            seen = jnp.bitwise_and(jnp.right_shift(tile[7:8].astype(jnp.int32), block), 1) == 1
            sx = jnp.where(seen, tile[0:1], FAR)
            sources.append(
                [jnp.broadcast_to(sx, (8, BLOCK))] + [spread_row(tile, k) for k in range(1, 7)]
            )
        for u, (hx, hy) in enumerate(cubes):
            tx, ty, tz, tb = [
                jnp.broadcast_to(mine[u * 8 : u * 8 + 8, k : k + 1], (8, BLOCK)) for k in range(4)
            ]
            total = None
            for n, w in enumerate(windows_of(hx, hy)):
                sx, sy, sz, sb, vx, vy, vz = sources[w]
                dx, dy, dz = tx - sx, ty - sy, tz - sz
                if n == 0:
                    itself = row8 + (g * GROUP + u * 8) == lane8
                    dx = jnp.where(itself, FAR, dx)
                q = dx * dx + dy * dy + dz * dz
                inv = lax.rsqrt(q)
                inv2 = inv * inv
                margin = jnp.maximum(CUTOFF_SQUARED - q, 0.0)
                scaled = q * (q * inv) * (tb * sb)
                damp = jnp.exp(-scaled)
                rest = 1.0 - damp
                near = margin * inv2
                inner = (near * margin) * (inv * rest)
                root = (3.0 * inv) * (rest - scaled * damp)
                scale = near * (root * lax.rsqrt(root))
                tensor = (scale * dx, scale * dy, scale * dz, inner)
                slot = step * 16 + u * 4 + n
                px[slot], py[slot], pz[slot], inner_s[slot] = tensor
                total = add_field(total, tensor, (vx, vy, vz))
            keep_sums(block, g, u, total)
        return carry

    lax.fori_loop(0, NBLK * NGRP, build, 0)

    def apply(step, carry):
        block, g = step // NGRP, step % NGRP
        sources = []
        for w in range(9):
            tile = moved[step * 9 + w]
            sources.append([spread_row(tile, k) for k in range(3)])
        for u, (hx, hy) in enumerate(cubes):
            total = None
            for n, w in enumerate(windows_of(hx, hy)):
                slot = step * 16 + u * 4 + n
                tensor = (px[slot], py[slot], pz[slot], inner_s[slot])
                total = add_field(total, tensor, sources[w])
            keep_sums(block, g, u, total)
        return carry

    ones = jnp.ones((8, BLOCK), jnp.float32)
    ones_half = ones.astype(jnp.bfloat16)

    def next_basis(level, halo):
        for b in range(NBLK):
            parts = [halves(sums[b, k], 2) for k in range(3)]
            field = dot_lanes(ones_half, jnp.concatenate(parts, axis=0), None)
            field = [
                field[:, 2 * k * BLOCK : (2 * k + 1) * BLOCK]
                + field[:, (2 * k + 1) * BLOCK : (2 * k + 2) * BLOCK]
                for k in range(3)
            ]
            field = jnp.where(row8 == 0, field[0], jnp.where(row8 == 1, field[1], field[2]))
            field = field * (1.0 / CUTOFF_SQUARED**2)
            v = basis[level, b]
            rows = side[b]
            image = rows[0:1] * v - rows[1:2] * field
            image = (image - CENTRE * v) * (1.0 / HALF)
            if level > 0:
                image = 2.0 * image - basis[level - 1, b]
            image = jnp.where(row8 < 3, image, 0.0)
            basis[level + 1, b] = image
            if halo is not None:
                halo[1, 1 + b // NBY, 1 + b % NBY] = image[:4]

    def put_moved(at, tile):
        moved[at] = tile

    started = [(halo_bytes, sends.at[0]), (table_bytes, sends.at[3])]
    moved_bytes = moved.at[pl.ds(0, 3 * NCOL - NBLK)]
    for level, halo in ((0, halo2), (1, halo3)):
        next_basis(level, halo)
        for copy in halo_copies(halo, sends.at[level + 1], recvs.at[level + 1], me, sizes):
            copy.start()
        bytes_of(moved_bytes, recvs.at[level + 1]).wait()
        windows(lambda role, cx, cy, halo=halo: halo[role, cx, cy], 4, put_moved)
        lax.fori_loop(0, NBLK * NGRP, apply, 0)
        started.append((moved_bytes, sends.at[level + 1]))
    next_basis(2, None)

    rows = []
    for a, b in GRAM:
        part = jnp.sum(basis[a] * basis[b], axis=0)
        rows.append(jnp.sum(part, axis=0, keepdims=True))
    rows.append(jnp.zeros((BLOCK - len(GRAM), BLOCK), jnp.float32))
    total = dot_lanes(ones, jnp.concatenate(rows, axis=0))[0:1]
    along, across = sum_stages(sizes)
    total, sent = reduce_over(along, total, slot_x, me[0], sends.at[4], recvs.at[4], me, sizes)
    started.append(sent)
    for b in range(NBLK):
        stacked = jnp.concatenate([basis[k, b] for k in range(4)], axis=0)
        flat[:, b * BLOCK : (b + 1) * BLOCK] = permuted(dot_rows, stacked, order[b])
    total, sent = reduce_over(
        across, total, slot_y, me[1] * sizes[2] + me[2], sends.at[5], recvs.at[5], me, sizes
    )
    started.append(sent)
    products = {}
    for k, (a, b) in enumerate(GRAM):
        products[a, b] = products[b, a] = total[:, k : k + 1]
    answer, left = gradient_steps(products)

    def combined(coefficients):
        value = 0.0
        for k, c in enumerate(coefficients):
            if c is not None:
                value = value + c * flat[8 * k : 8 * k + 3, :]
        return value

    answers[...] = jnp.concatenate(
        [combined(answer), combined(left), jnp.zeros((2, answers.shape[1]), jnp.float32)], axis=0
    )
    for view, sem in started:
        bytes_of(view, sem).wait()


def per_device(
    sizes, coords, polarizability, external_field, bead_live,
    ghost_x, ghost_y, ghost_z, pair_blocks, pair_live,
):
    nloc = coords.shape[1]
    vmem = pl.BlockSpec(memory_space=pltpu.VMEM)
    f32 = jnp.float32
    operands = (
        coords, polarizability.reshape(1, nloc), external_field, bead_live.reshape(1, nloc),
        ghost_x, ghost_y, ghost_z, pair_blocks, pair_live.reshape(1, pair_live.shape[0]),
    )
    tensors = pltpu.VMEM((NBLK * NGRP * 16, 8, BLOCK), f32)
    stages = (sizes[0], sizes[1] * sizes[2])
    answers = pl.pallas_call(
        functools.partial(field_kernel, sizes),
        out_shape=jax.ShapeDtypeStruct((8, nloc), f32),
        in_specs=[pl.BlockSpec(memory_space=pltpu.HBM)] * len(operands),
        out_specs=vmem,
        scratch_shapes=[pltpu.VMEM(x.shape, x.dtype) for x in operands]
        + [
            pltpu.SemaphoreType.DMA((len(operands),)),
            pltpu.VMEM((3, CX, CY, 8, BLOCK), f32),
            pltpu.VMEM((3, CX, CY, 4, BLOCK), f32),
            pltpu.VMEM((3, CX, CY, 4, BLOCK), f32),
            pltpu.VMEM((2, 3, 16, BLOCK), f32),
            pltpu.VMEM((2, 24, BLOCK), f32),
            pltpu.VMEM((2, 16, BLOCK), f32),
            pltpu.VMEM((2, 24, BLOCK), f32),
            pltpu.SemaphoreType.DMA((6,)),
            pltpu.SemaphoreType.DMA((6,)),
            pltpu.VMEM((NBLK, BLOCK, BLOCK), jnp.bfloat16),
            pltpu.VMEM((NBLK, 8, BLOCK), f32),
            pltpu.VMEM((NBLK * NGRP, GROUP, 8), f32),
            pltpu.VMEM((NBLK * NGRP * 9, 8, BLOCK), f32),
            pltpu.VMEM((NBLK * NGRP * 9, 4, BLOCK), f32),
            pltpu.VMEM((3, NCOL, BLOCK), f32),
            tensors, tensors, tensors, tensors,
            pltpu.VMEM((NBLK, 3, BLOCK, BLOCK), f32),
            pltpu.VMEM((4, NBLK, 8, BLOCK), f32),
            pltpu.VMEM((32, nloc), f32),
        ]
        + [pltpu.VMEM((n, 1, BLOCK), f32) for n in stages],
        compiler_params=pltpu.CompilerParams(
            collective_id=0, has_side_effects=True, vmem_limit_bytes=63 * 2**20
        ),
    )(*operands)
    return answers[0:3], polarizability[None] * answers[3:6]


def solution(mesh):
    sizes = tuple(mesh.shape[name] for name in ("gx", "gy", "gz"))
    wide = P(None, ("gx", "gy", "gz"))
    flat = P(("gx", "gy", "gz"))
    return jax.shard_map(
        functools.partial(per_device, sizes),
        mesh=mesh,
        in_specs=(wide, flat, wide, flat, wide, wide, wide, wide, flat),
        out_specs=(wide, wide),
        check_vma=False,
    )
```

```python
import functools
import math

import jax
import jax.numpy as jnp
from jax import lax
from jax.experimental import pallas as pl
from jax.experimental.pallas import tpu as pltpu
from jax.sharding import PartitionSpec as P

BLOCK = 128
NBX, NBY = 4, 2
NBLK = NBX * NBY
CX, CY = NBX + 2, NBY + 2
NCOL = CX * CY
GROUP = 32
NGRP = BLOCK // GROUP
BRICK = (16.0, 8.0, 8.0)
CUTOFF_SQUARED = 12.25
THOLE_FACTOR = 0.02
CENTRE, HALF = 12.5, 8.5
FAR = 1.0e6
MESH = pl.DeviceIdType.MESH
HIGHEST = lax.Precision.HIGHEST
OFFSETS = [
    (x, y, z)
    for x in (-1, 0, 1)
    for y in (-1, 0, 1)
    for z in (-1, 0, 1)
    if (x, y, z) != (0, 0, 0)
]
GRAM = [(a, b) for a in range(4) for b in range(a, 4)]


def dot_rows(left, right, precision=HIGHEST):
    return lax.dot_general(
        left, right, (((1,), (0,)), ((), ())), precision=precision,
        preferred_element_type=jnp.float32,
    )


def dot_lanes(left, right, precision=HIGHEST):
    return lax.dot_general(
        left, right, (((1,), (1,)), ((), ())), precision=precision,
        preferred_element_type=jnp.float32,
    )


def halves(x, parts):
    out = []
    for _ in range(parts):
        part = x.astype(jnp.bfloat16)
        out.append(part)
        x = x - part.astype(jnp.float32)
    return jnp.concatenate(out, axis=0)


def permuted(dot, x, one_hot):
    rows = x.shape[0]
    out = dot(halves(x, 3), one_hot, None)
    return out[:rows] + out[rows : 2 * rows] + out[2 * rows :]


def iota(shape, axis):
    return lax.broadcasted_iota(jnp.int32, shape, axis)


def own_span(step, count):
    return (0, count) if step == 0 else ((count - 1, 1) if step > 0 else (0, 1))


def halo_span(step, count):
    return (1, count) if step == 0 else ((0, 1) if step > 0 else (count + 1, 1))


def site_ranks(place):
    tie = iota((BLOCK, BLOCK), 0) < iota((BLOCK, BLOCK), 1)
    base = jnp.zeros((NBLK, BLOCK), jnp.float32)
    for axis, shift in ((2, 4), (0, 2), (1, 0)):
        key = base + place[axis]
        column = jnp.transpose(key)
        ranks = []
        for b in range(NBLK):
            left = jnp.broadcast_to(column[:, b : b + 1], (BLOCK, BLOCK))
            right = jnp.broadcast_to(key[b : b + 1, :], (BLOCK, BLOCK))
            before = jnp.logical_or(left < right, jnp.logical_and(left == right, tie))
            ranks.append(jnp.sum(jnp.where(before, 1.0, 0.0), axis=0, keepdims=True))
        rank = jnp.concatenate(ranks, axis=0).astype(jnp.int32)
        base = jnp.right_shift(rank, shift).astype(jnp.float32) * 512.0
    return rank


def site_lanes(rank):
    z, x, y = jnp.right_shift(rank, 4), jnp.right_shift(rank, 2) & 3, rank & 3
    cube = jnp.right_shift(z, 1) * 4 + jnp.right_shift(x, 1) * 2 + jnp.right_shift(y, 1)
    return cube * 8 + (z & 1) * 4 + (x & 1) * 2 + (y & 1)


def inverse_list(list_ref, row, first, entries, tables):
    blocks = jnp.zeros((tables, BLOCK), jnp.float32)
    lanes = jnp.zeros((tables, BLOCK), jnp.float32)
    spot = iota((BLOCK, BLOCK), 1).astype(jnp.float32)
    for r in range(entries // BLOCK):
        entry = list_ref[row : row + 1, r * BLOCK : (r + 1) * BLOCK]
        high = jnp.right_shift(entry, 7) - first
        low = jnp.bitwise_and(entry, BLOCK - 1)
        pick = (iota((tables, BLOCK), 0) == high).astype(jnp.float32)
        place = (iota((BLOCK, BLOCK), 0) == low).astype(jnp.float32)
        both = jnp.concatenate([place, place * spot], axis=0).astype(jnp.bfloat16)
        found = dot_lanes(pick.astype(jnp.bfloat16), both, None)
        blocks = blocks + found[:, :BLOCK] * float(r + 1)
        lanes = lanes + found[:, BLOCK:]
    return blocks, lanes


def inverse_blocks(list_ref, row, entries):
    rows = entries // BLOCK
    total = jnp.zeros((rows, BLOCK), jnp.float32)
    for r in range(rows):
        entry = list_ref[row : row + 1, r * BLOCK : (r + 1) * BLOCK]
        high = jnp.right_shift(entry, 7)
        low = jnp.bitwise_and(entry, BLOCK - 1)
        pick = jnp.where(iota((rows, BLOCK), 0) == high, float(r), 0.0)
        place = (iota((BLOCK, BLOCK), 0) == low).astype(jnp.float32)
        total = total + dot_lanes(
            pick.astype(jnp.bfloat16), place.astype(jnp.bfloat16), None
        )
    return total


def look_up(table, index):
    high = jnp.right_shift(index, 7)
    low = jnp.bitwise_and(index, BLOCK - 1)
    out = jnp.zeros(index.shape, jnp.float32)
    for r in range(table.shape[0]):
        row = jnp.broadcast_to(table[r : r + 1, :], index.shape)
        out = jnp.where(high == r, jnp.take_along_axis(row, low, axis=1), out)
    return out


def place_of(sizes):
    return tuple(lax.axis_index(name) for name in ("gx", "gy", "gz"))


def neighbour(me, sizes, step):
    return tuple(lax.rem(m + s + n, n) for m, s, n in zip(me, step, sizes))


def greet(targets):
    barrier = pltpu.get_barrier_semaphore()
    for target in targets:
        pl.semaphore_signal(barrier, inc=1, device_id=target, device_id_type=MESH)
    return barrier


def bytes_of(view, sem):
    return pltpu.make_async_copy(view, view, sem)


def hops(step):
    return sum(abs(s) for s in step)


def halo_copies(buffer, send_sem, recv_sem, me, sizes, distance=None):
    copies = []
    for step in sorted(OFFSETS, key=hops, reverse=True):
        if distance is not None and hops(step) != distance:
            continue
        (xs, xn), (ys, yn) = own_span(step[0], NBX), own_span(step[1], NBY)
        (xd, _), (yd, _) = halo_span(step[0], NBX), halo_span(step[1], NBY)
        copies.append(
            pltpu.make_async_remote_copy(
                src_ref=buffer.at[1, pl.ds(1 + xs, xn), pl.ds(1 + ys, yn)],
                dst_ref=buffer.at[1 - step[2], pl.ds(xd, xn), pl.ds(yd, yn)],
                send_sem=send_sem,
                recv_sem=recv_sem,
                device_id=neighbour(me, sizes, step),
                device_id_type=MESH,
            )
        )
    return copies


def sum_stages(sizes):
    def near(step):
        return tuple(s if 2 * s <= n else s - n for s, n in zip(step, sizes))

    along = [near((s, 0, 0)) for s in range(1, sizes[0])]
    across = [near((0, y, z)) for y in range(sizes[1]) for z in range(sizes[2]) if y + z > 0]
    return sorted(along, key=hops, reverse=True), sorted(across, key=hops, reverse=True)


def reduce_over(steps, total, slot, place, send, recv, me, sizes):
    slot[place] = total
    copies = []
    for step in steps:
        copies.append(
            pltpu.make_async_remote_copy(
                src_ref=slot.at[place],
                dst_ref=slot.at[place],
                send_sem=send,
                recv_sem=recv,
                device_id=neighbour(me, sizes, step),
                device_id_type=MESH,
            )
        )
    for copy in copies:
        copy.start()


def reduced(steps, slot, recv):
    bytes_of(slot.at[pl.ds(0, len(steps))], recv).wait()
    total = slot[0]
    for k in range(1, len(steps) + 1):
        total = total + slot[k]
    return total


def gradient_steps(products):
    def inner(left, right):
        value = 0.0
        for a, p in enumerate(left):
            for b, q in enumerate(right):
                if p is not None and q is not None:
                    value = value + p * q * products[a, b]
        return value

    def plus(p, q):
        return q if p is None else (p if q is None else p + q)

    def times(scale, p):
        return None if p is None else scale * p

    def applied(c):
        out = [times(CENTRE, p) for p in c]
        if c[0] is not None:
            out[1] = plus(out[1], HALF * c[0])
        for k in (1, 2):
            if c[k] is not None:
                out[k - 1] = plus(out[k - 1], (0.5 * HALF) * c[k])
                out[k + 1] = plus(out[k + 1], (0.5 * HALF) * c[k])
        return out

    left = [jnp.ones((1, 1), jnp.float32), None, None, None]
    direction = list(left)
    answer = [None] * 4
    norm = products[0, 0]
    for _ in range(3):
        image = applied(direction)
        step = norm / inner(direction, image)
        answer = [plus(p, times(step, q)) for p, q in zip(answer, direction)]
        left = [plus(p, times(-step, q)) for p, q in zip(left, image)]
        after = inner(left, left)
        direction = [plus(p, times(after / norm, q)) for p, q in zip(left, direction)]
        norm = after
    return answer, left


def field_kernel(
    sizes,
    coords_in, polar_in, external_in, live_in, ghost_x_in, ghost_y_in, ghost_z_in,
    pairs_in, alive_in,
    answers,
    coords, polar, external, live, ghost_x, ghost_y, ghost_z, pairs, alive, loads,
    halo1, halo2, halo3, tabs_y, tabs_z, own_y, own_z, sends, recvs,
    order, side, target, window, moved, marks, px, py, pz, inner_s, sums, basis, flat,
    slot_x, slot_y,
):
    me = place_of(sizes)
    outside = (
        coords_in, polar_in, external_in, live_in, ghost_x_in, ghost_y_in, ghost_z_in,
        pairs_in, alive_in,
    )
    inside = (coords, polar, external, live, ghost_x, ghost_y, ghost_z, pairs, alive)
    arriving = [
        pltpu.make_async_copy(far, near, loads.at[n])
        for n, (far, near) in enumerate(zip(outside, inside))
    ]
    for copy in arriving:
        copy.start()
    friends = dict.fromkeys(list(OFFSETS) + sum(sum_stages(sizes), []))
    barrier = greet([neighbour(me, sizes, step) for step in friends])
    arriving[0].wait()

    lanes_of = site_lanes(
        site_ranks(
            [
                jnp.concatenate(
                    [coords[k : k + 1, b * BLOCK : (b + 1) * BLOCK] for b in range(NBLK)], axis=0
                )
                for k in range(3)
            ]
        )
    )
    for copy in arriving[1:]:
        copy.wait()

    up_blocks, up_lanes = inverse_list(ghost_x, 0, 0, 2 * BLOCK, NBLK)
    down_blocks, down_lanes = inverse_list(ghost_x, 1, 0, 2 * BLOCK, NBLK)
    upper = iota((NBLK, BLOCK), 0) >= NBLK - NBY
    x_spot = jnp.where(
        upper, (up_blocks - 1.0) * BLOCK + up_lanes, (down_blocks - 1.0) * BLOCK + down_lanes
    )
    x_spot = jnp.maximum(x_spot, 0.0)
    lane = iota((1, BLOCK), 1)
    lane_f = lane.astype(jnp.float32)

    for b in range(NBLK):
        cut = slice(b * BLOCK, (b + 1) * BLOCK)
        alpha = polar[0:1, cut]
        living = live[0:1, cut].astype(jnp.float32)
        place = coords[:, cut]
        rhs = external[:, cut] * living
        code = lane_f + x_spot[b : b + 1, :] * BLOCK
        beta = lax.rsqrt(alpha) * math.sqrt(THOLE_FACTOR)
        tile = jnp.concatenate([place, beta, rhs, code], axis=0)
        more = jnp.concatenate(
            [living / alpha, living, jnp.zeros((6, BLOCK), jnp.float32)], axis=0
        )
        one_hot = jnp.where(iota((BLOCK, BLOCK), 0) == lanes_of[b : b + 1, :], 1.0, 0.0)
        one_hot = one_hot.astype(jnp.bfloat16)
        order[b] = one_hot
        ranked = permuted(dot_lanes, jnp.concatenate([tile, more], axis=0), one_hot)
        halo1[1, 1 + b // NBY, 1 + b % NBY] = ranked[:8]
        side[b] = ranked[8:]
        basis[0, b] = jnp.concatenate(
            [ranked[4:7], jnp.zeros((5, BLOCK), jnp.float32)], axis=0
        )
        flipped = jnp.transpose(ranked[:8])
        for g in range(NGRP):
            target[b * NGRP + g] = flipped[g * GROUP : (g + 1) * GROUP]

    pl.semaphore_wait(barrier, len(friends))
    for copy in halo_copies(halo1, sends.at[0], recvs.at[0], me, sizes):
        copy.start()

    def send_table(source, landing, step):
        pltpu.make_async_remote_copy(
            src_ref=source,
            dst_ref=landing,
            send_sem=sends.at[1],
            recv_sem=recvs.at[1],
            device_id=neighbour(me, sizes, step),
            device_id_type=MESH,
        ).start()

    for row, step_y in enumerate((1, -1)):
        blocks, lanes = inverse_list(ghost_y, row, 0, 6 * BLOCK, 12)
        own_y[row, 0:12] = (blocks - 1.0) * BLOCK + lanes
        for step_z in (-1, 1, 0):
            send_table(own_y.at[row], tabs_y.at[row, 1 - step_z], (0, step_y, step_z))
    for row, step_z in enumerate((1, -1)):
        own_z[row] = inverse_blocks(ghost_z, row, 24 * BLOCK)
        send_table(own_z.at[row], tabs_z.at[row], (0, 0, step_z))

    count = pairs.shape[1]
    bits = jnp.left_shift(alive[0:1, :], pairs[0:1, :]).astype(jnp.float32)
    bits = jnp.broadcast_to(bits, (8, count)).astype(jnp.bfloat16)
    listed = (iota((BLOCK, count), 0) == pairs[1:2, :]).astype(jnp.float32)
    listed_by = dot_lanes(bits, listed.astype(jnp.bfloat16), None)

    halo_bytes = window.at[pl.ds(0, 3 * NCOL - NBLK)]
    table_bytes = window.at[pl.ds(0, (6 * 16 + 2 * 24) // 8)]
    bytes_of(halo_bytes, recvs.at[0]).wait()
    bytes_of(table_bytes, recvs.at[1]).wait()

    for role in range(3):
        for part in range(NCOL // 8):
            codes = jnp.concatenate(
                [
                    halo1[role, c // CY, c % CY, 7:8, :]
                    for c in range(part * 8, part * 8 + 8)
                ],
                axis=0,
            ).astype(jnp.int32)
            spot = jnp.right_shift(codes, 7)
            own_lane = jnp.bitwise_and(codes, BLOCK - 1)
            col = iota((8, BLOCK), 0) + part * 8
            cx, cy = jnp.right_shift(col, 2), jnp.bitwise_and(col, 3)
            block_y = jnp.bitwise_and(cy + 1, 1)
            entry = ((cx - 1) * NBY + block_y) * BLOCK + own_lane
            entry = jnp.where(cx == 0, NBLK * BLOCK + spot, entry)
            entry = jnp.where(cx == CX - 1, (NBLK + NBY) * BLOCK + spot, entry)
            low = look_up(tabs_y[0, role, 0:12], entry)
            high = look_up(tabs_y[1, role, 0:12], entry)
            found = jnp.where(cy == 0, low, jnp.where(cy == CY - 1, high, 0.0))
            valid = found >= 0.0
            found = jnp.maximum(found, 0.0).astype(jnp.int32)
            entry = jnp.where(cy == 0, 12 * BLOCK + found, entry)
            entry = jnp.where(cy == CY - 1, 18 * BLOCK + found, entry)
            if role == 1:
                block = jnp.right_shift(entry, 7)
            else:
                layer = look_up(tabs_z[role // 2], entry)
                block = layer.astype(jnp.int32) + (24 if role == 0 else 48)
            mark = jnp.take_along_axis(listed_by, block, axis=1)
            marks[role, part * 8 : part * 8 + 8] = jnp.where(valid, mark, 0.0)

    row8 = iota((8, BLOCK), 0)
    lane8 = iota((8, BLOCK), 1)
    edge = [
        (jnp.where(m == 0, -n * size, 0.0), jnp.where(m == n - 1, n * size, 0.0))
        for m, n, size in zip(me, sizes, BRICK)
    ]

    def shifted(role, cx, cy):
        tile = halo1[role, cx, cy]
        col = cx * CY + cy
        if cx in (0, CX - 1):
            tile = tile + jnp.where(row8 == 0, edge[0][0 if cx == 0 else 1], 0.0)
        if cy in (0, CY - 1):
            tile = tile + jnp.where(row8 == 1, edge[1][0 if cy == 0 else 1], 0.0)
        if role != 1:
            tile = tile + jnp.where(row8 == 2, edge[2][role // 2], 0.0)
        return jnp.where(row8 == 7, marks[role, col : col + 1, :], tile)

    def windows(tile_at, rows, put, kinds):
        lanes = iota((rows, BLOCK), 1)
        z_site = jnp.right_shift(lanes, 5) * 2 + (jnp.right_shift(lanes, 2) & 1)
        x_site = (jnp.right_shift(lanes, 4) & 1) * 2 + (jnp.right_shift(lanes, 1) & 1)
        y_site = (jnp.right_shift(lanes, 3) & 1) * 2 + (lanes & 1)
        low_x = (x_site >= 1, x_site >= 3)
        low_y = (y_site >= 1, y_site >= 3)
        known = {}

        def layered(cx, cy, g):
            if (cx, cy) not in known:
                below, middle, above = [tile_at(role, cx, cy) for role in range(3)]
                known[cx, cy] = (
                    jnp.where(z_site >= 5, below, middle),
                    jnp.where(z_site >= 7, below, middle),
                    jnp.where(z_site < 1, above, middle),
                    jnp.where(z_site < 3, above, middle),
                )
            return known[cx, cy][g]

        def mixed_x(bx, half, cy, g):
            if (bx, half, cy, g) not in known:
                known[bx, half, cy, g] = jnp.where(
                    low_x[half], layered(bx, cy, g), layered(bx + 2, cy, g)
                )
            return known[bx, half, cy, g]

        def tile_of(kind, bx, by, g):
            if kind == 0:
                return layered(bx + 1, by + 1, g)
            if kind < 3:
                return mixed_x(bx, kind - 1, by + 1, g)
            if kind < 5:
                return jnp.where(
                    low_y[kind - 3], layered(bx + 1, by, g), layered(bx + 1, by + 2, g)
                )
            half_x, half_y = (kind - 5) // 2, (kind - 5) % 2
            return jnp.where(
                low_y[half_y], mixed_x(bx, half_x, by, g), mixed_x(bx, half_x, by + 2, g)
            )

        for g in range(NGRP):
            for bx in range(NBX):
                for by in range(NBY):
                    for kind in kinds:
                        put(((bx * NBY + by) * NGRP + g) * 9 + kind, tile_of(kind, bx, by, g))

    def put_window(at, tile):
        window[at] = tile

    windows(shifted, 8, put_window, range(9))

    cubes = [(hx, hy) for hx in range(2) for hy in range(2)]

    def windows_of(hx, hy):
        return (0, 1 + hx, 3 + hy, 5 + 2 * hx + hy)

    def spread_row(tile, k):
        return jnp.broadcast_to(tile[k : k + 1], (8, BLOCK))

    def add_field(total, tensor, moment):
        ax, ay, az, inner = tensor
        vx, vy, vz = moment
        along = ax * vx + ay * vy + az * vz
        parts = [along * a - inner * v for a, v in ((ax, vx), (ay, vy), (az, vz))]
        return parts if total is None else [t + p for t, p in zip(total, parts)]

    def keep_sums(block, g, u, total):
        for k in range(3):
            sums[block, k, pl.ds(pl.multiple_of(g * GROUP + u * 8, 8), 8)] = total[k]

    def build(step, carry):
        block, g = step // NGRP, step % NGRP
        mine = target[step]
        sources = []
        for w in range(9):
            tile = window[step * 9 + w]
            seen = jnp.bitwise_and(jnp.right_shift(tile[7:8].astype(jnp.int32), block), 1) == 1
            sx = jnp.where(seen, tile[0:1], FAR)
            sources.append(
                [jnp.broadcast_to(sx, (8, BLOCK))] + [spread_row(tile, k) for k in range(1, 7)]
            )
        for u, (hx, hy) in enumerate(cubes):
            tx, ty, tz, tb = [
                jnp.broadcast_to(mine[u * 8 : u * 8 + 8, k : k + 1], (8, BLOCK)) for k in range(4)
            ]
            total = None
            for n, w in enumerate(windows_of(hx, hy)):
                sx, sy, sz, sb, vx, vy, vz = sources[w]
                dx, dy, dz = tx - sx, ty - sy, tz - sz
                if n == 0:
                    itself = row8 + (g * GROUP + u * 8) == lane8
                    dx = jnp.where(itself, FAR, dx)
                q = dx * dx + dy * dy + dz * dz
                inv = lax.rsqrt(q)
                inv2 = inv * inv
                margin = jnp.maximum(CUTOFF_SQUARED - q, 0.0)
                scaled = q * (q * inv) * (tb * sb)
                damp = jnp.exp(-scaled)
                rest = 1.0 - damp
                near = margin * inv2
                inner = (near * margin) * (inv * rest)
                root = (3.0 * inv) * (rest - scaled * damp)
                scale = near * (root * lax.rsqrt(root))
                tensor = (scale * dx, scale * dy, scale * dz, inner)
                slot = step * 16 + u * 4 + n
                px[slot], py[slot], pz[slot], inner_s[slot] = tensor
                total = add_field(total, tensor, (vx, vy, vz))
            keep_sums(block, g, u, total)
        return carry

    lax.fori_loop(0, NBLK * NGRP, build, 0, unroll=4)

    def apply(parts, step, carry):
        block, g = step // NGRP, step % NGRP
        sources = {}
        for u, (hx, hy) in enumerate(cubes):
            total = None
            if 0 not in parts:
                rows = pl.ds(pl.multiple_of(g * GROUP + u * 8, 8), 8)
                total = [sums[block, k, rows] for k in range(3)]
            for n in parts:
                w = windows_of(hx, hy)[n]
                if w not in sources:
                    tile = moved[step * 9 + w]
                    sources[w] = [spread_row(tile, k) for k in range(3)]
                slot = step * 16 + u * 4 + n
                tensor = (px[slot], py[slot], pz[slot], inner_s[slot])
                total = add_field(total, tensor, sources[w])
            keep_sums(block, g, u, total)
        return carry

    ones = jnp.ones((8, BLOCK), jnp.float32)
    ones_half = ones.astype(jnp.bfloat16)

    def next_basis(level, halo):
        for b in range(NBLK):
            parts = [halves(sums[b, k], 2) for k in range(3)]
            field = dot_lanes(ones_half, jnp.concatenate(parts, axis=0), None)
            field = [
                field[:, 2 * k * BLOCK : (2 * k + 1) * BLOCK]
                + field[:, (2 * k + 1) * BLOCK : (2 * k + 2) * BLOCK]
                for k in range(3)
            ]
            field = jnp.where(row8 == 0, field[0], jnp.where(row8 == 1, field[1], field[2]))
            field = field * (1.0 / CUTOFF_SQUARED**2)
            v = basis[level, b]
            rows = side[b]
            image = rows[0:1] * v - rows[1:2] * field
            image = (image - CENTRE * v) * (1.0 / HALF)
            if level > 0:
                image = 2.0 * image - basis[level - 1, b]
            image = jnp.where(row8 < 3, image, 0.0)
            basis[level + 1, b] = image
            if halo is not None:
                halo[1, 1 + b // NBY, 1 + b % NBY] = image[:4]

    def put_moved(at, tile):
        moved[at] = tile

    started = [(halo_bytes, sends.at[0]), (table_bytes, sends.at[1])]
    halves_of = {1: 14, 2: 14, 3: 4}
    works = ((1, (0,), (0,)), (2, (1, 2, 3, 4), (1, 2)), (3, (5, 6, 7, 8), (3,)))

    def put_moved(at, tile):
        moved[at] = tile

    for level, halo in ((0, halo2), (1, halo3)):
        next_basis(level, halo)
        for distance in (3, 2, 1):
            sem = 2 + 3 * level + distance - 1
            for copy in halo_copies(halo, sends.at[sem], recvs.at[sem], me, sizes, distance):
                copy.start()
        for distance, kinds, parts in works:
            sem = 2 + 3 * level + distance - 1
            view = window.at[pl.ds(0, halves_of[distance])]
            bytes_of(view, recvs.at[sem]).wait()
            started.append((view, sends.at[sem]))
            windows(lambda role, cx, cy, halo=halo: halo[role, cx, cy], 4, put_moved, kinds)
            lax.fori_loop(0, NBLK * NGRP, functools.partial(apply, parts), 0, unroll=4)
    next_basis(2, None)

    rows = []
    for a, b in GRAM:
        part = jnp.sum(basis[a] * basis[b], axis=0)
        rows.append(jnp.sum(part, axis=0, keepdims=True))
    rows.append(jnp.zeros((BLOCK - len(GRAM), BLOCK), jnp.float32))
    total = dot_lanes(ones, jnp.concatenate(rows, axis=0))[0:1]
    along, across = sum_stages(sizes)
    reduce_over(along, total, slot_x, me[0], sends.at[8], recvs.at[8], me, sizes)
    for b in range(NBLK):
        stacked = jnp.concatenate([basis[k, b] for k in range(4)], axis=0)
        flat[:, b * BLOCK : (b + 1) * BLOCK] = permuted(dot_rows, stacked, order[b])
    total = reduced(along, slot_x, recvs.at[8])
    place = me[1] * sizes[2] + me[2]
    reduce_over(across, total, slot_y, place, sends.at[9], recvs.at[9], me, sizes)
    total = reduced(across, slot_y, recvs.at[9])
    started.append((slot_x.at[pl.ds(0, len(along))], sends.at[8]))
    started.append((slot_y.at[pl.ds(0, len(across))], sends.at[9]))
    products = {}
    for k, (a, b) in enumerate(GRAM):
        products[a, b] = products[b, a] = total[:, k : k + 1]
    answer, left = gradient_steps(products)

    def combined(coefficients):
        value = 0.0
        for k, c in enumerate(coefficients):
            if c is not None:
                value = value + c * flat[8 * k : 8 * k + 3, :]
        return value

    answers[...] = jnp.concatenate(
        [combined(answer), combined(left), jnp.zeros((2, answers.shape[1]), jnp.float32)], axis=0
    )
    for view, sem in started:
        bytes_of(view, sem).wait()


def per_device(
    sizes, coords, polarizability, external_field, bead_live,
    ghost_x, ghost_y, ghost_z, pair_blocks, pair_live,
):
    nloc = coords.shape[1]
    vmem = pl.BlockSpec(memory_space=pltpu.VMEM)
    f32 = jnp.float32
    operands = (
        coords, polarizability.reshape(1, nloc), external_field, bead_live.reshape(1, nloc),
        ghost_x, ghost_y, ghost_z, pair_blocks, pair_live.reshape(1, pair_live.shape[0]),
    )
    tensors = pltpu.VMEM((NBLK * NGRP * 16, 8, BLOCK), f32)
    stages = (sizes[0], sizes[1] * sizes[2])
    answers = pl.pallas_call(
        functools.partial(field_kernel, sizes),
        out_shape=pltpu.VMEM((8, nloc), f32),
        in_specs=[pl.BlockSpec(memory_space=pltpu.HBM)] * len(operands),
        out_specs=vmem,
        scratch_shapes=[pltpu.VMEM(x.shape, x.dtype) for x in operands]
        + [
            pltpu.SemaphoreType.DMA((len(operands),)),
            pltpu.VMEM((3, CX, CY, 8, BLOCK), f32),
            pltpu.VMEM((3, CX, CY, 4, BLOCK), f32),
            pltpu.VMEM((3, CX, CY, 4, BLOCK), f32),
            pltpu.VMEM((2, 3, 16, BLOCK), f32),
            pltpu.VMEM((2, 24, BLOCK), f32),
            pltpu.VMEM((2, 16, BLOCK), f32),
            pltpu.VMEM((2, 24, BLOCK), f32),
            pltpu.SemaphoreType.DMA((10,)),
            pltpu.SemaphoreType.DMA((10,)),
            pltpu.VMEM((NBLK, BLOCK, BLOCK), jnp.bfloat16),
            pltpu.VMEM((NBLK, 8, BLOCK), f32),
            pltpu.VMEM((NBLK * NGRP, GROUP, 8), f32),
            pltpu.VMEM((NBLK * NGRP * 9, 8, BLOCK), f32),
            pltpu.VMEM((NBLK * NGRP * 9, 4, BLOCK), f32),
            pltpu.VMEM((3, NCOL, BLOCK), f32),
            tensors, tensors, tensors, tensors,
            pltpu.VMEM((NBLK, 3, BLOCK, BLOCK), f32),
            pltpu.VMEM((4, NBLK, 8, BLOCK), f32),
            pltpu.VMEM((32, nloc), f32),
        ]
        + [pltpu.VMEM((n, 1, BLOCK), f32) for n in stages],
        compiler_params=pltpu.CompilerParams(
            collective_id=0, has_side_effects=True, vmem_limit_bytes=63 * 2**20
        ),
    )(*operands)
    return answers[0:3], polarizability[None] * answers[3:6]


def solution(mesh):
    sizes = tuple(mesh.shape[name] for name in ("gx", "gy", "gz"))
    wide = P(None, ("gx", "gy", "gz"))
    flat = P(("gx", "gy", "gz"))
    return jax.shard_map(
        functools.partial(per_device, sizes),
        mesh=mesh,
        in_specs=(wide, flat, wide, flat, wide, wide, wide, wide, flat),
        out_specs=(wide, wide),
        check_vma=False,
    )
```

```python
import functools
import math

import jax
import jax.numpy as jnp
from jax import lax
from jax.experimental import pallas as pl
from jax.experimental.pallas import tpu as pltpu
from jax.sharding import PartitionSpec as P

BLOCK = 128
NBX, NBY = 4, 2
NBLK = NBX * NBY
CX, CY = NBX + 2, NBY + 2
NCOL = CX * CY
GROUP = 32
NGRP = BLOCK // GROUP
BRICK = (16.0, 8.0, 8.0)
CUTOFF_SQUARED = 12.25
THOLE_FACTOR = 0.02
CENTRE, HALF = 12.5, 8.5
FAR = 1.0e6
MESH = pl.DeviceIdType.MESH
HIGHEST = lax.Precision.HIGHEST
OFFSETS = [
    (x, y, z)
    for x in (-1, 0, 1)
    for y in (-1, 0, 1)
    for z in (-1, 0, 1)
    if (x, y, z) != (0, 0, 0)
]
GRAM = [(a, b) for a in range(4) for b in range(a, 4)]


def dot_rows(left, right, precision=HIGHEST):
    return lax.dot_general(
        left, right, (((1,), (0,)), ((), ())), precision=precision,
        preferred_element_type=jnp.float32,
    )


def dot_lanes(left, right, precision=HIGHEST):
    return lax.dot_general(
        left, right, (((1,), (1,)), ((), ())), precision=precision,
        preferred_element_type=jnp.float32,
    )


def halves(x, parts):
    out = []
    for _ in range(parts):
        part = x.astype(jnp.bfloat16)
        out.append(part)
        x = x - part.astype(jnp.float32)
    return jnp.concatenate(out, axis=0)


def permuted(dot, x, one_hot):
    rows = x.shape[0]
    out = dot(halves(x, 3), one_hot, None)
    return out[:rows] + out[rows : 2 * rows] + out[2 * rows :]


def iota(shape, axis):
    return lax.broadcasted_iota(jnp.int32, shape, axis)


def own_span(step, count):
    return (0, count) if step == 0 else ((count - 1, 1) if step > 0 else (0, 1))


def halo_span(step, count):
    return (1, count) if step == 0 else ((0, 1) if step > 0 else (count + 1, 1))


def site_ranks(place):
    tie = iota((BLOCK, BLOCK), 0) < iota((BLOCK, BLOCK), 1)
    base = jnp.zeros((NBLK, BLOCK), jnp.float32)
    for axis, shift in ((2, 4), (0, 2), (1, 0)):
        key = base + place[axis]
        column = jnp.transpose(key)
        ranks = []
        for b in range(NBLK):
            left = jnp.broadcast_to(column[:, b : b + 1], (BLOCK, BLOCK))
            right = jnp.broadcast_to(key[b : b + 1, :], (BLOCK, BLOCK))
            before = jnp.logical_or(left < right, jnp.logical_and(left == right, tie))
            ranks.append(jnp.sum(jnp.where(before, 1.0, 0.0), axis=0, keepdims=True))
        rank = jnp.concatenate(ranks, axis=0).astype(jnp.int32)
        base = jnp.right_shift(rank, shift).astype(jnp.float32) * 512.0
    return rank


def site_lanes(rank):
    z, x, y = jnp.right_shift(rank, 4), jnp.right_shift(rank, 2) & 3, rank & 3
    cube = jnp.right_shift(z, 1) * 4 + jnp.right_shift(x, 1) * 2 + jnp.right_shift(y, 1)
    return cube * 8 + (z & 1) * 4 + (x & 1) * 2 + (y & 1)


def inverse_list(list_ref, row, first, entries, tables):
    blocks = jnp.zeros((tables, BLOCK), jnp.float32)
    lanes = jnp.zeros((tables, BLOCK), jnp.float32)
    spot = iota((BLOCK, BLOCK), 1).astype(jnp.float32)
    for r in range(entries // BLOCK):
        entry = list_ref[row : row + 1, r * BLOCK : (r + 1) * BLOCK]
        high = jnp.right_shift(entry, 7) - first
        low = jnp.bitwise_and(entry, BLOCK - 1)
        pick = (iota((tables, BLOCK), 0) == high).astype(jnp.float32)
        place = (iota((BLOCK, BLOCK), 0) == low).astype(jnp.float32)
        both = jnp.concatenate([place, place * spot], axis=0).astype(jnp.bfloat16)
        found = dot_lanes(pick.astype(jnp.bfloat16), both, None)
        blocks = blocks + found[:, :BLOCK] * float(r + 1)
        lanes = lanes + found[:, BLOCK:]
    return blocks, lanes


def inverse_blocks(list_ref, row, entries):
    rows = entries // BLOCK
    total = jnp.zeros((rows, BLOCK), jnp.float32)
    for r in range(rows):
        entry = list_ref[row : row + 1, r * BLOCK : (r + 1) * BLOCK]
        high = jnp.right_shift(entry, 7)
        low = jnp.bitwise_and(entry, BLOCK - 1)
        pick = jnp.where(iota((rows, BLOCK), 0) == high, float(r), 0.0)
        place = (iota((BLOCK, BLOCK), 0) == low).astype(jnp.float32)
        total = total + dot_lanes(
            pick.astype(jnp.bfloat16), place.astype(jnp.bfloat16), None
        )
    return total


def look_up(table, index):
    high = jnp.right_shift(index, 7)
    low = jnp.bitwise_and(index, BLOCK - 1)
    out = jnp.zeros(index.shape, jnp.float32)
    for r in range(table.shape[0]):
        row = jnp.broadcast_to(table[r : r + 1, :], index.shape)
        out = jnp.where(high == r, jnp.take_along_axis(row, low, axis=1), out)
    return out


def place_of(sizes):
    return tuple(lax.axis_index(name) for name in ("gx", "gy", "gz"))


def neighbour(me, sizes, step):
    return tuple(lax.rem(m + s + n, n) for m, s, n in zip(me, step, sizes))


def greet(targets):
    barrier = pltpu.get_barrier_semaphore()
    for target in targets:
        pl.semaphore_signal(barrier, inc=1, device_id=target, device_id_type=MESH)
    return barrier


def bytes_of(view, sem):
    return pltpu.make_async_copy(view, view, sem)


def hops(step):
    return sum(abs(s) for s in step)


def halo_copies(buffer, send_sem, recv_sem, me, sizes, distance=None):
    copies = []
    for step in sorted(OFFSETS, key=hops, reverse=True):
        if distance is not None and hops(step) != distance:
            continue
        (xs, xn), (ys, yn) = own_span(step[0], NBX), own_span(step[1], NBY)
        (xd, _), (yd, _) = halo_span(step[0], NBX), halo_span(step[1], NBY)
        copies.append(
            pltpu.make_async_remote_copy(
                src_ref=buffer.at[1, pl.ds(1 + xs, xn), pl.ds(1 + ys, yn)],
                dst_ref=buffer.at[1 - step[2], pl.ds(xd, xn), pl.ds(yd, yn)],
                send_sem=send_sem,
                recv_sem=recv_sem,
                device_id=neighbour(me, sizes, step),
                device_id_type=MESH,
            )
        )
    return copies


def sum_stages(sizes):
    def near(step):
        return tuple(s if 2 * s <= n else s - n for s, n in zip(step, sizes))

    along = [near((s, 0, 0)) for s in range(1, sizes[0])]
    across = [near((0, y, z)) for y in range(sizes[1]) for z in range(sizes[2]) if y + z > 0]
    return sorted(along, key=hops, reverse=True), sorted(across, key=hops, reverse=True)


def reduce_over(steps, total, slot, place, send, recv, me, sizes):
    slot[place] = total
    copies = []
    for step in steps:
        copies.append(
            pltpu.make_async_remote_copy(
                src_ref=slot.at[place],
                dst_ref=slot.at[place],
                send_sem=send,
                recv_sem=recv,
                device_id=neighbour(me, sizes, step),
                device_id_type=MESH,
            )
        )
    for copy in copies:
        copy.start()


def reduced(steps, slot, recv):
    bytes_of(slot.at[pl.ds(0, len(steps))], recv).wait()
    total = slot[0]
    for k in range(1, len(steps) + 1):
        total = total + slot[k]
    return total


def gradient_steps(products):
    def inner(left, right):
        value = 0.0
        for a, p in enumerate(left):
            for b, q in enumerate(right):
                if p is not None and q is not None:
                    value = value + p * q * products[a, b]
        return value

    def plus(p, q):
        return q if p is None else (p if q is None else p + q)

    def times(scale, p):
        return None if p is None else scale * p

    def applied(c):
        out = [times(CENTRE, p) for p in c]
        if c[0] is not None:
            out[1] = plus(out[1], HALF * c[0])
        for k in (1, 2):
            if c[k] is not None:
                out[k - 1] = plus(out[k - 1], (0.5 * HALF) * c[k])
                out[k + 1] = plus(out[k + 1], (0.5 * HALF) * c[k])
        return out

    left = [jnp.ones((1, 1), jnp.float32), None, None, None]
    direction = list(left)
    answer = [None] * 4
    norm = products[0, 0]
    for _ in range(3):
        image = applied(direction)
        step = norm / inner(direction, image)
        answer = [plus(p, times(step, q)) for p, q in zip(answer, direction)]
        left = [plus(p, times(-step, q)) for p, q in zip(left, image)]
        after = inner(left, left)
        direction = [plus(p, times(after / norm, q)) for p, q in zip(left, direction)]
        norm = after
    return answer, left


def field_kernel(
    sizes,
    coords_in, polar_in, external_in, live_in, ghost_x_in, ghost_y_in, ghost_z_in,
    pairs_in, alive_in,
    answers,
    coords, polar, external, live, ghost_x, ghost_y, ghost_z, pairs, alive, loads,
    halo1, halo2, halo3, tabs_y, tabs_z, own_y, own_z, sends, recvs,
    order, side, target, window, moved, marks, px, py, pz, inner_s, sums, basis, flat,
    slot_x, slot_y, two_steps, four_steps,
):
    me = place_of(sizes)
    outside = (
        coords_in, polar_in, external_in, live_in, ghost_x_in, ghost_y_in, ghost_z_in,
        pairs_in, alive_in,
    )
    inside = (coords, polar, external, live, ghost_x, ghost_y, ghost_z, pairs, alive)
    arriving = [
        pltpu.make_async_copy(far, near, loads.at[n])
        for n, (far, near) in enumerate(zip(outside, inside))
    ]
    for copy in arriving:
        copy.start()
    chained = sizes[0] == 16 and sizes[1] <= 8 and sizes[2] <= 4
    friends = dict.fromkeys(list(OFFSETS) + ([] if chained else sum(sum_stages(sizes), [])))

    def relay(sem, reach):
        if chained:
            for step in (reach, -reach):
                pl.semaphore_signal(
                    sem, inc=1, device_id=neighbour(me, sizes, (step, 0, 0)), device_id_type=MESH
                )

    def relayed(sem):
        if chained:
            pl.semaphore_wait(sem, 2)

    barrier = greet([neighbour(me, sizes, step) for step in friends])
    arriving[0].wait()

    lanes_of = site_lanes(
        site_ranks(
            [
                jnp.concatenate(
                    [coords[k : k + 1, b * BLOCK : (b + 1) * BLOCK] for b in range(NBLK)], axis=0
                )
                for k in range(3)
            ]
        )
    )
    for copy in arriving[1:]:
        copy.wait()

    up_blocks, up_lanes = inverse_list(ghost_x, 0, 0, 2 * BLOCK, NBLK)
    down_blocks, down_lanes = inverse_list(ghost_x, 1, 0, 2 * BLOCK, NBLK)
    upper = iota((NBLK, BLOCK), 0) >= NBLK - NBY
    x_spot = jnp.where(
        upper, (up_blocks - 1.0) * BLOCK + up_lanes, (down_blocks - 1.0) * BLOCK + down_lanes
    )
    x_spot = jnp.maximum(x_spot, 0.0)
    lane = iota((1, BLOCK), 1)
    lane_f = lane.astype(jnp.float32)

    for b in range(NBLK):
        cut = slice(b * BLOCK, (b + 1) * BLOCK)
        alpha = polar[0:1, cut]
        living = live[0:1, cut].astype(jnp.float32)
        place = coords[:, cut]
        rhs = external[:, cut] * living
        code = lane_f + x_spot[b : b + 1, :] * BLOCK
        beta = lax.rsqrt(alpha) * math.sqrt(THOLE_FACTOR)
        tile = jnp.concatenate([place, beta, rhs, code], axis=0)
        more = jnp.concatenate(
            [living / alpha, living, jnp.zeros((6, BLOCK), jnp.float32)], axis=0
        )
        one_hot = jnp.where(iota((BLOCK, BLOCK), 0) == lanes_of[b : b + 1, :], 1.0, 0.0)
        one_hot = one_hot.astype(jnp.bfloat16)
        order[b] = one_hot
        ranked = permuted(dot_lanes, jnp.concatenate([tile, more], axis=0), one_hot)
        halo1[1, 1 + b // NBY, 1 + b % NBY] = ranked[:8]
        side[b] = ranked[8:]
        basis[0, b] = jnp.concatenate(
            [ranked[4:7], jnp.zeros((5, BLOCK), jnp.float32)], axis=0
        )
        flipped = jnp.transpose(ranked[:8])
        for g in range(NGRP):
            target[b * NGRP + g] = flipped[g * GROUP : (g + 1) * GROUP]

    pl.semaphore_wait(barrier, len(friends))
    for copy in halo_copies(halo1, sends.at[0], recvs.at[0], me, sizes):
        copy.start()

    def send_table(source, landing, step):
        pltpu.make_async_remote_copy(
            src_ref=source,
            dst_ref=landing,
            send_sem=sends.at[1],
            recv_sem=recvs.at[1],
            device_id=neighbour(me, sizes, step),
            device_id_type=MESH,
        ).start()

    for row, step_y in enumerate((1, -1)):
        blocks, lanes = inverse_list(ghost_y, row, 0, 6 * BLOCK, 12)
        own_y[row, 0:12] = (blocks - 1.0) * BLOCK + lanes
        for step_z in (-1, 1, 0):
            send_table(own_y.at[row], tabs_y.at[row, 1 - step_z], (0, step_y, step_z))
    for row, step_z in enumerate((1, -1)):
        own_z[row] = inverse_blocks(ghost_z, row, 24 * BLOCK)
        send_table(own_z.at[row], tabs_z.at[row], (0, 0, step_z))

    count = pairs.shape[1]
    bits = jnp.left_shift(alive[0:1, :], pairs[0:1, :]).astype(jnp.float32)
    bits = jnp.broadcast_to(bits, (8, count)).astype(jnp.bfloat16)
    listed = (iota((BLOCK, count), 0) == pairs[1:2, :]).astype(jnp.float32)
    listed_by = dot_lanes(bits, listed.astype(jnp.bfloat16), None)

    halo_bytes = window.at[pl.ds(0, 3 * NCOL - NBLK)]
    table_bytes = window.at[pl.ds(0, (6 * 16 + 2 * 24) // 8)]
    bytes_of(halo_bytes, recvs.at[0]).wait()
    bytes_of(table_bytes, recvs.at[1]).wait()
    relay(two_steps, 2)

    for role in range(3):
        for part in range(NCOL // 8):
            codes = jnp.concatenate(
                [
                    halo1[role, c // CY, c % CY, 7:8, :]
                    for c in range(part * 8, part * 8 + 8)
                ],
                axis=0,
            ).astype(jnp.int32)
            spot = jnp.right_shift(codes, 7)
            own_lane = jnp.bitwise_and(codes, BLOCK - 1)
            col = iota((8, BLOCK), 0) + part * 8
            cx, cy = jnp.right_shift(col, 2), jnp.bitwise_and(col, 3)
            block_y = jnp.bitwise_and(cy + 1, 1)
            entry = ((cx - 1) * NBY + block_y) * BLOCK + own_lane
            entry = jnp.where(cx == 0, NBLK * BLOCK + spot, entry)
            entry = jnp.where(cx == CX - 1, (NBLK + NBY) * BLOCK + spot, entry)
            low = look_up(tabs_y[0, role, 0:12], entry)
            high = look_up(tabs_y[1, role, 0:12], entry)
            found = jnp.where(cy == 0, low, jnp.where(cy == CY - 1, high, 0.0))
            valid = found >= 0.0
            found = jnp.maximum(found, 0.0).astype(jnp.int32)
            entry = jnp.where(cy == 0, 12 * BLOCK + found, entry)
            entry = jnp.where(cy == CY - 1, 18 * BLOCK + found, entry)
            if role == 1:
                block = jnp.right_shift(entry, 7)
            else:
                layer = look_up(tabs_z[role // 2], entry)
                block = layer.astype(jnp.int32) + (24 if role == 0 else 48)
            mark = jnp.take_along_axis(listed_by, block, axis=1)
            marks[role, part * 8 : part * 8 + 8] = jnp.where(valid, mark, 0.0)

    row8 = iota((8, BLOCK), 0)
    lane8 = iota((8, BLOCK), 1)
    edge = [
        (jnp.where(m == 0, -n * size, 0.0), jnp.where(m == n - 1, n * size, 0.0))
        for m, n, size in zip(me, sizes, BRICK)
    ]

    def shifted(role, cx, cy):
        tile = halo1[role, cx, cy]
        col = cx * CY + cy
        if cx in (0, CX - 1):
            tile = tile + jnp.where(row8 == 0, edge[0][0 if cx == 0 else 1], 0.0)
        if cy in (0, CY - 1):
            tile = tile + jnp.where(row8 == 1, edge[1][0 if cy == 0 else 1], 0.0)
        if role != 1:
            tile = tile + jnp.where(row8 == 2, edge[2][role // 2], 0.0)
        return jnp.where(row8 == 7, marks[role, col : col + 1, :], tile)

    def windows(tile_at, rows, put, kinds):
        lanes = iota((rows, BLOCK), 1)
        z_site = jnp.right_shift(lanes, 5) * 2 + (jnp.right_shift(lanes, 2) & 1)
        x_site = (jnp.right_shift(lanes, 4) & 1) * 2 + (jnp.right_shift(lanes, 1) & 1)
        y_site = (jnp.right_shift(lanes, 3) & 1) * 2 + (lanes & 1)
        low_x = (x_site >= 1, x_site >= 3)
        low_y = (y_site >= 1, y_site >= 3)
        known = {}

        def layered(cx, cy, g):
            if (cx, cy) not in known:
                below, middle, above = [tile_at(role, cx, cy) for role in range(3)]
                known[cx, cy] = (
                    jnp.where(z_site >= 5, below, middle),
                    jnp.where(z_site >= 7, below, middle),
                    jnp.where(z_site < 1, above, middle),
                    jnp.where(z_site < 3, above, middle),
                )
            return known[cx, cy][g]

        def mixed_x(bx, half, cy, g):
            if (bx, half, cy, g) not in known:
                known[bx, half, cy, g] = jnp.where(
                    low_x[half], layered(bx, cy, g), layered(bx + 2, cy, g)
                )
            return known[bx, half, cy, g]

        def tile_of(kind, bx, by, g):
            if kind == 0:
                return layered(bx + 1, by + 1, g)
            if kind < 3:
                return mixed_x(bx, kind - 1, by + 1, g)
            if kind < 5:
                return jnp.where(
                    low_y[kind - 3], layered(bx + 1, by, g), layered(bx + 1, by + 2, g)
                )
            half_x, half_y = (kind - 5) // 2, (kind - 5) % 2
            return jnp.where(
                low_y[half_y], mixed_x(bx, half_x, by, g), mixed_x(bx, half_x, by + 2, g)
            )

        for g in range(NGRP):
            for bx in range(NBX):
                for by in range(NBY):
                    for kind in kinds:
                        put(((bx * NBY + by) * NGRP + g) * 9 + kind, tile_of(kind, bx, by, g))

    def put_window(at, tile):
        window[at] = tile

    windows(shifted, 8, put_window, range(9))

    cubes = [(hx, hy) for hx in range(2) for hy in range(2)]

    def windows_of(hx, hy):
        return (0, 1 + hx, 3 + hy, 5 + 2 * hx + hy)

    def spread_row(tile, k):
        return jnp.broadcast_to(tile[k : k + 1], (8, BLOCK))

    def add_field(total, tensor, moment):
        ax, ay, az, inner = tensor
        vx, vy, vz = moment
        along = ax * vx + ay * vy + az * vz
        parts = [along * a - inner * v for a, v in ((ax, vx), (ay, vy), (az, vz))]
        return parts if total is None else [t + p for t, p in zip(total, parts)]

    def keep_sums(block, g, u, total):
        for k in range(3):
            sums[block, k, pl.ds(pl.multiple_of(g * GROUP + u * 8, 8), 8)] = total[k]

    def build(step, carry):
        block, g = step // NGRP, step % NGRP
        mine = target[step]
        sources = []
        for w in range(9):
            tile = window[step * 9 + w]
            seen = jnp.bitwise_and(jnp.right_shift(tile[7:8].astype(jnp.int32), block), 1) == 1
            sx = jnp.where(seen, tile[0:1], FAR)
            sources.append(
                [jnp.broadcast_to(sx, (8, BLOCK))] + [spread_row(tile, k) for k in range(1, 7)]
            )
        for u, (hx, hy) in enumerate(cubes):
            tx, ty, tz, tb = [
                jnp.broadcast_to(mine[u * 8 : u * 8 + 8, k : k + 1], (8, BLOCK)) for k in range(4)
            ]
            total = None
            for n, w in enumerate(windows_of(hx, hy)):
                sx, sy, sz, sb, vx, vy, vz = sources[w]
                dx, dy, dz = tx - sx, ty - sy, tz - sz
                if n == 0:
                    itself = row8 + (g * GROUP + u * 8) == lane8
                    dx = jnp.where(itself, FAR, dx)
                q = dx * dx + dy * dy + dz * dz
                inv = lax.rsqrt(q)
                inv2 = inv * inv
                margin = jnp.maximum(CUTOFF_SQUARED - q, 0.0)
                scaled = q * (q * inv) * (tb * sb)
                damp = jnp.exp(-scaled)
                rest = 1.0 - damp
                near = margin * inv2
                inner = (near * margin) * (inv * rest)
                root = (3.0 * inv) * (rest - scaled * damp)
                scale = near * (root * lax.rsqrt(root))
                tensor = (scale * dx, scale * dy, scale * dz, inner)
                slot = step * 16 + u * 4 + n
                px[slot], py[slot], pz[slot], inner_s[slot] = tensor
                total = add_field(total, tensor, (vx, vy, vz))
            keep_sums(block, g, u, total)
        return carry

    lax.fori_loop(0, NBLK * NGRP, build, 0, unroll=4)

    def apply(parts, step, carry):
        block, g = step // NGRP, step % NGRP
        sources = {}
        for u, (hx, hy) in enumerate(cubes):
            total = None
            if 0 not in parts:
                rows = pl.ds(pl.multiple_of(g * GROUP + u * 8, 8), 8)
                total = [sums[block, k, rows] for k in range(3)]
            for n in parts:
                w = windows_of(hx, hy)[n]
                if w not in sources:
                    tile = moved[step * 9 + w]
                    sources[w] = [spread_row(tile, k) for k in range(3)]
                slot = step * 16 + u * 4 + n
                tensor = (px[slot], py[slot], pz[slot], inner_s[slot])
                total = add_field(total, tensor, sources[w])
            keep_sums(block, g, u, total)
        return carry

    ones = jnp.ones((8, BLOCK), jnp.float32)
    ones_half = ones.astype(jnp.bfloat16)

    def next_basis(level, halo):
        for b in range(NBLK):
            parts = [halves(sums[b, k], 2) for k in range(3)]
            field = dot_lanes(ones_half, jnp.concatenate(parts, axis=0), None)
            field = [
                field[:, 2 * k * BLOCK : (2 * k + 1) * BLOCK]
                + field[:, (2 * k + 1) * BLOCK : (2 * k + 2) * BLOCK]
                for k in range(3)
            ]
            field = jnp.where(row8 == 0, field[0], jnp.where(row8 == 1, field[1], field[2]))
            field = field * (1.0 / CUTOFF_SQUARED**2)
            v = basis[level, b]
            rows = side[b]
            image = rows[0:1] * v - rows[1:2] * field
            image = (image - CENTRE * v) * (1.0 / HALF)
            if level > 0:
                image = 2.0 * image - basis[level - 1, b]
            image = jnp.where(row8 < 3, image, 0.0)
            basis[level + 1, b] = image
            if halo is not None:
                halo[1, 1 + b // NBY, 1 + b % NBY] = image[:4]

    def put_moved(at, tile):
        moved[at] = tile

    started = [(halo_bytes, sends.at[0]), (table_bytes, sends.at[1])]
    halves_of = {1: 14, 2: 14, 3: 4}
    works = ((1, (0,), (0,)), (2, (1, 2, 3, 4), (1, 2)), (3, (5, 6, 7, 8), (3,)))

    def put_moved(at, tile):
        moved[at] = tile

    def gram_row(a, b):
        part = jnp.sum(basis[a] * basis[b], axis=0)
        return jnp.sum(part, axis=0, keepdims=True)

    for level, halo in ((0, halo2), (1, halo3)):
        next_basis(level, halo)
        for distance in (3, 2, 1):
            sem = 2 + 3 * level + distance - 1
            for copy in halo_copies(halo, sends.at[sem], recvs.at[sem], me, sizes, distance):
                copy.start()
        if level == 1:
            early = {(a, b): gram_row(a, b) for a, b in GRAM if b < 3}
        for distance, kinds, parts in works:
            sem = 2 + 3 * level + distance - 1
            view = window.at[pl.ds(0, halves_of[distance])]
            bytes_of(view, recvs.at[sem]).wait()
            started.append((view, sends.at[sem]))
            windows(lambda role, cx, cy, halo=halo: halo[role, cx, cy], 4, put_moved, kinds)
            lax.fori_loop(0, NBLK * NGRP, functools.partial(apply, parts), 0, unroll=8)
            if level == 0 and distance == 3:
                relayed(two_steps)
                relay(four_steps, 4)
    next_basis(2, None)

    rows = [early[a, b] if b < 3 else gram_row(a, b) for a, b in GRAM]
    rows.append(jnp.zeros((BLOCK - len(GRAM), BLOCK), jnp.float32))
    total = dot_lanes(ones, jnp.concatenate(rows, axis=0))[0:1]
    along, across = sum_stages(sizes)
    relayed(four_steps)
    reduce_over(along, total, slot_x, me[0], sends.at[8], recvs.at[8], me, sizes)
    for b in range(NBLK):
        stacked = jnp.concatenate([basis[k, b] for k in range(4)], axis=0)
        flat[:, b * BLOCK : (b + 1) * BLOCK] = permuted(dot_rows, stacked, order[b])
    total = reduced(along, slot_x, recvs.at[8])
    place = me[1] * sizes[2] + me[2]
    reduce_over(across, total, slot_y, place, sends.at[9], recvs.at[9], me, sizes)
    total = reduced(across, slot_y, recvs.at[9])
    started.append((slot_x.at[pl.ds(0, len(along))], sends.at[8]))
    started.append((slot_y.at[pl.ds(0, len(across))], sends.at[9]))
    products = {}
    for k, (a, b) in enumerate(GRAM):
        products[a, b] = products[b, a] = total[:, k : k + 1]
    answer, left = gradient_steps(products)

    def combined(coefficients):
        value = 0.0
        for k, c in enumerate(coefficients):
            if c is not None:
                value = value + c * flat[8 * k : 8 * k + 3, :]
        return value

    answers[...] = jnp.concatenate(
        [combined(answer), combined(left), jnp.zeros((2, answers.shape[1]), jnp.float32)], axis=0
    )
    for view, sem in started:
        bytes_of(view, sem).wait()


def per_device(
    sizes, coords, polarizability, external_field, bead_live,
    ghost_x, ghost_y, ghost_z, pair_blocks, pair_live,
):
    nloc = coords.shape[1]
    vmem = pl.BlockSpec(memory_space=pltpu.VMEM)
    f32 = jnp.float32
    operands = (
        coords, polarizability.reshape(1, nloc), external_field, bead_live.reshape(1, nloc),
        ghost_x, ghost_y, ghost_z, pair_blocks, pair_live.reshape(1, pair_live.shape[0]),
    )
    tensors = pltpu.VMEM((NBLK * NGRP * 16, 8, BLOCK), f32)
    stages = (sizes[0], sizes[1] * sizes[2])
    answers = pl.pallas_call(
        functools.partial(field_kernel, sizes),
        out_shape=pltpu.VMEM((8, nloc), f32),
        in_specs=[pl.BlockSpec(memory_space=pltpu.HBM)] * len(operands),
        out_specs=vmem,
        scratch_shapes=[pltpu.VMEM(x.shape, x.dtype) for x in operands]
        + [
            pltpu.SemaphoreType.DMA((len(operands),)),
            pltpu.VMEM((3, CX, CY, 8, BLOCK), f32),
            pltpu.VMEM((3, CX, CY, 4, BLOCK), f32),
            pltpu.VMEM((3, CX, CY, 4, BLOCK), f32),
            pltpu.VMEM((2, 3, 16, BLOCK), f32),
            pltpu.VMEM((2, 24, BLOCK), f32),
            pltpu.VMEM((2, 16, BLOCK), f32),
            pltpu.VMEM((2, 24, BLOCK), f32),
            pltpu.SemaphoreType.DMA((10,)),
            pltpu.SemaphoreType.DMA((10,)),
            pltpu.VMEM((NBLK, BLOCK, BLOCK), jnp.bfloat16),
            pltpu.VMEM((NBLK, 8, BLOCK), f32),
            pltpu.VMEM((NBLK * NGRP, GROUP, 8), f32),
            pltpu.VMEM((NBLK * NGRP * 9, 8, BLOCK), f32),
            pltpu.VMEM((NBLK * NGRP * 9, 4, BLOCK), f32),
            pltpu.VMEM((3, NCOL, BLOCK), f32),
            tensors, tensors, tensors, tensors,
            pltpu.VMEM((NBLK, 3, BLOCK, BLOCK), f32),
            pltpu.VMEM((4, NBLK, 8, BLOCK), f32),
            pltpu.VMEM((32, nloc), f32),
        ]
        + [pltpu.VMEM((n, 1, BLOCK), f32) for n in stages]
        + [pltpu.SemaphoreType.REGULAR] * 2,
        compiler_params=pltpu.CompilerParams(
            collective_id=0, has_side_effects=True, vmem_limit_bytes=63 * 2**20
        ),
    )(*operands)
    return answers[0:3], polarizability[None] * answers[3:6]


def solution(mesh):
    sizes = tuple(mesh.shape[name] for name in ("gx", "gy", "gz"))
    wide = P(None, ("gx", "gy", "gz"))
    flat = P(("gx", "gy", "gz"))
    return jax.shard_map(
        functools.partial(per_device, sizes),
        mesh=mesh,
        in_specs=(wide, flat, wide, flat, wide, wide, wide, wide, flat),
        out_specs=(wide, wide),
        check_vma=False,
    )
```

```python
import functools
import math

import jax
import jax.numpy as jnp
from jax import lax
from jax.experimental import pallas as pl
from jax.experimental.pallas import tpu as pltpu
from jax.sharding import PartitionSpec as P

BLOCK = 128
NBX, NBY = 4, 2
NBLK = NBX * NBY
CX, CY = NBX + 2, NBY + 2
NCOL = CX * CY
GROUP = 32
NGRP = BLOCK // GROUP
BRICK = (16.0, 8.0, 8.0)
CUTOFF_SQUARED = 12.25
THOLE_FACTOR = 0.02
CENTRE, HALF = 12.5, 8.5
FAR = 1.0e6
MESH = pl.DeviceIdType.MESH
HIGHEST = lax.Precision.HIGHEST
OFFSETS = [
    (x, y, z)
    for x in (-1, 0, 1)
    for y in (-1, 0, 1)
    for z in (-1, 0, 1)
    if (x, y, z) != (0, 0, 0)
]
GRAM = [(a, b) for a in range(4) for b in range(a, 4)]


def dot_rows(left, right, precision=HIGHEST):
    return lax.dot_general(
        left, right, (((1,), (0,)), ((), ())), precision=precision,
        preferred_element_type=jnp.float32,
    )


def dot_lanes(left, right, precision=HIGHEST):
    return lax.dot_general(
        left, right, (((1,), (1,)), ((), ())), precision=precision,
        preferred_element_type=jnp.float32,
    )


def halves(x, parts):
    out = []
    for _ in range(parts):
        part = x.astype(jnp.bfloat16)
        out.append(part)
        x = x - part.astype(jnp.float32)
    return jnp.concatenate(out, axis=0)


def permuted(dot, x, one_hot):
    rows = x.shape[0]
    out = dot(halves(x, 3), one_hot, None)
    return out[:rows] + out[rows : 2 * rows] + out[2 * rows :]


def iota(shape, axis):
    return lax.broadcasted_iota(jnp.int32, shape, axis)


def own_span(step, count):
    return (0, count) if step == 0 else ((count - 1, 1) if step > 0 else (0, 1))


def halo_span(step, count):
    return (1, count) if step == 0 else ((0, 1) if step > 0 else (count + 1, 1))


def site_ranks(place):
    tie = iota((BLOCK, BLOCK), 0) < iota((BLOCK, BLOCK), 1)
    base = jnp.zeros((NBLK, BLOCK), jnp.float32)
    for axis, shift in ((2, 4), (0, 2), (1, 0)):
        key = base + place[axis]
        column = jnp.transpose(key)
        ranks = []
        for b in range(NBLK):
            left = jnp.broadcast_to(column[:, b : b + 1], (BLOCK, BLOCK))
            right = jnp.broadcast_to(key[b : b + 1, :], (BLOCK, BLOCK))
            before = jnp.logical_or(left < right, jnp.logical_and(left == right, tie))
            ranks.append(jnp.sum(jnp.where(before, 1.0, 0.0), axis=0, keepdims=True))
        rank = jnp.concatenate(ranks, axis=0).astype(jnp.int32)
        base = jnp.right_shift(rank, shift).astype(jnp.float32) * 512.0
    return rank


def site_lanes(rank):
    z, x, y = jnp.right_shift(rank, 4), jnp.right_shift(rank, 2) & 3, rank & 3
    cube = jnp.right_shift(z, 1) * 4 + jnp.right_shift(x, 1) * 2 + jnp.right_shift(y, 1)
    return cube * 8 + (z & 1) * 4 + (x & 1) * 2 + (y & 1)


def inverse_list(list_ref, row, first, entries, tables):
    blocks = jnp.zeros((tables, BLOCK), jnp.float32)
    lanes = jnp.zeros((tables, BLOCK), jnp.float32)
    spot = iota((BLOCK, BLOCK), 1).astype(jnp.float32)
    for r in range(entries // BLOCK):
        entry = list_ref[row : row + 1, r * BLOCK : (r + 1) * BLOCK]
        high = jnp.right_shift(entry, 7) - first
        low = jnp.bitwise_and(entry, BLOCK - 1)
        pick = (iota((tables, BLOCK), 0) == high).astype(jnp.float32)
        place = (iota((BLOCK, BLOCK), 0) == low).astype(jnp.float32)
        both = jnp.concatenate([place, place * spot], axis=0).astype(jnp.bfloat16)
        found = dot_lanes(pick.astype(jnp.bfloat16), both, None)
        blocks = blocks + found[:, :BLOCK] * float(r + 1)
        lanes = lanes + found[:, BLOCK:]
    return blocks, lanes


def inverse_blocks(list_ref, row, entries):
    rows = entries // BLOCK
    total = jnp.zeros((rows, BLOCK), jnp.float32)
    for r in range(rows):
        entry = list_ref[row : row + 1, r * BLOCK : (r + 1) * BLOCK]
        high = jnp.right_shift(entry, 7)
        low = jnp.bitwise_and(entry, BLOCK - 1)
        pick = jnp.where(iota((rows, BLOCK), 0) == high, float(r), 0.0)
        place = (iota((BLOCK, BLOCK), 0) == low).astype(jnp.float32)
        total = total + dot_lanes(
            pick.astype(jnp.bfloat16), place.astype(jnp.bfloat16), None
        )
    return total


def look_up(table, index):
    high = jnp.right_shift(index, 7)
    low = jnp.bitwise_and(index, BLOCK - 1)
    out = jnp.zeros(index.shape, jnp.float32)
    for r in range(table.shape[0]):
        row = jnp.broadcast_to(table[r : r + 1, :], index.shape)
        out = jnp.where(high == r, jnp.take_along_axis(row, low, axis=1), out)
    return out


def place_of(sizes):
    return tuple(lax.axis_index(name) for name in ("gx", "gy", "gz"))


def neighbour(me, sizes, step):
    return tuple(lax.rem(m + s + n, n) for m, s, n in zip(me, step, sizes))


def greet(targets):
    barrier = pltpu.get_barrier_semaphore()
    for target in targets:
        pl.semaphore_signal(barrier, inc=1, device_id=target, device_id_type=MESH)
    return barrier


def bytes_of(view, sem):
    return pltpu.make_async_copy(view, view, sem)


def hops(step):
    return sum(abs(s) for s in step)


def halo_copies(buffer, send_sem, recv_sem, me, sizes, distance=None):
    copies = []
    for step in sorted(OFFSETS, key=hops, reverse=True):
        if distance is not None and hops(step) != distance:
            continue
        (xs, xn), (ys, yn) = own_span(step[0], NBX), own_span(step[1], NBY)
        (xd, _), (yd, _) = halo_span(step[0], NBX), halo_span(step[1], NBY)
        copies.append(
            pltpu.make_async_remote_copy(
                src_ref=buffer.at[1, pl.ds(1 + xs, xn), pl.ds(1 + ys, yn)],
                dst_ref=buffer.at[1 - step[2], pl.ds(xd, xn), pl.ds(yd, yn)],
                send_sem=send_sem,
                recv_sem=recv_sem,
                device_id=neighbour(me, sizes, step),
                device_id_type=MESH,
            )
        )
    return copies


def sum_stages(sizes):
    def near(step):
        return tuple(s if 2 * s <= n else s - n for s, n in zip(step, sizes))

    along = [near((s, 0, 0)) for s in range(1, sizes[0])]
    across = [near((0, y, z)) for y in range(sizes[1]) for z in range(sizes[2]) if y + z > 0]
    return sorted(along, key=hops, reverse=True), sorted(across, key=hops, reverse=True)


def reduce_over(steps, total, slot, place, send, recv, me, sizes):
    slot[place] = total
    copies = []
    for step in steps:
        copies.append(
            pltpu.make_async_remote_copy(
                src_ref=slot.at[place],
                dst_ref=slot.at[place],
                send_sem=send,
                recv_sem=recv,
                device_id=neighbour(me, sizes, step),
                device_id_type=MESH,
            )
        )
    for copy in copies:
        copy.start()


def reduced(steps, slot, recv):
    bytes_of(slot.at[pl.ds(0, len(steps))], recv).wait()
    total = slot[0]
    for k in range(1, len(steps) + 1):
        total = total + slot[k]
    return total


def gradient_steps(products):
    def inner(left, right):
        value = 0.0
        for a, p in enumerate(left):
            for b, q in enumerate(right):
                if p is not None and q is not None:
                    value = value + p * q * products[a, b]
        return value

    def plus(p, q):
        return q if p is None else (p if q is None else p + q)

    def times(scale, p):
        return None if p is None else scale * p

    def applied(c):
        out = [times(CENTRE, p) for p in c]
        if c[0] is not None:
            out[1] = plus(out[1], HALF * c[0])
        for k in (1, 2):
            if c[k] is not None:
                out[k - 1] = plus(out[k - 1], (0.5 * HALF) * c[k])
                out[k + 1] = plus(out[k + 1], (0.5 * HALF) * c[k])
        return out

    left = [jnp.ones((1, 1), jnp.float32), None, None, None]
    direction = list(left)
    answer = [None] * 4
    norm = products[0, 0]
    for _ in range(3):
        image = applied(direction)
        step = norm / inner(direction, image)
        answer = [plus(p, times(step, q)) for p, q in zip(answer, direction)]
        left = [plus(p, times(-step, q)) for p, q in zip(left, image)]
        after = inner(left, left)
        direction = [plus(p, times(after / norm, q)) for p, q in zip(left, direction)]
        norm = after
    return answer, left


def field_kernel(
    sizes,
    coords_in, polar_in, external_in, live_in, ghost_x_in, ghost_y_in, ghost_z_in,
    pairs_in, alive_in,
    answers,
    coords, polar, external, live, ghost_x, ghost_y, ghost_z, pairs, alive, loads,
    halo1, halo2, halo3, tabs_y, tabs_z, own_y, own_z, sends, recvs,
    order, side, target, window, moved, marks, px, py, pz, inner_s, sums, basis, flat,
    slot_x, slot_y, two_steps, four_steps,
):
    me = place_of(sizes)
    outside = (
        coords_in, polar_in, external_in, live_in, ghost_x_in, ghost_y_in, ghost_z_in,
        pairs_in, alive_in,
    )
    inside = (coords, polar, external, live, ghost_x, ghost_y, ghost_z, pairs, alive)
    arriving = [
        pltpu.make_async_copy(far, near, loads.at[n])
        for n, (far, near) in enumerate(zip(outside, inside))
    ]
    for copy in arriving:
        copy.start()
    chained = sizes[0] == 16 and sizes[1] <= 8 and sizes[2] <= 4
    friends = dict.fromkeys(list(OFFSETS) + ([] if chained else sum(sum_stages(sizes), [])))

    def relay(sem, reach):
        if chained:
            for step in (reach, -reach):
                pl.semaphore_signal(
                    sem, inc=1, device_id=neighbour(me, sizes, (step, 0, 0)), device_id_type=MESH
                )

    def relayed(sem):
        if chained:
            pl.semaphore_wait(sem, 2)

    barrier = greet([neighbour(me, sizes, step) for step in friends])
    arriving[0].wait()

    lanes_of = site_lanes(
        site_ranks(
            [
                jnp.concatenate(
                    [coords[k : k + 1, b * BLOCK : (b + 1) * BLOCK] for b in range(NBLK)], axis=0
                )
                for k in range(3)
            ]
        )
    )
    for copy in arriving[1:]:
        copy.wait()

    up_blocks, up_lanes = inverse_list(ghost_x, 0, 0, 2 * BLOCK, NBLK)
    down_blocks, down_lanes = inverse_list(ghost_x, 1, 0, 2 * BLOCK, NBLK)
    upper = iota((NBLK, BLOCK), 0) >= NBLK - NBY
    x_spot = jnp.where(
        upper, (up_blocks - 1.0) * BLOCK + up_lanes, (down_blocks - 1.0) * BLOCK + down_lanes
    )
    x_spot = jnp.maximum(x_spot, 0.0)
    lane = iota((1, BLOCK), 1)
    lane_f = lane.astype(jnp.float32)

    for b in range(NBLK):
        cut = slice(b * BLOCK, (b + 1) * BLOCK)
        alpha = polar[0:1, cut]
        living = live[0:1, cut].astype(jnp.float32)
        place = coords[:, cut]
        rhs = external[:, cut] * living
        code = lane_f + x_spot[b : b + 1, :] * BLOCK
        beta = lax.rsqrt(alpha) * math.sqrt(THOLE_FACTOR)
        tile = jnp.concatenate([place, beta, rhs, code], axis=0)
        more = jnp.concatenate(
            [living / alpha, living, jnp.zeros((6, BLOCK), jnp.float32)], axis=0
        )
        one_hot = jnp.where(iota((BLOCK, BLOCK), 0) == lanes_of[b : b + 1, :], 1.0, 0.0)
        one_hot = one_hot.astype(jnp.bfloat16)
        order[b] = one_hot
        ranked = permuted(dot_lanes, jnp.concatenate([tile, more], axis=0), one_hot)
        halo1[1, 1 + b // NBY, 1 + b % NBY] = ranked[:8]
        side[b] = ranked[8:]
        basis[0, b] = jnp.concatenate(
            [ranked[4:7], jnp.zeros((5, BLOCK), jnp.float32)], axis=0
        )
        flipped = jnp.transpose(ranked[:8])
        for g in range(NGRP):
            target[b * NGRP + g] = flipped[g * GROUP : (g + 1) * GROUP]

    pl.semaphore_wait(barrier, len(friends))
    for copy in halo_copies(halo1, sends.at[0], recvs.at[0], me, sizes):
        copy.start()

    def send_table(source, landing, step):
        pltpu.make_async_remote_copy(
            src_ref=source,
            dst_ref=landing,
            send_sem=sends.at[1],
            recv_sem=recvs.at[1],
            device_id=neighbour(me, sizes, step),
            device_id_type=MESH,
        ).start()

    for row, step_y in enumerate((1, -1)):
        blocks, lanes = inverse_list(ghost_y, row, 0, 6 * BLOCK, 12)
        own_y[row, 0:12] = (blocks - 1.0) * BLOCK + lanes
        for step_z in (-1, 1, 0):
            send_table(own_y.at[row], tabs_y.at[row, 1 - step_z], (0, step_y, step_z))
    for row, step_z in enumerate((1, -1)):
        own_z[row] = inverse_blocks(ghost_z, row, 24 * BLOCK)
        send_table(own_z.at[row], tabs_z.at[row], (0, 0, step_z))

    count = pairs.shape[1]
    bits = jnp.left_shift(alive[0:1, :], pairs[0:1, :]).astype(jnp.float32)
    bits = jnp.broadcast_to(bits, (8, count)).astype(jnp.bfloat16)
    listed = (iota((BLOCK, count), 0) == pairs[1:2, :]).astype(jnp.float32)
    listed_by = dot_lanes(bits, listed.astype(jnp.bfloat16), None)

    halo_bytes = window.at[pl.ds(0, 3 * NCOL - NBLK)]
    table_bytes = window.at[pl.ds(0, (6 * 16 + 2 * 24) // 8)]
    bytes_of(halo_bytes, recvs.at[0]).wait()
    bytes_of(table_bytes, recvs.at[1]).wait()
    relay(two_steps, 2)

    for role in range(3):
        for part in range(NCOL // 8):
            codes = jnp.concatenate(
                [
                    halo1[role, c // CY, c % CY, 7:8, :]
                    for c in range(part * 8, part * 8 + 8)
                ],
                axis=0,
            ).astype(jnp.int32)
            spot = jnp.right_shift(codes, 7)
            own_lane = jnp.bitwise_and(codes, BLOCK - 1)
            col = iota((8, BLOCK), 0) + part * 8
            cx, cy = jnp.right_shift(col, 2), jnp.bitwise_and(col, 3)
            block_y = jnp.bitwise_and(cy + 1, 1)
            entry = ((cx - 1) * NBY + block_y) * BLOCK + own_lane
            entry = jnp.where(cx == 0, NBLK * BLOCK + spot, entry)
            entry = jnp.where(cx == CX - 1, (NBLK + NBY) * BLOCK + spot, entry)
            low = look_up(tabs_y[0, role, 0:12], entry)
            high = look_up(tabs_y[1, role, 0:12], entry)
            found = jnp.where(cy == 0, low, jnp.where(cy == CY - 1, high, 0.0))
            valid = found >= 0.0
            found = jnp.maximum(found, 0.0).astype(jnp.int32)
            entry = jnp.where(cy == 0, 12 * BLOCK + found, entry)
            entry = jnp.where(cy == CY - 1, 18 * BLOCK + found, entry)
            if role == 1:
                block = jnp.right_shift(entry, 7)
            else:
                layer = look_up(tabs_z[role // 2], entry)
                block = layer.astype(jnp.int32) + (24 if role == 0 else 48)
            mark = jnp.take_along_axis(listed_by, block, axis=1)
            marks[role, part * 8 : part * 8 + 8] = jnp.where(valid, mark, 0.0)

    row8 = iota((8, BLOCK), 0)
    lane8 = iota((8, BLOCK), 1)
    edge = [
        (jnp.where(m == 0, -n * size, 0.0), jnp.where(m == n - 1, n * size, 0.0))
        for m, n, size in zip(me, sizes, BRICK)
    ]

    def shifted(role, cx, cy):
        tile = halo1[role, cx, cy]
        col = cx * CY + cy
        if cx in (0, CX - 1):
            tile = tile + jnp.where(row8 == 0, edge[0][0 if cx == 0 else 1], 0.0)
        if cy in (0, CY - 1):
            tile = tile + jnp.where(row8 == 1, edge[1][0 if cy == 0 else 1], 0.0)
        if role != 1:
            tile = tile + jnp.where(row8 == 2, edge[2][role // 2], 0.0)
        return jnp.where(row8 == 7, marks[role, col : col + 1, :], tile)

    def windows(tile_at, rows, put, kinds):
        lanes = iota((rows, BLOCK), 1)
        z_site = jnp.right_shift(lanes, 5) * 2 + (jnp.right_shift(lanes, 2) & 1)
        x_site = (jnp.right_shift(lanes, 4) & 1) * 2 + (jnp.right_shift(lanes, 1) & 1)
        y_site = (jnp.right_shift(lanes, 3) & 1) * 2 + (lanes & 1)
        low_x = (x_site >= 1, x_site >= 3)
        low_y = (y_site >= 1, y_site >= 3)
        known = {}

        def layered(cx, cy, g):
            if (cx, cy) not in known:
                below, middle, above = [tile_at(role, cx, cy) for role in range(3)]
                known[cx, cy] = (
                    jnp.where(z_site >= 5, below, middle),
                    jnp.where(z_site >= 7, below, middle),
                    jnp.where(z_site < 1, above, middle),
                    jnp.where(z_site < 3, above, middle),
                )
            return known[cx, cy][g]

        def mixed_x(bx, half, cy, g):
            if (bx, half, cy, g) not in known:
                known[bx, half, cy, g] = jnp.where(
                    low_x[half], layered(bx, cy, g), layered(bx + 2, cy, g)
                )
            return known[bx, half, cy, g]

        def tile_of(kind, bx, by, g):
            if kind == 0:
                return layered(bx + 1, by + 1, g)
            if kind < 3:
                return mixed_x(bx, kind - 1, by + 1, g)
            if kind < 5:
                return jnp.where(
                    low_y[kind - 3], layered(bx + 1, by, g), layered(bx + 1, by + 2, g)
                )
            half_x, half_y = (kind - 5) // 2, (kind - 5) % 2
            return jnp.where(
                low_y[half_y], mixed_x(bx, half_x, by, g), mixed_x(bx, half_x, by + 2, g)
            )

        for g in range(NGRP):
            for bx in range(NBX):
                for by in range(NBY):
                    for kind in kinds:
                        put(((bx * NBY + by) * NGRP + g) * 9 + kind, tile_of(kind, bx, by, g))

    def put_window(at, tile):
        window[at] = tile

    windows(shifted, 8, put_window, range(9))

    cubes = [(hx, hy) for hx in range(2) for hy in range(2)]

    def windows_of(hx, hy):
        return (0, 1 + hx, 3 + hy, 5 + 2 * hx + hy)

    def spread_row(tile, k):
        return jnp.broadcast_to(tile[k : k + 1], (8, BLOCK))

    def add_field(total, tensor, moment):
        ax, ay, az, inner = tensor
        vx, vy, vz = moment
        along = ax * vx + ay * vy + az * vz
        parts = [along * a - inner * v for a, v in ((ax, vx), (ay, vy), (az, vz))]
        return parts if total is None else [t + p for t, p in zip(total, parts)]

    def keep_sums(block, g, u, total):
        for k in range(3):
            sums[block, k, pl.ds(pl.multiple_of(g * GROUP + u * 8, 8), 8)] = total[k]

    def build(step, carry):
        block, g = step // NGRP, step % NGRP
        mine = target[step]
        sources = []
        for w in range(9):
            tile = window[step * 9 + w]
            seen = jnp.bitwise_and(jnp.right_shift(tile[7:8].astype(jnp.int32), block), 1) == 1
            sx = jnp.where(seen, tile[0:1], FAR)
            sources.append(
                [jnp.broadcast_to(sx, (8, BLOCK))] + [spread_row(tile, k) for k in range(1, 7)]
            )
        for u, (hx, hy) in enumerate(cubes):
            tx, ty, tz, tb = [
                jnp.broadcast_to(mine[u * 8 : u * 8 + 8, k : k + 1], (8, BLOCK)) for k in range(4)
            ]
            total = None
            for n, w in enumerate(windows_of(hx, hy)):
                sx, sy, sz, sb, vx, vy, vz = sources[w]
                dx, dy, dz = tx - sx, ty - sy, tz - sz
                if n == 0:
                    itself = row8 + (g * GROUP + u * 8) == lane8
                    dx = jnp.where(itself, FAR, dx)
                q = dx * dx + dy * dy + dz * dz
                inv = lax.rsqrt(q)
                inv2 = inv * inv
                margin = jnp.maximum(CUTOFF_SQUARED - q, 0.0)
                scaled = q * (q * inv) * (tb * sb)
                damp = jnp.exp(-scaled)
                rest = 1.0 - damp
                near = margin * inv2
                inner = (near * margin) * (inv * rest)
                root = (3.0 * inv) * (rest - scaled * damp)
                scale = near * (root * lax.rsqrt(root))
                tensor = (scale * dx, scale * dy, scale * dz, inner)
                slot = step * 16 + u * 4 + n
                px[slot], py[slot], pz[slot], inner_s[slot] = tensor
                total = add_field(total, tensor, (vx, vy, vz))
            keep_sums(block, g, u, total)
        return carry

    lax.fori_loop(0, NBLK * NGRP, build, 0, unroll=8)

    def apply(parts, step, carry):
        block, g = step // NGRP, step % NGRP
        sources = {}
        for u, (hx, hy) in enumerate(cubes):
            total = None
            if 0 not in parts:
                rows = pl.ds(pl.multiple_of(g * GROUP + u * 8, 8), 8)
                total = [sums[block, k, rows] for k in range(3)]
            for n in parts:
                w = windows_of(hx, hy)[n]
                if w not in sources:
                    tile = moved[step * 9 + w]
                    sources[w] = [spread_row(tile, k) for k in range(3)]
                slot = step * 16 + u * 4 + n
                tensor = (px[slot], py[slot], pz[slot], inner_s[slot])
                total = add_field(total, tensor, sources[w])
            keep_sums(block, g, u, total)
        return carry

    ones = jnp.ones((8, BLOCK), jnp.float32)
    ones_half = ones.astype(jnp.bfloat16)

    def next_basis(level, halo):
        for b in range(NBLK):
            parts = [halves(sums[b, k], 2) for k in range(3)]
            field = dot_lanes(ones_half, jnp.concatenate(parts, axis=0), None)
            field = [
                field[:, 2 * k * BLOCK : (2 * k + 1) * BLOCK]
                + field[:, (2 * k + 1) * BLOCK : (2 * k + 2) * BLOCK]
                for k in range(3)
            ]
            field = jnp.where(row8 == 0, field[0], jnp.where(row8 == 1, field[1], field[2]))
            field = field * (1.0 / CUTOFF_SQUARED**2)
            v = basis[level, b]
            rows = side[b]
            image = rows[0:1] * v - rows[1:2] * field
            image = (image - CENTRE * v) * (1.0 / HALF)
            if level > 0:
                image = 2.0 * image - basis[level - 1, b]
            image = jnp.where(row8 < 3, image, 0.0)
            basis[level + 1, b] = image
            if halo is not None:
                halo[1, 1 + b // NBY, 1 + b % NBY] = image[:4]

    def put_moved(at, tile):
        moved[at] = tile

    started = [(halo_bytes, sends.at[0]), (table_bytes, sends.at[1])]
    halves_of = {1: 14, 2: 14, 3: 4}
    works = ((1, (0,), (0,)), (2, (1, 2, 3, 4), (1, 2)), (3, (5, 6, 7, 8), (3,)))

    def put_moved(at, tile):
        moved[at] = tile

    def gram_row(a, b):
        part = jnp.sum(basis[a] * basis[b], axis=0)
        return jnp.sum(part, axis=0, keepdims=True)

    for level, halo in ((0, halo2), (1, halo3)):
        next_basis(level, halo)
        for distance in (3, 2, 1):
            sem = 2 + 3 * level + distance - 1
            for copy in halo_copies(halo, sends.at[sem], recvs.at[sem], me, sizes, distance):
                copy.start()
        if level == 1:
            early = {(a, b): gram_row(a, b) for a, b in GRAM if b < 3}
        for distance, kinds, parts in works:
            sem = 2 + 3 * level + distance - 1
            view = window.at[pl.ds(0, halves_of[distance])]
            bytes_of(view, recvs.at[sem]).wait()
            started.append((view, sends.at[sem]))
            windows(lambda role, cx, cy, halo=halo: halo[role, cx, cy], 4, put_moved, kinds)
            lax.fori_loop(0, NBLK * NGRP, functools.partial(apply, parts), 0, unroll=8)
            if level == 0 and distance == 3:
                relayed(two_steps)
                relay(four_steps, 4)
    next_basis(2, None)

    rows = [early[a, b] if b < 3 else gram_row(a, b) for a, b in GRAM]
    rows.append(jnp.zeros((BLOCK - len(GRAM), BLOCK), jnp.float32))
    total = dot_lanes(ones, jnp.concatenate(rows, axis=0))[0:1]
    along, across = sum_stages(sizes)
    relayed(four_steps)
    reduce_over(along, total, slot_x, me[0], sends.at[8], recvs.at[8], me, sizes)
    for b in range(NBLK):
        stacked = jnp.concatenate([basis[k, b] for k in range(4)], axis=0)
        flat[:, b * BLOCK : (b + 1) * BLOCK] = permuted(dot_rows, stacked, order[b])
    total = reduced(along, slot_x, recvs.at[8])
    place = me[1] * sizes[2] + me[2]
    reduce_over(across, total, slot_y, place, sends.at[9], recvs.at[9], me, sizes)
    total = reduced(across, slot_y, recvs.at[9])
    started.append((slot_x.at[pl.ds(0, len(along))], sends.at[8]))
    started.append((slot_y.at[pl.ds(0, len(across))], sends.at[9]))
    products = {}
    for k, (a, b) in enumerate(GRAM):
        products[a, b] = products[b, a] = total[:, k : k + 1]
    answer, left = gradient_steps(products)

    def combined(coefficients):
        value = 0.0
        for k, c in enumerate(coefficients):
            if c is not None:
                value = value + c * flat[8 * k : 8 * k + 3, :]
        return value

    answers[...] = jnp.concatenate(
        [combined(answer), combined(left), jnp.zeros((2, answers.shape[1]), jnp.float32)], axis=0
    )
    for view, sem in started:
        bytes_of(view, sem).wait()


def per_device(
    sizes, coords, polarizability, external_field, bead_live,
    ghost_x, ghost_y, ghost_z, pair_blocks, pair_live,
):
    nloc = coords.shape[1]
    vmem = pl.BlockSpec(memory_space=pltpu.VMEM)
    f32 = jnp.float32
    operands = (
        coords, polarizability.reshape(1, nloc), external_field, bead_live.reshape(1, nloc),
        ghost_x, ghost_y, ghost_z, pair_blocks, pair_live.reshape(1, pair_live.shape[0]),
    )
    tensors = pltpu.VMEM((NBLK * NGRP * 16, 8, BLOCK), f32)
    stages = (sizes[0], sizes[1] * sizes[2])
    answers = pl.pallas_call(
        functools.partial(field_kernel, sizes),
        out_shape=pltpu.VMEM((8, nloc), f32),
        in_specs=[pl.BlockSpec(memory_space=pltpu.HBM)] * len(operands),
        out_specs=vmem,
        scratch_shapes=[pltpu.VMEM(x.shape, x.dtype) for x in operands]
        + [
            pltpu.SemaphoreType.DMA((len(operands),)),
            pltpu.VMEM((3, CX, CY, 8, BLOCK), f32),
            pltpu.VMEM((3, CX, CY, 4, BLOCK), f32),
            pltpu.VMEM((3, CX, CY, 4, BLOCK), f32),
            pltpu.VMEM((2, 3, 16, BLOCK), f32),
            pltpu.VMEM((2, 24, BLOCK), f32),
            pltpu.VMEM((2, 16, BLOCK), f32),
            pltpu.VMEM((2, 24, BLOCK), f32),
            pltpu.SemaphoreType.DMA((10,)),
            pltpu.SemaphoreType.DMA((10,)),
            pltpu.VMEM((NBLK, BLOCK, BLOCK), jnp.bfloat16),
            pltpu.VMEM((NBLK, 8, BLOCK), f32),
            pltpu.VMEM((NBLK * NGRP, GROUP, 8), f32),
            pltpu.VMEM((NBLK * NGRP * 9, 8, BLOCK), f32),
            pltpu.VMEM((NBLK * NGRP * 9, 4, BLOCK), f32),
            pltpu.VMEM((3, NCOL, BLOCK), f32),
            tensors, tensors, tensors, tensors,
            pltpu.VMEM((NBLK, 3, BLOCK, BLOCK), f32),
            pltpu.VMEM((4, NBLK, 8, BLOCK), f32),
            pltpu.VMEM((32, nloc), f32),
        ]
        + [pltpu.VMEM((n, 1, BLOCK), f32) for n in stages]
        + [pltpu.SemaphoreType.REGULAR] * 2,
        compiler_params=pltpu.CompilerParams(
            collective_id=0, has_side_effects=True, vmem_limit_bytes=63 * 2**20
        ),
    )(*operands)
    return answers[0:3], polarizability[None] * answers[3:6]


def solution(mesh):
    sizes = tuple(mesh.shape[name] for name in ("gx", "gy", "gz"))
    wide = P(None, ("gx", "gy", "gz"))
    flat = P(("gx", "gy", "gz"))
    return jax.shard_map(
        functools.partial(per_device, sizes),
        mesh=mesh,
        in_specs=(wide, flat, wide, flat, wide, wide, wide, wide, flat),
        out_specs=(wide, wide),
        check_vma=False,
    )
```
